32 devices in a mesh: canvas: 4 (over y, core), rows: 8 (over z, x).
Axes of the slice: x: 2, y: 2, z: 4, core: 2. Of those that a mesh axis runs over, the one named last changes fastest.
Arguments:
- features: bfloat16 [4, 144, 48, 2048], P('canvas', 'rows'), may hold values from -13 to 13
- segment_map: int32 [4, 144, 48], P('canvas', 'rows'), may hold values from 0 to 7, as said below
- pixel_mask: int32 [4, 144, 48], P('canvas', 'rows'), may hold values from 0 to 1, as said below
- inner_weight: bfloat16 [2048, 256], P('rows'), may hold values from -0.125 to 0.125
- atrous_weight: bfloat16 [3, 9, 2048, 256], P(None, None, 'rows'), may hold values from -0.046875 to 0.046875
- pool_weight: bfloat16 [2048, 256], P('rows'), may hold values from -0.125 to 0.125
- proj_weight: bfloat16 [1280, 256], P('rows'), may hold values from -0.15625 to 0.15625
- norm_gains: float32 [6, 256], replicated, may hold values from 0.1 to 1.9
- norm_shifts: float32 [6, 256], replicated, may hold values from -3 to 3
- cotangent: bfloat16 [4, 576, 192, 256], P('canvas', 'rows'), may hold values from -6 to 6
Outputs:
- upsampled: bfloat16 [4, 576, 192, 256], P('canvas', 'rows')
- grad_features: float32 [4, 144, 48, 2048], P('canvas', 'rows')
- grad_inner: float32 [2048, 256], P('rows')
- grad_atrous: float32 [3, 9, 2048, 256], P(None, None, 'rows')
- grad_pool: float32 [2048, 256], P('rows')
- grad_proj: float32 [1280, 256], P('rows')
- grad_gains: float32 [6, 256], replicated
- grad_shifts: float32 [6, 256], replicated
The draws below stay inside these ranges and needn't reach their ends.
Inputs may be any that keep to these rules, and one draw needn't show every extreme that they name: `segment_map`: each canvas is a grid of images: its rows are cut into 4 runs of whole rows and its columns into 2 runs of whole columns, and a pixel's number is (row run) * 2 + (column run); the cuts depend only on the canvas; every row run is at least 24 rows and every column run at least 12 columns. `pixel_mask`: 0 marks padding along each image's lower and right edges; every image of every canvas has pixels marked 1.
All inputs are finite; a program needn't handle non-finite values.
Results may differ from the reference program's by a relative error of at most 0.0058.
Values may be sent and summed in bfloat16 or wider, within the bound.
No kernel may reach another device: no remote copies, remote signals or barrier semaphores. Data moves between devices by JAX's collectives and lax.ppermute only.
A program may use at most 448 MiB of HBM per device.

```python
import jax
import jax.numpy as jnp
from jax import lax

CHANNELS = 2048
BRANCH = 256
JOINED = 1280
COLS = 48
COL_IMAGES = 2
CANVASES = 4
CANVAS_ROWS = 144
ROW_IMAGES = 4
IMAGES = 8


def image_grid(key):
    col_key, row_key = jax.random.split(key)
    col_spread = COLS // (4 * COL_IMAGES)
    col_jitter = jax.random.randint(col_key, (CANVASES, COL_IMAGES - 1), -col_spread, col_spread + 1)
    col_cuts = jnp.arange(1, COL_IMAGES, dtype=jnp.int32) * COLS // COL_IMAGES
    col_cuts = col_cuts[None, :] + col_jitter
    row_jitter = jax.random.randint(row_key, (CANVASES, ROW_IMAGES - 1), -6, 7)
    row_cuts = jnp.arange(1, ROW_IMAGES, dtype=jnp.int32) * CANVAS_ROWS // ROW_IMAGES
    row_cuts = row_cuts[None, :] + row_jitter
    column = jnp.arange(COLS, dtype=jnp.int32)
    height = jnp.arange(CANVAS_ROWS, dtype=jnp.int32)
    col_label = jnp.sum((column[None, None, :] >= col_cuts[:, :, None]).astype(jnp.int32), axis=1)
    row_label = jnp.sum((height[None, None, :] >= row_cuts[:, :, None]).astype(jnp.int32), axis=1)
    col_ends = jnp.concatenate([col_cuts, jnp.full((CANVASES, 1), COLS, jnp.int32)], axis=1)
    row_ends = jnp.concatenate([row_cuts, jnp.full((CANVASES, 1), CANVAS_ROWS, jnp.int32)], axis=1)
    return (row_label, col_label, row_ends, col_ends)


def segment_labels(row_label, col_label):
    return (row_label[:, :, None] * COL_IMAGES + col_label[:, None, :]).astype(jnp.int32)


def draw_segment_map(key, part):
    row_label, col_label, row_ends, col_ends = image_grid(key)
    return segment_labels(row_label, col_label)


def draw_pixel_mask(key, part):
    row_label, col_label, row_ends, col_ends = image_grid(key)
    key = jax.random.fold_in(key, 12)
    row_key, col_key = jax.random.split(key)
    row_pad = jax.random.randint(row_key, (CANVASES, IMAGES), 0, 6)
    col_pad = jax.random.randint(col_key, (CANVASES, IMAGES), 0, 4)
    labels = segment_labels(row_label, col_label)
    flat = labels.reshape(CANVASES, CANVAS_ROWS * COLS)
    row_cut = jnp.take_along_axis(row_ends, row_label, axis=1)
    col_cut = jnp.take_along_axis(col_ends, col_label, axis=1)
    pad_rows = jnp.take_along_axis(row_pad, flat, axis=1).reshape(CANVASES, CANVAS_ROWS, COLS)
    pad_cols = jnp.take_along_axis(col_pad, flat, axis=1).reshape(CANVASES, CANVAS_ROWS, COLS)
    height = jnp.arange(CANVAS_ROWS, dtype=jnp.int32)
    column = jnp.arange(COLS, dtype=jnp.int32)
    inside = (height[None, :, None] < row_cut[:, :, None] - pad_rows) & (column[None, None, :] < col_cut[:, None, :] - pad_cols)
    return inside.astype(jnp.int32)


def draw_features(key, part):
    row_label, col_label, row_ends, col_ends = image_grid(key)
    labels = segment_labels(row_label, col_label)
    key = jax.random.fold_in(key, 13)
    noise_key, offset_key = jax.random.split(key)
    heights = jnp.arange(CANVAS_ROWS, dtype=jnp.float32) / (CANVAS_ROWS - 1)
    noise = jnp.clip(jax.random.normal(noise_key, (CANVASES, CANVAS_ROWS, COLS, CHANNELS), jnp.float32), -5.0, 5.0)
    offsets = jnp.clip(0.5 * jax.random.normal(offset_key, (CANVASES, IMAGES, CHANNELS), jnp.float32), -2.0, 2.0)
    profile = 0.6 + 1.2 * heights
    chosen = offsets[jnp.arange(CANVASES, dtype=jnp.int32)[:, None, None], labels]
    return (profile[None, :, None, None] * (noise + chosen)).astype(jnp.bfloat16)


def block_scale(stream_key, dims, pieces, least, largest):
    loudness = 1.0
    for dim, parts in pieces:
        draws = jax.random.uniform(jax.random.fold_in(jax.random.fold_in(stream_key, 6), dim), (parts,), jnp.float32, least / len(pieces), largest / len(pieces))
        loudness = loudness * jnp.repeat(jnp.exp(draws), dims[dim] // parts).reshape((-1,) + (1,) * (len(dims) - 1 - dim))
    return loudness


def bell_draw(key, shape, deviation, limit, cuts=(), held_as=jnp.bfloat16):
    drawn = jax.random.normal(key, shape, jnp.float32) * deviation
    if len(cuts) > 0:
        drawn = block_scale(key, shape, cuts, -0.22, 0.18) * drawn
    return jnp.clip(drawn, min=-limit, max=limit).astype(held_as)


def setup_inputs(seed: int = 0) -> dict:
    arg_keys = jax.random.split(jax.random.key(seed), 11)
    features = draw_features(jax.random.fold_in(arg_keys[10], 71), 0)
    segment_map = draw_segment_map(jax.random.fold_in(arg_keys[10], 71), 0)
    pixel_mask = draw_pixel_mask(jax.random.fold_in(arg_keys[10], 71), 0)
    inner_weight = bell_draw(arg_keys[3], (CHANNELS, BRANCH), CHANNELS ** -0.5, 0.125, ((0, 8),))
    atrous_weight = bell_draw(arg_keys[4], (3, 9, CHANNELS, BRANCH), (9 * CHANNELS) ** -0.5, 0.046875, ((2, 8),))
    pool_weight = bell_draw(arg_keys[5], (CHANNELS, BRANCH), CHANNELS ** -0.5, 0.125, ((0, 8),))
    proj_weight = bell_draw(arg_keys[6], (JOINED, BRANCH), JOINED ** -0.5, 0.15625, ((0, 8),))
    norm_gains = jnp.clip(1.0 + 0.18 * jax.random.normal(arg_keys[7], (6, BRANCH), jnp.float32), 0.1, 1.9)
    norm_shifts = bell_draw(arg_keys[8], (6, BRANCH), 0.5, 3.0, (), jnp.float32)
    cotangent = bell_draw(arg_keys[9], (CANVASES, 4 * CANVAS_ROWS, 4 * COLS, BRANCH), 1.0, 6.0, ((0, 4), (1, 8)))
    return {"features": features, "segment_map": segment_map, "pixel_mask": pixel_mask, "inner_weight": inner_weight, "atrous_weight": atrous_weight, "pool_weight": pool_weight, "proj_weight": proj_weight, "norm_gains": norm_gains, "norm_shifts": norm_shifts, "cotangent": cotangent}


@jax.custom_vjp
def low(v):
    return lax.optimization_barrier(v.astype(jnp.bfloat16)).astype(jnp.float32)

@jax.custom_vjp
def low_back(v):
    return v

def low_keep(v):
    return (low(v), None)

def low_pass(kept, grad):
    return (grad,)

def back_keep(v):
    return (v, None)

def back_low(kept, grad):
    return (low(grad),)
low.defvjp(low_keep, low_pass)
low_back.defvjp(back_keep, back_low)
dilations = (6, 12, 18)
epsilon = 1e-05
prev_weights = (0.375, 0.125, 0.0, 0.0)
self_weights = (0.625, 0.875, 0.875, 0.625)
next_weights = (0.0, 0.0, 0.125, 0.375)
highest = lax.Precision.HIGHEST

def upsample_axis(values, dim_index):
    extent = values.shape[dim_index]
    first_row = lax.slice_in_dim(values, 0, 1, axis=dim_index)
    last_row = lax.slice_in_dim(values, extent - 1, extent, axis=dim_index)
    padded = jnp.concatenate([first_row, values, last_row], axis=dim_index)
    before = lax.slice_in_dim(padded, 0, extent, axis=dim_index)
    middle = lax.slice_in_dim(padded, 1, extent + 1, axis=dim_index)
    after = lax.slice_in_dim(padded, 2, extent + 2, axis=dim_index)
    phases = [prev_weights[member] * before + self_weights[member] * middle + next_weights[member] * after for member in range(4)]
    stacked = jnp.stack(phases, axis=dim_index + 1)
    shape_out = list(values.shape)
    shape_out[dim_index] = 4 * extent
    return stacked.reshape(shape_out)

def atrous_branch(masked, kernel, segments, dilation):
    rows_total = masked.shape[1]
    cols_total = masked.shape[2]
    products = jnp.einsum('nhwc,kcb->nhwkb', masked, kernel, precision=highest)
    padded = jnp.pad(products, ((0, 0), (dilation, dilation), (dilation, dilation), (0, 0), (0, 0)))
    seg_padded = jnp.pad(segments, ((0, 0), (dilation, dilation), (dilation, dilation)), constant_values=-1)
    result = jnp.zeros(products.shape[:3] + products.shape[4:], jnp.float32)
    for row_tap in range(3):
        for col_tap in range(3):
            row_start = dilation + (row_tap - 1) * dilation
            col_start = dilation + (col_tap - 1) * dilation
            moved = padded[:, row_start:row_start + rows_total, col_start:col_start + cols_total, 3 * row_tap + col_tap]
            source = seg_padded[:, row_start:row_start + rows_total, col_start:col_start + cols_total]
            same = (source == segments).astype(jnp.float32)
            result = result + same[..., None] * moved
    return result

def normalize(values, weight_map, total_count, scale_vec, shift_vec, reduce_dims):
    average = lax.optimization_barrier(jnp.sum(weight_map * values, axis=reduce_dims)) / total_count
    spread = lax.optimization_barrier(jnp.sum(weight_map * values * values, axis=reduce_dims)) / total_count - average * average
    centered = (values - average) * lax.rsqrt(spread + epsilon)
    return scale_vec * centered + shift_vec

def forward(feature_in, inner_kernel, atrous_kernel, pool_kernel, proj_kernel, gain_rows, shift_rows, segment_map, valid_mask):
    masked = feature_in * valid_mask
    pixel_total = jnp.sum(valid_mask)
    pixel_dims = (0, 1, 2)
    conv_outs = [low_back(jnp.einsum('nhwc,cb->nhwb', masked, inner_kernel, precision=highest))]
    for branch, dilation in enumerate(dilations):
        conv_outs.append(low_back(atrous_branch(masked, atrous_kernel[branch], segment_map, dilation)))
    branch_acts = []
    for branch, conv_out in enumerate(conv_outs):
        pre_act = normalize(conv_out, valid_mask, pixel_total, gain_rows[branch], shift_rows[branch], pixel_dims)
        branch_acts.append(low(jax.nn.silu(pre_act)))
    members = (segment_map[..., None] == jnp.arange(IMAGES, dtype=jnp.int32)).astype(jnp.float32)
    pool_counts = lax.optimization_barrier(jnp.sum(members * valid_mask, axis=(1, 2)))
    pooled = jnp.einsum('nhws,nhwc->nsc', members, masked, precision=highest) / pool_counts[..., None]
    pool_out = jnp.einsum('nsc,cb->nsb', pooled, pool_kernel, precision=highest)
    entries = pool_out.shape[0] * pool_out.shape[1]
    pool_pre = normalize(pool_out, jnp.ones_like(pool_out[..., :1]), entries, gain_rows[4], shift_rows[4], (0, 1))
    pool_act = low(jax.nn.silu(pool_pre))
    branch_acts.append(jnp.einsum('nhws,nsb->nhwb', members, pool_act, precision=highest))
    concat_act = jnp.concatenate(branch_acts, axis=-1)
    proj_out = low_back(jnp.einsum('nhwk,kb->nhwb', concat_act, proj_kernel, precision=highest))
    proj_pre = normalize(proj_out, valid_mask, pixel_total, gain_rows[5], shift_rows[5], pixel_dims)
    proj_act = low(jax.nn.silu(proj_pre))
    return upsample_axis(upsample_axis(proj_act, 1), 2)

def reference(features, segment_map, pixel_mask, inner_weight, atrous_weight, pool_weight, proj_weight, norm_gains, norm_shifts, cotangent):
    valid_mask = pixel_mask.astype(jnp.float32)[..., None]

    def wrapped(feature_in, inner_kernel, atrous_kernel, pool_kernel, proj_kernel, gain_rows, shift_rows):
        return forward(feature_in, inner_kernel, atrous_kernel, pool_kernel, proj_kernel, gain_rows, shift_rows, segment_map, valid_mask)
    primal = (features.astype(jnp.float32), inner_weight.astype(jnp.float32), atrous_weight.astype(jnp.float32), pool_weight.astype(jnp.float32), proj_weight.astype(jnp.float32), norm_gains.astype(jnp.float32), norm_shifts.astype(jnp.float32))
    output, pullback = jax.vjp(wrapped, *primal)
    gradients = pullback(cotangent.astype(jnp.float32))
    return (output.astype(jnp.bfloat16), gradients[0], gradients[1], gradients[2], gradients[3], gradients[4], gradients[5], gradients[6])
```

```python
import functools

import jax
import jax.numpy as jnp
from jax import lax
from jax.experimental import pallas as pl
from jax.experimental.pallas import tpu as pltpu
from jax.sharding import PartitionSpec as P

COL_IMAGES = 2
LANES = 128
SIDE = 24
GROUP = 6

dilations = (6, 12, 18)
epsilon = 1e-05
prev_weights = (0.375, 0.125, 0.0, 0.0)
self_weights = (0.625, 0.875, 0.875, 0.625)
next_weights = (0.0, 0.0, 0.125, 0.375)
vmem_bytes = 58 << 20
in_place = pl.BlockSpec(memory_space=pl.ANY)
in_vmem = pl.BlockSpec(memory_space=pltpu.VMEM)


def swap(values, axis, bit):
    count = lax.axis_size(axis)
    return lax.ppermute(values, axis, [(i, i ^ bit) for i in range(count)])


def bits_of(count):
    bits, bit = [], 1
    while bit < count:
        bits.append(bit)
        bit *= 2
    return bits


def sum_over(values, axis):
    for bit in bits_of(lax.axis_size(axis)):
        values = values + swap(values, axis, bit)
    return values


def gather_over(values, axis):
    index = lax.axis_index(axis)
    for bit in bits_of(lax.axis_size(axis)):
        other = swap(values, axis, bit)
        values = jnp.where(
            (index & bit) == 0,
            jnp.concatenate([values, other], axis=0),
            jnp.concatenate([other, values], axis=0),
        )
    return values


def scatter_over(values, axis):
    index = lax.axis_index(axis)
    for bit in reversed(bits_of(lax.axis_size(axis))):
        half = values.shape[0] // 2
        low, high = values[:half], values[half:]
        mine = (index & bit) == 0
        values = jnp.where(mine, low, high) + swap(jnp.where(mine, high, low), axis, bit)
    return values


def step_rows(values, steps, wrap=False):
    count = lax.axis_size("rows")
    if wrap:
        pairs = [(i, (i + steps) % count) for i in range(count)]
    else:
        pairs = [(i, i + steps) for i in range(count) if 0 <= i + steps < count]
    return lax.ppermute(values, "rows", pairs)


def halves(first, lower, upper):
    return jnp.where(
        first, jnp.concatenate([lower, upper], axis=0), jnp.concatenate([upper, lower], axis=0)
    )


def place():
    row = lax.axis_index("rows")
    return row // 2, row % 2, lax.axis_index("canvas")


def copy_all(copies, sems):
    started = []
    for number, (source, target) in enumerate(copies):
        copy = pltpu.make_async_copy(source, target, sems.at[number])
        copy.start()
        started.append(copy)
    return started


def spread(mask, width):
    return jnp.concatenate([mask] * (width // LANES), axis=1)


def shift_columns(source, rows, columns, distance, masks, side, left, right):
    width = source.shape[-1]
    empty = jnp.zeros((GROUP, SIDE, width), jnp.float32)
    side[:, 0:SIDE, :] = empty
    side[:, SIDE + columns : columns + 2 * SIDE, :] = empty
    mask_left = spread(masks[0], width)
    mask_right = spread(masks[1], width)

    def step(group, carry):
        starts = [
            pl.multiple_of((group * GROUP + member) * columns, columns) for member in range(GROUP)
        ]
        for member, start in enumerate(starts):
            side[member, SIDE : SIDE + columns, :] = source[pl.ds(start, columns), :].astype(
                jnp.float32
            )
        for member, start in enumerate(starts):
            first = SIDE - distance
            left[pl.ds(start, columns), :] = (
                side[member, first : first + columns, :] * mask_left
            ).astype(jnp.bfloat16)
            first = SIDE + distance
            right[pl.ds(start, columns), :] = (
                side[member, first : first + columns, :] * mask_right
            ).astype(jnp.bfloat16)
        return carry

    lax.fori_loop(0, rows // GROUP, step, 0)


def forward_kernel(
    dilation, with_inner, geometry, own, other, shard, *refs
):
    rows, columns, shards, parts, piece = geometry
    received = refs[: (shards - 1) * parts]
    (
        row_mask,
        col_mask,
        main,
        above,
        below,
        weights_out,
        *rest,
    ) = refs[(shards - 1) * parts :]
    if with_inner:
        inner_out, *rest = rest
    feat, side, left, right, weights, total, sems, out_sem = rest
    depth, across, canvas = place()
    part = canvas % parts
    pixels = rows * columns
    band = pixels // 2
    slice_rows = parts * piece
    feature_copies = copy_all(
        [
            (own, feat.at[pl.ds(pl.multiple_of(across * band, band), band)]),
            (other, feat.at[pl.ds(pl.multiple_of((1 - across) * band, band), band)]),
        ],
        sems,
    )
    copies = [
        (shard, weights.at[:, pl.ds(pl.multiple_of(depth * slice_rows, slice_rows), slice_rows)])
    ]
    for step in range(1, shards):
        origin = lax.rem(depth - step + shards, shards)
        for index in range(parts):
            start = origin * slice_rows + (part ^ index) * piece
            copies.append(
                (
                    received[(step - 1) * parts + index],
                    weights.at[:, pl.ds(pl.multiple_of(start, piece), piece)],
                )
            )
    weight_copies = copy_all(copies, sems.at[pl.ds(2, len(copies))])
    for copy in feature_copies:
        copy.wait()
    shift_columns(feat, rows, columns, dilation, (col_mask[0], col_mask[1]), side, left, right)
    total[...] = jnp.zeros_like(total)
    for copy in weight_copies:
        copy.wait()
    keep = pltpu.make_async_copy(weights, weights_out, out_sem)
    keep.start()
    tile = pixels // 4
    shift = dilation * columns
    for row_tap in range(3):
        for first in range(0, pixels, tile):
            span = slice(first, first + tile)
            product = jnp.dot(
                left[span, :], weights[3 * row_tap], preferred_element_type=jnp.float32
            )
            product += jnp.dot(
                feat[span, :], weights[3 * row_tap + 1], preferred_element_type=jnp.float32
            )
            product += jnp.dot(
                right[span, :], weights[3 * row_tap + 2], preferred_element_type=jnp.float32
            )
            mask = spread(row_mask[row_tap, span, :].astype(jnp.float32), product.shape[1])
            target = (2 - row_tap) * shift + first
            total[target : target + tile, :] += product * mask
    if with_inner:
        for first in range(0, pixels, tile):
            span = slice(first, first + tile)
            inner_out[span, :] = jnp.dot(
                feat[span, :], weights[9], preferred_element_type=jnp.float32
            )
    above[...] = total[0:shift, :].astype(jnp.bfloat16)
    main[...] = total[shift : shift + pixels, :]
    below[...] = total[shift + pixels : 2 * shift + pixels, :].astype(jnp.bfloat16)
    keep.wait()


def forward_branch(own, other, shard, received, row_mask, col_mask, dilation, with_inner, geometry):
    rows, columns, shards, parts, piece = geometry
    pixels = rows * columns
    channels = own.shape[1]
    width = shard.shape[2]
    taps = shard.shape[0]
    shift = dilation * columns
    out_shape = [
        jax.ShapeDtypeStruct((pixels, width), jnp.float32),
        jax.ShapeDtypeStruct((shift, width), jnp.bfloat16),
        jax.ShapeDtypeStruct((shift, width), jnp.bfloat16),
        jax.ShapeDtypeStruct((taps, channels, width), jnp.bfloat16),
    ]
    out_specs = [in_vmem, in_vmem, in_vmem, in_place]
    if with_inner:
        out_shape.append(jax.ShapeDtypeStruct((pixels, width), jnp.float32))
        out_specs.append(in_vmem)
    copies = 3 + len(received)
    return pl.pallas_call(
        functools.partial(forward_kernel, dilation, with_inner, geometry),
        in_specs=[in_place] * copies + [in_vmem, in_vmem],
        out_specs=out_specs,
        out_shape=out_shape,
        scratch_shapes=[
            pltpu.VMEM((pixels, channels), jnp.bfloat16),
            pltpu.VMEM((GROUP, columns + 2 * SIDE, channels), jnp.float32),
            pltpu.VMEM((pixels, channels), jnp.bfloat16),
            pltpu.VMEM((pixels, channels), jnp.bfloat16),
            pltpu.VMEM((taps, channels, width), jnp.bfloat16),
            pltpu.VMEM((pixels + 2 * shift, width), jnp.float32),
            pltpu.SemaphoreType.DMA((copies,)),
            pltpu.SemaphoreType.DMA,
        ],
        compiler_params=pltpu.CompilerParams(vmem_limit_bytes=vmem_bytes),
        cost_estimate=pl.CostEstimate(
            flops=2 * taps * pixels * channels * width,
            bytes_accessed=2 * pixels * channels + 4 * taps * channels * width,
            transcendentals=0,
        ),
        name=f"forward_{dilation}",
    )(own, other, shard, *received, row_mask, col_mask)


def load_gradient(rows, columns, dilation, refs, target, sems):
    depth, across, canvas = place()
    own, other, above, below = refs
    band = rows * columns // 2
    shift = dilation * columns
    return copy_all(
        [
            (own, target.at[pl.ds(pl.multiple_of(shift + across * band, columns), band)]),
            (other, target.at[pl.ds(pl.multiple_of(shift + (1 - across) * band, columns), band)]),
            (above, target.at[pl.ds(0, shift)]),
            (below, target.at[pl.ds(shift + 2 * band, shift)]),
        ],
        sems,
    )


def weight_kernel(dilation, with_inner, geometry, own, other, *refs):
    rows, columns, shards, parts, piece = geometry
    gradient, refs = refs[:4], refs[4:]
    if with_inner:
        inner, refs = refs[:2], refs[2:]
    row_mask, col_mask, keep, send, feat, side, moved, result, sems = refs
    tap = pl.program_id(0)
    depth, across, canvas = place()
    part = canvas % parts
    pixels = rows * columns
    band = pixels // 2
    shift = dilation * columns

    @pl.when(tap == 0)
    def _():
        offsets = [
            pl.multiple_of(across * band, band),
            pl.multiple_of((1 - across) * band, band),
        ]
        copies = [(own, feat.at[pl.ds(offsets[0], band)]), (other, feat.at[pl.ds(offsets[1], band)])]
        if with_inner:
            copies += [
                (inner[0], moved.at[3, pl.ds(offsets[0], band)]),
                (inner[1], moved.at[3, pl.ds(offsets[1], band)]),
            ]
        first = load_gradient(rows, columns, dilation, gradient, moved.at[1], sems)
        second = copy_all(copies, sems.at[pl.ds(4, len(copies))])
        for copy in first:
            copy.wait()
        shift_columns(
            moved.at[1],
            rows + 2 * dilation,
            columns,
            dilation,
            (col_mask[0], col_mask[1]),
            side,
            moved.at[2],
            moved.at[0],
        )
        for copy in second:
            copy.wait()

    row_tap = tap // 3
    source = jnp.where(tap < 9, tap % 3, 3)
    offset = jnp.where(tap < 9, (2 - row_tap) * shift, 0)
    mask = spread(row_mask[row_tap], result.shape[1])
    shifted = moved[source, pl.ds(pl.multiple_of(offset, columns), pixels), :] * mask
    result[...] = lax.dot_general(
        feat[...], shifted, (((0,), (0,)), ((), ())), preferred_element_type=jnp.float32
    )
    low = part & 1
    for origin in range(shards):
        step = lax.rem(depth - origin + shards, shards)
        for pair in range(parts // 2):
            slot = pair ^ (part // 2)
            base = origin * parts * piece + 2 * pair * piece
            start = pl.multiple_of(base + low * piece, piece)
            keep[slot, step, 0] = result[pl.ds(start, piece), :].astype(jnp.bfloat16)
            start = pl.multiple_of(base + (1 - low) * piece, piece)
            send[slot, step, 0] = result[pl.ds(start, piece), :].astype(jnp.bfloat16)


def weight_branch(own, other, gradient, inner, row_mask, col_mask, dilation, geometry):
    rows, columns, shards, parts, piece = geometry
    pixels = rows * columns
    channels = own.shape[1]
    width = gradient[0].shape[1]
    with_inner = inner is not None
    taps = 10 if with_inner else 9
    extended = pixels + 2 * dilation * columns
    block = pl.BlockSpec((parts // 2, shards, 1, piece, width), lambda t: (0, 0, t, 0, 0))
    part_shape = jax.ShapeDtypeStruct((parts // 2, shards, taps, piece, width), jnp.bfloat16)
    arrays = [own, other, *gradient] + (list(inner) if with_inner else [])
    whole = lambda shape: pl.BlockSpec(shape, lambda t: (0,) * len(shape))
    return pl.pallas_call(
        functools.partial(weight_kernel, dilation, with_inner, geometry),
        grid=(taps,),
        in_specs=[in_place] * len(arrays) + [whole(row_mask.shape), whole(col_mask.shape)],
        out_specs=[block, block],
        out_shape=[part_shape, part_shape],
        scratch_shapes=[
            pltpu.VMEM((pixels, channels), jnp.bfloat16),
            pltpu.VMEM((GROUP, columns + 2 * SIDE, width), jnp.float32),
            pltpu.VMEM((taps - 6, extended, width), jnp.bfloat16),
            pltpu.VMEM((channels, width), jnp.float32),
            pltpu.SemaphoreType.DMA((len(arrays),)),
        ],
        compiler_params=pltpu.CompilerParams(vmem_limit_bytes=vmem_bytes),
        cost_estimate=pl.CostEstimate(
            flops=2 * taps * pixels * channels * width,
            bytes_accessed=2 * pixels * channels + 2 * taps * channels * width,
            transcendentals=0,
        ),
        name=f"weight_{dilation}",
    )(*arrays, row_mask, col_mask)


def feature_kernel(geometry, block_channels, *refs):
    rows, columns, shards, parts, piece = geometry
    branches = len(dilations)
    gradients = [refs[4 * branch : 4 * branch + 4] for branch in range(branches)]
    refs = refs[4 * branches :]
    inner, refs = refs[:2], refs[2:]
    row_masks, refs = refs[:branches], refs[branches:]
    col_masks, refs = refs[:branches], refs[branches:]
    weights, refs = refs[:branches], refs[branches:]
    keep, send, side, straight, result, sems = refs[0], refs[1], refs[2], refs[3], refs[4], refs[5]
    moved = refs[6:]
    depth, across, canvas = place()
    pixels = rows * columns
    band = pixels // 2

    @pl.when(pl.program_id(0) == 0)
    def _():
        offsets = [
            pl.multiple_of(across * band, band),
            pl.multiple_of((1 - across) * band, band),
        ]
        waits = [
            load_gradient(
                rows, columns, dilation, gradients[branch], moved[branch].at[1], sems.at[pl.ds(4 * branch, 4)]
            )
            for branch, dilation in enumerate(dilations)
        ]
        last = copy_all(
            [
                (inner[0], straight.at[pl.ds(offsets[0], band)]),
                (inner[1], straight.at[pl.ds(offsets[1], band)]),
            ],
            sems.at[pl.ds(4 * branches, 2)],
        )
        for branch, dilation in enumerate(dilations):
            for copy in waits[branch]:
                copy.wait()
            shift_columns(
                moved[branch].at[1],
                rows + 2 * dilation,
                columns,
                dilation,
                (col_masks[branch][0], col_masks[branch][1]),
                side,
                moved[branch].at[2],
                moved[branch].at[0],
            )
        for copy in last:
            copy.wait()

    tile = pixels // 4
    for first in range(0, pixels, tile):
        span = slice(first, first + tile)
        product = lax.dot_general(
            straight[span, :],
            weights[-1][9],
            (((1,), (1,)), ((), ())),
            preferred_element_type=jnp.float32,
        )
        for branch, dilation in enumerate(dilations):
            shift = dilation * columns
            for row_tap in range(3):
                mask = spread(row_masks[branch][row_tap, span, :], straight.shape[1])
                start = (2 - row_tap) * shift + first
                for col_tap in range(3):
                    product += lax.dot_general(
                        moved[branch][col_tap, start : start + tile, :] * mask,
                        weights[branch][3 * row_tap + col_tap],
                        (((1,), (1,)), ((), ())),
                        preferred_element_type=jnp.float32,
                    )
        result[span, :] = product
    keep[...] = result[pl.ds(pl.multiple_of(across * band, band), band), :]
    send[...] = result[pl.ds(pl.multiple_of((1 - across) * band, band), band), :].astype(
        jnp.bfloat16
    )


def feature_branches(gradients, inner, row_masks, col_masks, weights, geometry):
    rows, columns, shards, parts, piece = geometry
    pixels = rows * columns
    band = pixels // 2
    channels, width = weights[0].shape[1:]
    block_channels = min(256, channels)
    arrays = [array for gradient in gradients for array in gradient] + list(inner)
    whole = lambda array: pl.BlockSpec(array.shape, lambda t: (0,) * array.ndim)
    taps = sum(array.shape[0] for array in weights)
    return pl.pallas_call(
        functools.partial(feature_kernel, geometry, block_channels),
        grid=(channels // block_channels,),
        in_specs=[in_place] * len(arrays)
        + [whole(array) for array in row_masks]
        + [whole(array) for array in col_masks]
        + [
            pl.BlockSpec((array.shape[0], block_channels, width), lambda t: (0, t, 0))
            for array in weights
        ],
        out_specs=[pl.BlockSpec((band, block_channels), lambda t: (0, t))] * 2,
        out_shape=[
            jax.ShapeDtypeStruct((band, channels), jnp.float32),
            jax.ShapeDtypeStruct((band, channels), jnp.bfloat16),
        ],
        scratch_shapes=[
            pltpu.VMEM((GROUP, columns + 2 * SIDE, width), jnp.float32),
            pltpu.VMEM((pixels, width), jnp.bfloat16),
            pltpu.VMEM((pixels, block_channels), jnp.float32),
            pltpu.SemaphoreType.DMA((len(arrays),)),
        ]
        + [
            pltpu.VMEM((3, pixels + 2 * dilation * columns, width), jnp.bfloat16)
            for dilation in dilations
        ],
        compiler_params=pltpu.CompilerParams(vmem_limit_bytes=vmem_bytes),
        cost_estimate=pl.CostEstimate(
            flops=2 * taps * pixels * channels * width,
            bytes_accessed=6 * band * channels + 2 * taps * channels * width,
            transcendentals=0,
        ),
        name="feature_gradient",
    )(*arrays, *row_masks, *col_masks, *weights)


def interp_matrix(out_first, out_count, in_first, in_count, row_limit):
    out_rows = out_first + jnp.arange(out_count, dtype=jnp.int32)
    source = jnp.floor_divide(out_rows, 4)
    residue = out_rows - 4 * source
    targets = in_first + jnp.arange(in_count, dtype=jnp.int32)
    matrix = jnp.zeros((out_count, in_count), jnp.float32)
    for offset, coeffs in ((-1, prev_weights), (0, self_weights), (1, next_weights)):
        factor = jnp.zeros((out_count,), jnp.float32)
        for member in range(4):
            factor = factor + jnp.where(residue == member, coeffs[member], 0.0)
        clamped = jnp.clip(source + offset, 0, row_limit - 1)
        matrix = matrix + factor[:, None] * (clamped[:, None] == targets[None, :]).astype(
            jnp.float32
        )
    return matrix


def silu_slope(values):
    logistic = jax.nn.sigmoid(values)
    return logistic * (1.0 + values * (1.0 - logistic))


def normalize(values, sum_rows, total_count, scale_vec, shift_vec):
    average = sum_rows[0] / total_count
    spread_of = sum_rows[1] / total_count - average * average
    inverse = lax.rsqrt(spread_of + epsilon)
    centered = (values - average) * inverse
    return (centered, inverse, scale_vec * centered + shift_vec)


def input_grad(slope, centered, inverse, scale_vec, totals, total_count, weight_map):
    return (
        scale_vec
        * inverse
        * (slope - weight_map * (totals[0] + centered * totals[1]) / total_count)
    )


def moments_of(values, weight_map):
    weighted = weight_map * values
    return [jnp.sum(weighted, axis=0), jnp.sum(weighted * values, axis=0)]


def per_device(
    features,
    segment_map,
    pixel_mask,
    inner_weight,
    atrous_weight,
    pool_weight,
    proj_weight,
    norm_gains,
    norm_shifts,
    cotangent,
):
    highest = lax.Precision.HIGHEST
    row_count = lax.axis_size("rows")
    canvas_count = lax.axis_size("canvas") * features.shape[0]
    band_rows, columns, channels = features.shape[1:]
    branch_width = norm_gains.shape[1]
    canvas_rows = band_rows * row_count
    image_count = COL_IMAGES * (canvas_rows // 36)
    row_index = lax.axis_index("rows")
    canvas_index = lax.axis_index("canvas")
    shards = row_count // 2
    depth = row_index // 2
    first_band = row_index % 2 == 0
    top_row = (row_index == 0).astype(jnp.float32)
    row_first = row_index * band_rows
    rows = 2 * band_rows
    band = band_rows * columns
    pixels = rows * columns
    slice_rows = channels // row_count
    parts = min(lax.axis_size("canvas"), max(slice_rows // 16, 1))
    piece = slice_rows // parts
    part = canvas_index % parts
    geometry = (rows, columns, shards, parts, piece)

    flat_mask = pixel_mask.reshape(band, 1)
    valid_mask = flat_mask.astype(jnp.float32)
    segments = segment_map.reshape(band)
    row_ids = segment_map[0, :, 0] // COL_IMAGES + 1
    col_ids = segment_map[0, 0, :] % COL_IMAGES
    both_ids = halves(first_band, row_ids, swap(row_ids, "rows", 1))
    reach = max(dilations)
    all_ids = jnp.concatenate(
        [step_rows(both_ids[rows - reach :], 2), both_ids, step_rows(both_ids[:reach], -2)]
    )
    row_masks, col_masks = [], []
    places = jnp.arange(columns)
    for dilation in dilations:
        checks = []
        for row_tap in range(3):
            start = reach - (row_tap - 1) * dilation
            checks.append(all_ids[start : start + rows] == both_ids)
        checks.append(jnp.ones_like(checks[0]))
        table = jnp.stack(checks).astype(jnp.bfloat16)
        row_masks.append(
            jnp.broadcast_to(table[:, :, None, None], (4, rows, columns, LANES)).reshape(
                4, pixels, LANES
            )
        )
        table = []
        for offset in (-dilation, dilation):
            moved = places + offset
            inside = (moved >= 0) & (moved < columns)
            table.append(inside & (jnp.roll(col_ids, -offset) == col_ids))
        table = jnp.stack(table).astype(jnp.float32)
        col_masks.append(jnp.broadcast_to(table[:, :, None], (2, columns, LANES)))

    masked = features.reshape(band, channels) * flat_mask.astype(jnp.bfloat16)
    slices = [masked[:, i * slice_rows : (i + 1) * slice_rows] for i in range(row_count)]
    even = jnp.concatenate(slices[0::2], axis=1)
    odd = jnp.concatenate(slices[1::2], axis=1)
    feat_own, feat_send = lax.optimization_barrier(
        (jnp.where(first_band, even, odd), jnp.where(first_band, odd, even))
    )
    feat_other = swap(feat_send, "rows", 1)

    flat_atrous = atrous_weight.reshape(len(dilations), 9, slice_rows, branch_width)
    shard_weights = [flat_atrous[branch] for branch in range(len(dilations))]
    shard_weights[-1] = jnp.concatenate([shard_weights[-1], inner_weight[None]], axis=0)
    received = []
    for branch in (2, 1, 0):
        quarter = lax.dynamic_slice_in_dim(shard_weights[branch], part * piece, piece, axis=1)
        pieces = [[step_rows(quarter, 2 * step, wrap=True)] for step in range(1, shards)]
        for bit in reversed(bits_of(parts)):
            for chain in pieces:
                chain.extend([swap(item, "canvas", bit) for item in chain])
        order = [0]
        for bit in reversed(bits_of(parts)):
            order.extend([item | bit for item in order])
        received.append([chain[order.index(j)] for chain in pieces for j in range(parts)])
    received = received[::-1]
    proj_full = gather_over(proj_weight, "rows")

    members = (segments[:, None] == jnp.arange(image_count, dtype=jnp.int32)).astype(jnp.float32)
    member_low = members.astype(jnp.bfloat16)
    seg_sums = jnp.einsum("ps,pc->sc", member_low, masked, preferred_element_type=jnp.float32)
    seg_counts = jnp.sum(members * valid_mask, axis=0)
    seg_all = sum_over(
        jnp.concatenate(
            [seg_sums, jnp.broadcast_to(seg_counts[:, None], (image_count, LANES))], axis=1
        ),
        "rows",
    )
    total_counts = seg_all[:, channels : channels + 1]
    pooled = lax.dynamic_slice_in_dim(seg_all, row_index * slice_rows, slice_rows, axis=1)
    pooled = pooled / total_counts
    pool_matrix = pool_weight.astype(jnp.float32)
    pool_out = sum_over(jnp.dot(pooled, pool_matrix, precision=highest), "rows")

    conv_outs = [None] * (len(dilations) + 1)
    weights_full = [None] * len(dilations)
    for branch in (2, 1, 0):
        dilation = dilations[branch]
        with_inner = branch == len(dilations) - 1
        result = forward_branch(
            feat_own,
            feat_other,
            shard_weights[branch],
            received[branch],
            row_masks[branch],
            col_masks[branch],
            dilation,
            with_inner,
            geometry,
        )
        main, above, below, weights_full[branch] = result[:4]
        shift = dilation * columns
        main = jnp.concatenate(
            [
                main[:shift] + step_rows(below, 2).astype(jnp.float32),
                main[shift : pixels - shift],
                main[pixels - shift :] + step_rows(above, -2).astype(jnp.float32),
            ],
            axis=0,
        )
        sums = [(branch + 1, main)]
        if with_inner:
            sums.append((0, result[4]))
        for number, partial in sums:
            mine = jnp.where(first_band, partial[:band], partial[band:])
            sent = jnp.where(first_band, partial[band:], partial[:band]).astype(jnp.bfloat16)
            conv_outs[number] = mine + swap(sent, "rows", 1).astype(jnp.float32)

    rows_of = []
    for conv_out in conv_outs:
        rows_of += moments_of(conv_out, valid_mask)
    rows_of += [
        top_row * jnp.sum(pool_out, axis=0),
        top_row * jnp.sum(pool_out * pool_out, axis=0),
        jnp.broadcast_to(jnp.sum(valid_mask), (branch_width,)),
    ]
    sums = sum_over(sum_over(jnp.stack(rows_of), "rows"), "canvas")
    pixel_total = sums[10]
    entries = float(canvas_count * image_count)
    normals = [
        normalize(
            conv_out,
            sums[2 * branch : 2 * branch + 2],
            pixel_total,
            norm_gains[branch],
            norm_shifts[branch],
        )
        for branch, conv_out in enumerate(conv_outs)
    ]
    pool_norm = normalize(pool_out, sums[8:10], entries, norm_gains[4], norm_shifts[4])
    pool_act = jax.nn.silu(pool_norm[2]).astype(jnp.bfloat16)
    pool_map = jnp.dot(member_low, pool_act, preferred_element_type=jnp.float32)
    concat_act = jnp.concatenate(
        [jax.nn.silu(item[2]).astype(jnp.bfloat16) for item in normals]
        + [pool_map.astype(jnp.bfloat16)],
        axis=-1,
    )
    proj_out = jnp.dot(concat_act, proj_full, preferred_element_type=jnp.float32)
    proj_totals = sum_over(
        sum_over(jnp.stack(moments_of(proj_out, valid_mask)), "rows"), "canvas"
    )
    proj_norm = normalize(proj_out, proj_totals, pixel_total, norm_gains[5], norm_shifts[5])
    proj_act = jax.nn.silu(proj_norm[2]).astype(jnp.bfloat16)

    act_rows = proj_act.reshape(band_rows, columns, branch_width)
    ext_act = jnp.concatenate(
        [step_rows(act_rows[band_rows - 1 :], 1), act_rows, step_rows(act_rows[:1], -1)], axis=0
    )
    row_matrix = interp_matrix(
        4 * row_first, 4 * band_rows, row_first - 1, band_rows + 2, canvas_rows
    ).astype(jnp.bfloat16)
    col_matrix = interp_matrix(0, 4 * columns, 0, columns, columns)
    rows_up = jnp.einsum("or,rwb->owb", row_matrix, ext_act, preferred_element_type=jnp.float32)
    upsampled = jnp.einsum("pw,owb->opb", col_matrix, rows_up, precision=highest).astype(
        jnp.bfloat16
    )
    col_grad = jnp.einsum(
        "pw,opb->owb",
        col_matrix.astype(jnp.bfloat16),
        cotangent[0],
        preferred_element_type=jnp.float32,
    )
    grad_ext = jnp.concatenate(
        [step_rows(col_grad[4 * band_rows - 2 :], 1), col_grad, step_rows(col_grad[:2], -1)], axis=0
    )
    back_matrix = interp_matrix(
        4 * row_first - 2, 4 * band_rows + 4, row_first, band_rows, canvas_rows
    )
    act_grad = jnp.einsum("or,owb->rwb", back_matrix, grad_ext, precision=highest)
    act_grad = act_grad.reshape(band, branch_width)

    proj_slope = act_grad * silu_slope(proj_norm[2])
    proj_local = jnp.stack(
        [jnp.sum(proj_slope, axis=0), jnp.sum(proj_slope * proj_norm[0], axis=0)]
    )
    proj_grad_totals = sum_over(sum_over(proj_local, "rows"), "canvas")
    proj_grad = input_grad(
        proj_slope,
        proj_norm[0],
        proj_norm[1],
        norm_gains[5],
        proj_grad_totals,
        pixel_total,
        valid_mask,
    ).astype(jnp.bfloat16)
    joined_grad = lax.dot_general(
        proj_grad, proj_full, (((1,), (1,)), ((), ())), preferred_element_type=jnp.float32
    )
    slopes = [
        joined_grad[:, branch * branch_width : (branch + 1) * branch_width]
        * silu_slope(normals[branch][2])
        for branch in range(4)
    ]
    rows_of = []
    for branch, slope in enumerate(slopes):
        rows_of += [jnp.sum(slope, axis=0), jnp.sum(slope * normals[branch][0], axis=0)]
    seg_grads = lax.dot_general(
        members, joined_grad[:, 4 * branch_width :], (((0,), (0,)), ((), ())), precision=highest
    )
    pool_terms = seg_grads * silu_slope(pool_norm[2])
    rows_of += [jnp.sum(pool_terms, axis=0), jnp.sum(pool_terms * pool_norm[0], axis=0)]
    sums = sum_over(jnp.concatenate([jnp.stack(rows_of), seg_grads], axis=0), "rows")
    seg_grads = sums[10:]
    sums = sum_over(sums[:10], "canvas")
    branch_totals = [sums[2 * branch : 2 * branch + 2] for branch in range(5)]
    conv_grads = [
        input_grad(
            slopes[branch],
            normals[branch][0],
            normals[branch][1],
            norm_gains[branch],
            branch_totals[branch],
            pixel_total,
            valid_mask,
        ).astype(jnp.bfloat16)
        for branch in range(4)
    ]

    pool_grad = input_grad(
        seg_grads * silu_slope(pool_norm[2]),
        pool_norm[0],
        pool_norm[1],
        norm_gains[4],
        branch_totals[4],
        entries,
        1.0,
    )
    pooled_grad = (
        lax.dot_general(pool_matrix, pool_grad, (((1,), (1,)), ((), ())), precision=highest)
        / total_counts[:, 0]
    )
    pooled_grad = gather_over(pooled_grad, "rows")
    grad_pool = sum_over(
        lax.dot_general(pooled, pool_grad, (((0,), (0,)), ((), ())), precision=highest), "canvas"
    )

    others = [None] * 4
    gradients = [None] * len(dilations)
    for branch, dilation in enumerate(dilations):
        grad = conv_grads[branch + 1]
        other = swap(grad, "rows", 1)
        shift = dilation * columns
        top = jnp.where(first_band, grad[:shift], other[:shift])
        bottom = jnp.where(first_band, other[band - shift :], grad[band - shift :])
        gradients[branch] = (grad, other, step_rows(bottom, 2), step_rows(top, -2))
    inner_grads = (conv_grads[0], swap(conv_grads[0], "rows", 1))

    finished = []
    for branch, dilation in enumerate(dilations):
        kept, sent = weight_branch(
            feat_own,
            feat_other,
            gradients[branch],
            inner_grads if branch == len(dilations) - 1 else None,
            row_masks[branch],
            col_masks[branch],
            dilation,
            geometry,
        )
        part_sum = kept.astype(jnp.float32) + swap(sent, "canvas", 1).astype(jnp.float32)
        for bit in bits_of(parts)[1:]:
            half = part_sum.shape[0] // 2
            index = jnp.arange(half)
            low = jnp.stack([part_sum[2 * i] for i in range(half)])
            high = jnp.stack([part_sum[2 * i + 1] for i in range(half)]).astype(jnp.bfloat16)
            part_sum = low + swap(high, "canvas", bit).astype(jnp.float32)
        part_sum = part_sum[0]
        moving = part_sum.astype(jnp.bfloat16)
        total = part_sum[0]
        for step in range(1, shards):
            total = total + step_rows(moving[step], -2 * step, wrap=True).astype(jnp.float32)
        for bit in bits_of(lax.axis_size("canvas")):
            if bit >= parts:
                total = total + swap(total, "canvas", bit)
        blocks = lax.optimization_barrier(total.astype(jnp.bfloat16))[:, None]
        for bit in reversed(bits_of(parts)):
            other = swap(blocks, "canvas", bit)
            here = (part & bit) == 0
            stacked = jnp.where(
                here, jnp.stack([blocks, other], axis=2), jnp.stack([other, blocks], axis=2)
            )
            blocks = stacked.reshape(
                (stacked.shape[0], stacked.shape[1] * 2) + stacked.shape[3:]
            )
        finished.append(
            blocks.reshape(blocks.shape[0], slice_rows, branch_width).astype(jnp.float32)
        )
    grad_inner = finished[-1][9]
    grad_atrous = jnp.stack([finished[0], finished[1], finished[2][:9]])

    grad_proj = lax.dot_general(
        concat_act, proj_grad, (((0,), (0,)), ((), ())), preferred_element_type=jnp.float32
    )
    grad_proj = sum_over(scatter_over(grad_proj, "rows"), "canvas")

    kept, sent = feature_branches(
        gradients, inner_grads, row_masks, col_masks, weights_full, geometry
    )
    other = swap(sent, "rows", 1).astype(jnp.float32)
    even = jnp.where(first_band, kept, other)
    odd = jnp.where(first_band, other, kept)
    joined = []
    for shard in range(shards):
        span = slice(shard * slice_rows, (shard + 1) * slice_rows)
        joined += [even[:, span], odd[:, span]]
    spread_pool = lax.dot_general(
        members, pooled_grad, (((1,), (1,)), ((), ())), precision=highest
    )
    grad_features = (jnp.concatenate(joined, axis=1) + spread_pool) * valid_mask

    grad_gains = jnp.stack([totals[1] for totals in branch_totals] + [proj_grad_totals[1]])
    grad_shifts = jnp.stack([totals[0] for totals in branch_totals] + [proj_grad_totals[0]])
    return (
        upsampled[None],
        grad_features.reshape(features.shape),
        grad_inner,
        grad_atrous,
        grad_pool,
        grad_proj,
        grad_gains,
        grad_shifts,
    )


def solution(mesh):
    in_specs = (
        P("canvas", "rows", None, None),
        P("canvas", "rows", None),
        P("canvas", "rows", None),
        P("rows", None),
        P(None, None, "rows", None),
        P("rows", None),
        P("rows", None),
        P(),
        P(),
        P("canvas", "rows", None, None),
    )
    out_specs = (
        P("canvas", "rows", None, None),
        P("canvas", "rows", None, None),
        P("rows", None),
        P(None, None, "rows", None),
        P("rows", None),
        P("rows", None),
        P(),
        P(),
    )
    return jax.shard_map(
        per_device, mesh=mesh, in_specs=in_specs, out_specs=out_specs, check_vma=False
    )
```

```python
import functools

import jax
import jax.numpy as jnp
from jax import lax
from jax.experimental import pallas as pl
from jax.experimental.pallas import tpu as pltpu
from jax.sharding import PartitionSpec as P

COL_IMAGES = 2
LANES = 128
SIDE = 24
TILE = 16
GROUP = 6

dilations = (6, 12, 18)
epsilon = 1e-05
prev_weights = (0.375, 0.125, 0.0, 0.0)
self_weights = (0.625, 0.875, 0.875, 0.625)
next_weights = (0.0, 0.0, 0.125, 0.375)
vmem_bytes = 58 << 20
in_place = pl.BlockSpec(memory_space=pl.ANY)
in_vmem = pl.BlockSpec(memory_space=pltpu.VMEM)


def swap(values, axis, bit):
    count = lax.axis_size(axis)
    return lax.ppermute(values, axis, [(i, i ^ bit) for i in range(count)])


def bits_of(count):
    bits, bit = [], 1
    while bit < count:
        bits.append(bit)
        bit *= 2
    return bits


def sum_over(values, axis):
    bits = bits_of(lax.axis_size(axis))
    for first in range(0, len(bits), 2):
        pair = bits[first : first + 2]
        found = [swap(values, axis, bit) for bit in pair]
        if len(pair) == 2:
            found.append(swap(values, axis, pair[0] ^ pair[1]))
            values = (values + found[0]) + (found[1] + found[2])
        else:
            values = values + found[0]
    return values


def trade(above, below, width):
    count = lax.axis_size("rows")
    odd = (lax.axis_index("rows") // width) % 2 == 1
    first = swap(jnp.where(odd, above, below), "rows", width)
    pairs = []
    for band in range(count):
        other = band + width if (band // width) % 2 else band - width
        if 0 <= other < count:
            pairs.append((band, other))
    second = lax.ppermute(jnp.where(odd, below, above), "rows", pairs)
    return jnp.where(odd, first, second), jnp.where(odd, second, first)


def tie(*values):
    return lax.optimization_barrier(values)


def halves(first, lower, upper):
    return jnp.where(
        first, jnp.concatenate([lower, upper], axis=0), jnp.concatenate([upper, lower], axis=0)
    )


def place():
    row = lax.axis_index("rows")
    return row // 2, row % 2, lax.axis_index("canvas")


def other_rows(across, band):
    start = (1 - across) * band
    return [
        pl.ds(pl.multiple_of(start + piece * (band // 2), band // 2), band // 2)
        for piece in range(2)
    ]


def copy_all(copies, sems):
    started = []
    for number, (source, target) in enumerate(copies):
        copy = pltpu.make_async_copy(source, target, sems.at[number])
        copy.start()
        started.append(copy)
    return started


def spread(mask, width):
    return jnp.concatenate([mask] * (width // LANES), axis=1)


def spread_rows(mask, columns, width):
    mask = jnp.concatenate([mask] * (columns // TILE), axis=1)
    return spread(mask.reshape(mask.shape[0] * columns, LANES), width)


def shift_columns(source, rows, columns, distance, masks, side, left, right):
    width = source.shape[-1]
    empty = jnp.zeros((GROUP, SIDE, width), jnp.float32)
    side[:, 0:SIDE, :] = empty
    side[:, SIDE + columns : columns + 2 * SIDE, :] = empty
    mask_left = spread(masks[0], width)
    mask_right = spread(masks[1], width)

    def step(group, carry):
        starts = [
            pl.multiple_of((group * GROUP + member) * columns, columns) for member in range(GROUP)
        ]
        for member, start in enumerate(starts):
            side[member, SIDE : SIDE + columns, :] = source[pl.ds(start, columns), :].astype(
                jnp.float32
            )
        for member, start in enumerate(starts):
            first = SIDE - distance
            left[pl.ds(start, columns), :] = (
                side[member, first : first + columns, :] * mask_left
            ).astype(jnp.bfloat16)
            first = SIDE + distance
            right[pl.ds(start, columns), :] = (
                side[member, first : first + columns, :] * mask_right
            ).astype(jnp.bfloat16)
        return carry

    lax.fori_loop(0, rows // GROUP, step, 0)


def forward_kernel(which, with_inner, first_tap, half, geometry, own, *refs):
    rows, columns, shards, parts, piece = geometry
    group = shards // 2
    steps = range(1 - half, group)
    others, refs = refs[:2], refs[2:]
    if not half:
        own_taps, refs = refs[: len(which) + with_inner], refs[len(which) + with_inner :]
    pieces, refs = refs[: 2 * len(steps)], refs[2 * len(steps) :]
    count = len(which)
    row_masks, refs = refs[:count], refs[count:]
    col_masks, refs = refs[:count], refs[count:]
    earlier = ()
    if half:
        earlier, refs = refs[: count + with_inner], refs[count + with_inner :]
        mains, refs = refs[:count], refs[count:]
        above, below, *refs = refs
    else:
        mains, refs = refs[:count], refs[count:]
    if with_inner:
        inner_out, *refs = refs
    weights_out, feat, side, left, right, weights, *refs = refs
    if half:
        totals, refs = refs[: count + with_inner], refs[count + with_inner :]
    else:
        totals = list(mains) + ([inner_out] if with_inner else [])
    sems, out_sem = refs
    depth, across, canvas = place()
    part = canvas % parts
    taps, channels, width = weights.shape
    pixels = rows * columns
    band = pixels // 2
    slice_rows = parts * piece
    upper = depth // group
    if half:
        upper = 1 - upper
    lanes = pl.ds(pl.multiple_of(upper * channels, channels), channels)
    feature_copies = copy_all(
        [
            (own.at[:, lanes], feat.at[pl.ds(pl.multiple_of(across * band, band), band)]),
            *[
                (array.at[:, lanes], feat.at[target])
                for array, target in zip(others, other_rows(across, band))
            ],
        ],
        sems,
    )
    span = pl.ds(first_tap, taps)
    copies = []
    if not half:
        start = pl.multiple_of((depth % group) * slice_rows, slice_rows)
        rows_of = pl.ds(start, slice_rows)
        for number, array in enumerate(own_taps):
            if number < count:
                target = weights.at[pl.ds(9 * number, 9), rows_of]
                copies.append((array.at[dilations.index(which[number])], target))
            else:
                copies.append((array, weights.at[9 * count, rows_of]))
    for number, step in enumerate(steps):
        origin = (depth % group) ^ step
        for index in range(parts):
            start = origin * slice_rows + (part ^ index) * piece
            copies.append(
                (
                    pieces[2 * number + index % 2].at[index // 2, span],
                    weights.at[:, pl.ds(pl.multiple_of(start, piece), piece)],
                )
            )
    copies += list(zip(earlier, totals))
    weight_copies = copy_all(copies, sems.at[pl.ds(3, len(copies))])
    for copy in feature_copies:
        copy.wait()
    tile = pixels // 4
    keep = None
    for number, dilation in enumerate(which):
        shift = dilation * columns
        total = totals[number]
        shift_columns(
            feat,
            rows,
            columns,
            dilation,
            (col_masks[number][0], col_masks[number][1]),
            side,
            left,
            right,
        )
        if not half:
            total[...] = jnp.zeros_like(total)
        if number == 0:
            for copy in weight_copies:
                copy.wait()
            keep = pltpu.make_async_copy(weights, weights_out, out_sem)
            keep.start()
        for row_tap in range(3):
            tap = 9 * number + 3 * row_tap
            for first in range(0, pixels, tile):
                span = slice(first, first + tile)
                product = jnp.dot(
                    left[span, :], weights[tap], preferred_element_type=jnp.float32
                )
                product += jnp.dot(
                    feat[span, :], weights[tap + 1], preferred_element_type=jnp.float32
                )
                product += jnp.dot(
                    right[span, :], weights[tap + 2], preferred_element_type=jnp.float32
                )
                mask = spread_rows(
                    row_masks[number][row_tap, first // columns : (first + tile) // columns],
                    columns,
                    width,
                ).astype(jnp.float32)
                target = (2 - row_tap) * shift + first
                total[target : target + tile, :] += product * mask
    if with_inner:
        for first in range(0, pixels, tile):
            span = slice(first, first + tile)
            product = jnp.dot(feat[span, :], weights[9 * count], preferred_element_type=jnp.float32)
            if half:
                product += totals[count][span, :]
            inner_out[span, :] = product
    if half:
        edge = 0
        for number, dilation in enumerate(which):
            shift = dilation * columns
            total = totals[number]
            above[edge : edge + shift, :] = total[0:shift, :].astype(jnp.bfloat16)
            mains[number][...] = total[shift : shift + pixels, :]
            below[edge : edge + shift, :] = total[
                shift + pixels : 2 * shift + pixels, :
            ].astype(jnp.bfloat16)
            edge += shift
    keep.wait()


def forward_branches(
    own, others, own_taps, pieces, row_masks, col_masks, earlier, which, with_inner, first_tap, geometry
):
    rows, columns, shards, parts, piece = geometry
    half = int(earlier is not None)
    pixels = rows * columns
    channels = own.shape[1] // 2
    width = pieces[0].shape[-1]
    count = len(which)
    taps = 9 * count + with_inner
    sums = [
        jax.ShapeDtypeStruct((pixels + 2 * dilation * columns, width), jnp.float32)
        for dilation in which
    ] + [jax.ShapeDtypeStruct((pixels, width), jnp.float32)] * with_inner
    out_shape = sums
    if half:
        edge = jax.ShapeDtypeStruct((sum(which) * columns, width), jnp.bfloat16)
        plain = jax.ShapeDtypeStruct((pixels, width), jnp.float32)
        out_shape = [plain] * count + [edge, edge] + [plain] * with_inner
    out_specs = [in_vmem] * len(out_shape) + [in_place]
    out_shape = out_shape + [jax.ShapeDtypeStruct((taps, channels, width), jnp.bfloat16)]
    earlier = list(earlier) if half else []
    own_taps = [] if half else [own_taps[0]] * count + [own_taps[1]] * with_inner
    inputs = [own, *others, *own_taps, *pieces]
    copies = 3 + len(own_taps) + (len(pieces) // 2) * parts + len(earlier)
    return pl.pallas_call(
        functools.partial(forward_kernel, which, with_inner, first_tap, half, geometry),
        in_specs=[in_place] * len(inputs) + [in_vmem] * (2 * count) + [in_place] * len(earlier),
        out_specs=out_specs,
        out_shape=out_shape,
        scratch_shapes=[
            pltpu.VMEM((pixels, channels), jnp.bfloat16),
            pltpu.VMEM((GROUP, columns + 2 * SIDE, channels), jnp.float32),
            pltpu.VMEM((pixels, channels), jnp.bfloat16),
            pltpu.VMEM((pixels, channels), jnp.bfloat16),
            pltpu.VMEM((taps, channels, width), jnp.bfloat16),
        ]
        + [pltpu.VMEM(array.shape, jnp.float32) for array in (sums if half else [])]
        + [pltpu.SemaphoreType.DMA((copies,)), pltpu.SemaphoreType.DMA],
        compiler_params=pltpu.CompilerParams(vmem_limit_bytes=vmem_bytes),
        cost_estimate=pl.CostEstimate(
            flops=2 * taps * pixels * channels * width,
            bytes_accessed=2 * pixels * channels + 4 * taps * channels * width,
            transcendentals=0,
        ),
        name=f"forward_{half}_" + "_".join(str(dilation) for dilation in which),
    )(*inputs, *row_masks, *col_masks, *earlier)


def load_gradient(rows, columns, dilation, refs, target, sems):
    depth, across, canvas = place()
    own, other, above, below = refs
    band = rows * columns // 2
    shift = dilation * columns
    return copy_all(
        [
            (own, target.at[pl.ds(pl.multiple_of(shift + across * band, columns), band)]),
            (other, target.at[pl.ds(pl.multiple_of(shift + (1 - across) * band, columns), band)]),
            (above, target.at[pl.ds(0, shift)]),
            (below, target.at[pl.ds(shift + 2 * band, shift)]),
        ],
        sems,
    )


def turned(index, count):
    result = 0
    for bit in bits_of(count):
        result = 2 * result + (index // bit) % 2
    return result


def weight_kernel(dilation, with_inner, geometry, own, *refs):
    rows, columns, shards, parts, piece = geometry
    others, refs = refs[:2], refs[2:]
    gradient, refs = refs[:4], refs[4:]
    if with_inner:
        inner, refs = refs[:2], refs[2:]
    row_mask, col_mask, keep, send, feat, side, moved, result, *refs = refs
    if with_inner:
        straight, *refs = refs
    sems, out_sems = refs
    depth, across, canvas = place()
    part = canvas % parts
    low = part % 2
    pixels = rows * columns
    band = pixels // 2
    shift = dilation * columns
    width = result.shape[-1]
    offsets = [pl.multiple_of(across * band, band), pl.multiple_of((1 - across) * band, band)]
    copies = [(own, feat.at[pl.ds(offsets[0], band)])]
    copies += [
        (array, feat.at[target]) for array, target in zip(others, other_rows(across, band))
    ]
    if with_inner:
        copies += [
            (inner[0], straight.at[pl.ds(offsets[0], band)]),
            (inner[1], straight.at[pl.ds(offsets[1], band)]),
        ]
    first = load_gradient(rows, columns, dilation, gradient, moved.at[1], sems)
    second = copy_all(copies, sems.at[pl.ds(4, len(copies))])
    for copy in first:
        copy.wait()
    shift_columns(
        moved.at[1],
        rows + 2 * dilation,
        columns,
        dilation,
        (col_mask[0], col_mask[1]),
        side,
        moved.at[2],
        moved.at[0],
    )
    for copy in second:
        copy.wait()

    def put(slot, taps, first_tap):
        copies = []
        for step in range(shards):
            origin = depth ^ step
            for pair in range(parts // 2):
                base = origin * parts * piece + 2 * (pair ^ (part // 2)) * piece
                for target, offset in ((keep, low), (send, 1 - low)):
                    start = pl.multiple_of(base + offset * piece, piece)
                    copies.append(
                        (
                            result.at[slot, pl.ds(0, taps), pl.ds(start, piece)],
                            target.at[pair, turned(step, shards), pl.ds(first_tap, taps)],
                        )
                    )
        return copy_all(copies, out_sems.at[slot])

    pending = [None, None]
    for row_tap in range(3):
        slot = row_tap % 2
        start = (2 - row_tap) * shift
        mask = spread_rows(row_mask[row_tap], columns, width)
        shifted = jnp.concatenate(
            [moved[col_tap, start : start + pixels, :] * mask for col_tap in range(3)], axis=1
        )
        product = lax.dot_general(
            feat[...], shifted, (((0,), (0,)), ((), ())), preferred_element_type=jnp.float32
        )
        if pending[slot] is not None:
            for copy in pending[slot]:
                copy.wait()
        for col_tap in range(3):
            result[slot, col_tap] = product[:, col_tap * width : (col_tap + 1) * width].astype(
                jnp.bfloat16
            )
        pending[slot] = put(slot, 3, 3 * row_tap)
    if with_inner:
        product = lax.dot_general(
            feat[...], straight[...], (((0,), (0,)), ((), ())), preferred_element_type=jnp.float32
        )
        for copy in pending[1]:
            copy.wait()
        result[1, 0] = product.astype(jnp.bfloat16)
        pending[1] = put(1, 1, 9)
    for slot in range(2):
        for copy in pending[slot]:
            copy.wait()


def weight_branch(own, others, gradient, inner, row_mask, col_mask, dilation, geometry):
    rows, columns, shards, parts, piece = geometry
    pixels = rows * columns
    channels = own.shape[1]
    width = gradient[0].shape[1]
    with_inner = inner is not None
    taps = 10 if with_inner else 9
    extended = pixels + 2 * dilation * columns
    part_shape = jax.ShapeDtypeStruct((parts // 2, shards, taps, piece, width), jnp.bfloat16)
    arrays = [own, *others, *gradient] + (list(inner) if with_inner else [])
    return pl.pallas_call(
        functools.partial(weight_kernel, dilation, with_inner, geometry),
        in_specs=[in_place] * len(arrays) + [in_vmem, in_vmem],
        out_specs=[in_place, in_place],
        out_shape=[part_shape, part_shape],
        scratch_shapes=[
            pltpu.VMEM((pixels, channels), jnp.bfloat16),
            pltpu.VMEM((GROUP, columns + 2 * SIDE, width), jnp.float32),
            pltpu.VMEM((3, extended, width), jnp.bfloat16),
            pltpu.VMEM((2, 3, channels, width), jnp.bfloat16),
        ]
        + ([pltpu.VMEM((pixels, width), jnp.bfloat16)] if with_inner else [])
        + [
            pltpu.SemaphoreType.DMA((len(arrays),)),
            pltpu.SemaphoreType.DMA((2, parts * shards)),
        ],
        compiler_params=pltpu.CompilerParams(vmem_limit_bytes=vmem_bytes),
        cost_estimate=pl.CostEstimate(
            flops=2 * taps * pixels * channels * width,
            bytes_accessed=2 * pixels * channels + 2 * taps * channels * width,
            transcendentals=0,
        ),
        name=f"weight_{dilation}",
    )(*arrays, row_mask, col_mask)


def feature_kernel(geometry, layout, *refs):
    rows, columns, shards, parts, piece = geometry
    branches = len(dilations)
    gradients = [refs[4 * branch : 4 * branch + 4] for branch in range(branches)]
    refs = refs[4 * branches :]
    inner, refs = refs[:2], refs[2:]
    row_masks, refs = refs[:branches], refs[branches:]
    col_masks, refs = refs[:branches], refs[branches:]
    weights, refs = refs[: len(layout)], refs[len(layout) :]
    taps_of = {}
    for array, names in zip(weights, layout):
        for number, name in enumerate(names):
            taps_of[name] = (array, 9 * number)
    inner_taps = taps_of[0]
    keep, send, side, straight, result, sems = refs[0], refs[1], refs[2], refs[3], refs[4], refs[5]
    moved = refs[6:]
    depth, across, canvas = place()
    pixels = rows * columns
    band = pixels // 2

    @pl.when(pl.program_id(0) == 0)
    def _():
        offsets = [
            pl.multiple_of(across * band, band),
            pl.multiple_of((1 - across) * band, band),
        ]
        waits = [
            load_gradient(
                rows, columns, dilation, gradients[branch], moved[branch].at[1], sems.at[pl.ds(4 * branch, 4)]
            )
            for branch, dilation in enumerate(dilations)
        ]
        last = copy_all(
            [
                (inner[0], straight.at[pl.ds(offsets[0], band)]),
                (inner[1], straight.at[pl.ds(offsets[1], band)]),
            ],
            sems.at[pl.ds(4 * branches, 2)],
        )
        for branch, dilation in enumerate(dilations):
            for copy in waits[branch]:
                copy.wait()
            shift_columns(
                moved[branch].at[1],
                rows + 2 * dilation,
                columns,
                dilation,
                (col_masks[branch][0], col_masks[branch][1]),
                side,
                moved[branch].at[2],
                moved[branch].at[0],
            )
        for copy in last:
            copy.wait()

    tile = pixels // 4
    for first in range(0, pixels, tile):
        span = slice(first, first + tile)
        product = lax.dot_general(
            straight[span, :],
            inner_taps[0][inner_taps[1]],
            (((1,), (1,)), ((), ())),
            preferred_element_type=jnp.float32,
        )
        for branch, dilation in enumerate(dilations):
            shift = dilation * columns
            taps, base = taps_of[dilation]
            for row_tap in range(3):
                mask = spread_rows(
                    row_masks[branch][row_tap, first // columns : (first + tile) // columns],
                    columns,
                    straight.shape[1],
                )
                start = (2 - row_tap) * shift + first
                for col_tap in range(3):
                    product += lax.dot_general(
                        moved[branch][col_tap, start : start + tile, :] * mask,
                        taps[base + 3 * row_tap + col_tap],
                        (((1,), (1,)), ((), ())),
                        preferred_element_type=jnp.float32,
                    )
        result[span, :] = product
    keep[...] = result[pl.ds(pl.multiple_of(across * band, band), band), :]
    send[...] = result[pl.ds(pl.multiple_of((1 - across) * band, band), band), :].astype(
        jnp.bfloat16
    )


def feature_branches(gradients, inner, row_masks, col_masks, weights, layout, geometry):
    rows, columns, shards, parts, piece = geometry
    pixels = rows * columns
    band = pixels // 2
    channels, width = weights[0].shape[1:]
    block_channels = min(256, channels)
    arrays = [array for gradient in gradients for array in gradient] + list(inner)
    whole = lambda array: pl.BlockSpec(array.shape, lambda t: (0,) * array.ndim)
    taps = sum(array.shape[0] for array in weights)
    return pl.pallas_call(
        functools.partial(feature_kernel, geometry, layout),
        grid=(channels // block_channels,),
        in_specs=[in_place] * len(arrays)
        + [whole(array) for array in row_masks]
        + [whole(array) for array in col_masks]
        + [
            pl.BlockSpec((array.shape[0], block_channels, width), lambda t: (0, t, 0))
            for array in weights
        ],
        out_specs=[pl.BlockSpec((band, block_channels), lambda t: (0, t))] * 2,
        out_shape=[
            jax.ShapeDtypeStruct((band, channels), jnp.float32),
            jax.ShapeDtypeStruct((band, channels), jnp.bfloat16),
        ],
        scratch_shapes=[
            pltpu.VMEM((GROUP, columns + 2 * SIDE, width), jnp.float32),
            pltpu.VMEM((pixels, width), jnp.bfloat16),
            pltpu.VMEM((pixels, block_channels), jnp.float32),
            pltpu.SemaphoreType.DMA((len(arrays),)),
        ]
        + [
            pltpu.VMEM((3, pixels + 2 * dilation * columns, width), jnp.bfloat16)
            for dilation in dilations
        ],
        compiler_params=pltpu.CompilerParams(vmem_limit_bytes=vmem_bytes),
        cost_estimate=pl.CostEstimate(
            flops=2 * taps * pixels * channels * width,
            bytes_accessed=6 * band * channels + 2 * taps * channels * width,
            transcendentals=0,
        ),
        name="feature_gradient",
    )(*arrays, *row_masks, *col_masks, *weights)


def interp_matrix(out_first, out_count, in_first, in_count, row_limit):
    out_rows = out_first + jnp.arange(out_count, dtype=jnp.int32)
    source = jnp.floor_divide(out_rows, 4)
    residue = out_rows - 4 * source
    targets = in_first + jnp.arange(in_count, dtype=jnp.int32)
    matrix = jnp.zeros((out_count, in_count), jnp.float32)
    for offset, coeffs in ((-1, prev_weights), (0, self_weights), (1, next_weights)):
        factor = jnp.zeros((out_count,), jnp.float32)
        for member in range(4):
            factor = factor + jnp.where(residue == member, coeffs[member], 0.0)
        clamped = jnp.clip(source + offset, 0, row_limit - 1)
        matrix = matrix + factor[:, None] * (clamped[:, None] == targets[None, :]).astype(
            jnp.float32
        )
    return matrix


def silu_slope(values):
    logistic = jax.nn.sigmoid(values)
    return logistic * (1.0 + values * (1.0 - logistic))


def normalize(values, sum_rows, total_count, scale_vec, shift_vec):
    average = sum_rows[0] / total_count
    spread_of = sum_rows[1] / total_count - average * average
    inverse = lax.rsqrt(spread_of + epsilon)
    centered = (values - average) * inverse
    return (centered, inverse, scale_vec * centered + shift_vec)


def input_grad(slope, centered, inverse, scale_vec, totals, total_count, weight_map):
    return (
        scale_vec
        * inverse
        * (slope - weight_map * (totals[0] + centered * totals[1]) / total_count)
    )


def moments_of(values, weight_map):
    weighted = weight_map * values
    return [jnp.sum(weighted, axis=0), jnp.sum(weighted * values, axis=0)]


def per_device(
    features,
    segment_map,
    pixel_mask,
    inner_weight,
    atrous_weight,
    pool_weight,
    proj_weight,
    norm_gains,
    norm_shifts,
    cotangent,
):
    highest = lax.Precision.HIGHEST
    row_count = lax.axis_size("rows")
    canvas_count = lax.axis_size("canvas") * features.shape[0]
    band_rows, columns, channels = features.shape[1:]
    branch_width = norm_gains.shape[1]
    canvas_rows = band_rows * row_count
    image_count = COL_IMAGES * (canvas_rows // 36)
    row_index = lax.axis_index("rows")
    canvas_index = lax.axis_index("canvas")
    shards = row_count // 2
    depth = row_index // 2
    first_band = row_index % 2 == 0
    row_first = row_index * band_rows
    rows = 2 * band_rows
    band = band_rows * columns
    pixels = rows * columns
    slice_rows = channels // row_count
    parts = min(lax.axis_size("canvas"), max(slice_rows // 16, 1))
    piece = slice_rows // parts
    part = canvas_index % parts
    geometry = (rows, columns, shards, parts, piece)

    flat_mask = pixel_mask.reshape(band, 1)
    valid_mask = flat_mask.astype(jnp.float32)
    segments = segment_map.reshape(band)
    places = jnp.arange(columns)
    col_ids = segment_map[0, 0, :] % COL_IMAGES
    col_masks = {}
    for dilation in dilations:
        table = []
        for offset in (-dilation, dilation):
            moved = places + offset
            inside = (moved >= 0) & (moved < columns)
            table.append(inside & (jnp.roll(col_ids, -offset) == col_ids))
        table = jnp.stack(table).astype(jnp.float32)
        col_masks[dilation] = jnp.broadcast_to(table[:, :, None], (2, columns, LANES))

    taps = lax.dynamic_slice_in_dim(
        atrous_weight.reshape(9 * len(dilations), slice_rows, branch_width),
        part * piece,
        piece,
        axis=1,
    )
    inner_taps = lax.dynamic_slice_in_dim(inner_weight, part * piece, piece, axis=0)[None]
    quarter = jnp.concatenate(
        [
            item
            for dilation in (18, 0, 12, 6)
            for item in (
                [taps[9 * dilations.index(dilation) :][:9]] if dilation else [inner_taps]
            )
        ],
        axis=0,
    )
    own_taps = (
        atrous_weight.reshape(len(dilations), 9, slice_rows, branch_width),
        inner_weight,
    )
    row_ids = segment_map[0, :, 0] // COL_IMAGES + 1
    both_ids = halves(first_band, row_ids, swap(row_ids, "rows", 1))
    low_mask = flat_mask.astype(jnp.bfloat16)
    flat_features = features.reshape(band, channels)
    slices = [flat_features[:, i * slice_rows : (i + 1) * slice_rows] for i in range(row_count)]
    even = jnp.concatenate(slices[0::2], axis=1)
    odd = jnp.concatenate(slices[1::2], axis=1)
    middle = band // 2
    feat_send = jnp.where(first_band, odd, even) * low_mask
    feat_own, quarter_later, *feat_parts = tie(
        jnp.where(first_band, even, odd) * low_mask,
        quarter,
        feat_send[:middle],
        feat_send[middle:],
    )
    group = shards // 2

    def along(start, bits):
        found = [start]
        for bit in bits:
            found = found + [swap(item, "rows", 2 * bit) for item in found]
        return found

    def between(item):
        chain = [item]
        for bit in bits_of(parts)[1:]:
            chain = chain + [swap(other, "canvas", bit) for other in chain]
        return chain

    def from_partner(chain):
        stacked = jnp.stack(chain)
        return [stacked, swap(stacked, "canvas", 1)]

    def sum_step(values, bit):
        return values + swap(values, "rows", bit)

    def gather_step(values, bit):
        other = swap(values, "rows", bit)
        both = jnp.where(
            (row_index & bit) == 0,
            jnp.stack([values, other], axis=1),
            jnp.stack([other, values], axis=1),
        )
        return both.reshape((2 * values.shape[0],) + values.shape[1:])

    rounds = bits_of(row_count)
    near = along(quarter, bits_of(group))[1:]
    feat_first = swap(feat_parts[0], "rows", 1)
    reach = max(dilations)

    def row_checks(all_ids, outside):
        masks = {}
        for dilation in dilations:
            checks = []
            for row_tap in range(3):
                start = reach - (row_tap - 1) * dilation
                target = all_ids[start : start + rows]
                same = target == all_ids[reach : reach + rows]
                checks.append(jnp.where(target == 0, outside, same))
            table = jnp.stack(checks).astype(jnp.bfloat16)
            masks[dilation] = jnp.broadcast_to(table[:, :, None, None], (3, rows, TILE, LANES))
        return masks

    near_masks = row_checks(jnp.pad(both_ids, (reach, reach)), True)
    col_matrix = interp_matrix(0, 4 * columns, 0, columns, columns)
    col_grad = jnp.einsum(
        "pw,opb->owb",
        col_matrix.astype(jnp.bfloat16),
        cotangent[0],
        preferred_element_type=jnp.float32,
    )
    near, both_ids, col_grad, near_masks = tie(near, both_ids, col_grad, near_masks)

    far_first = swap(quarter_later, "rows", 2 * group)
    near_chains = [between(item) for item in near]
    feat_second = swap(feat_parts[1], "rows", 1)
    members = (segments[:, None] == jnp.arange(image_count, dtype=jnp.int32)).astype(jnp.float32)
    member_low = members.astype(jnp.bfloat16)
    seg_sums = jnp.einsum(
        "ps,pc->sc", member_low, flat_features * low_mask, preferred_element_type=jnp.float32
    )
    seg_counts = jnp.sum(members * valid_mask, axis=0)
    seg_all = jnp.concatenate(
        [seg_sums, jnp.broadcast_to(seg_counts[:, None], (image_count, LANES))], axis=1
    )
    far_first, near_chains, feat_first, feat_second, seg_all, proj_full = tie(
        far_first, near_chains, feat_first, feat_second, seg_all, proj_weight[None]
    )

    feat_others = (feat_first, feat_second)
    far = along(far_first, bits_of(group))
    far_chains = [between(far_first)]
    near_pieces = [item for chain in near_chains for item in from_partner(chain)]
    seg_all = sum_step(seg_all, rounds[0])
    proj_full = gather_step(proj_full, rounds[-1])
    first_taps = {18: 0, 12: 10, 6: 19}

    def forward(which, pieces, earlier=None):
        return forward_branches(
            feat_own,
            feat_others,
            own_taps,
            pieces,
            [near_masks[dilation] for dilation in which],
            [col_masks[dilation] for dilation in which],
            earlier,
            which,
            int(which == (18,)),
            first_taps[which[0]],
            geometry,
        )

    total_18, total_inner, weights_00 = forward((18,), near_pieces)
    (far, far_chains, seg_all, proj_full, total_18, total_inner, near_pieces) = tie(
        far, far_chains, seg_all, proj_full, total_18, total_inner, near_pieces
    )

    far_chains = far_chains + [between(item) for item in far[1:]]
    far_pieces = from_partner(far_chains[0])
    total_12, total_6, weights_01 = forward((12, 6), near_pieces)
    seg_all = sum_step(seg_all, rounds[1])
    proj_full = gather_step(proj_full, rounds[-2])
    far_chains, far_pieces, total_12, total_6, seg_all, proj_full, both_ids = tie(
        far_chains, far_pieces, total_12, total_6, seg_all, proj_full, both_ids
    )

    far_pieces = far_pieces + [item for chain in far_chains[1:] for item in from_partner(chain)]
    def to_partner(partials):
        sent = [
            jnp.where(first_band, partial[band:], partial[:band]).astype(jnp.bfloat16)
            for partial in partials
        ]
        return swap(jnp.concatenate(sent, axis=1), "rows", 1)

    def complete(partial, back):
        mine = jnp.where(first_band, partial[:band], partial[band:])
        return mine + back.astype(jnp.float32)

    def beyond_bands(dilation, main, above, below):
        shift = dilation * columns
        here = all_ids[reach : reach + rows]
        mask = here[:dilation] == all_ids[reach - dilation : reach]
        mask = jnp.broadcast_to(mask[:, None], (dilation, columns)).reshape(shift, 1)
        below = below.astype(jnp.float32) * mask.astype(jnp.float32)
        mask = here[rows - dilation :] == all_ids[reach + rows : reach + rows + dilation]
        mask = jnp.broadcast_to(mask[:, None], (dilation, columns)).reshape(shift, 1)
        above = above.astype(jnp.float32) * mask.astype(jnp.float32)
        return jnp.concatenate(
            [
                main[:shift] + below,
                main[shift : pixels - shift],
                main[pixels - shift :] + above,
            ],
            axis=0,
        )

    main_18, above_18, below_18, main_inner, weights_10 = forward(
        (18,), far_pieces, [total_18, total_inner]
    )
    far_pieces, main_18, above_18, below_18, main_inner, seg_all, proj_full, both_ids = tie(
        far_pieces, main_18, above_18, below_18, main_inner, seg_all, proj_full, both_ids
    )
    id_above, id_below = trade(both_ids[:reach], both_ids[rows - reach :], 2)
    all_ids = jnp.concatenate([id_above, both_ids, id_below])
    for bit in rounds[2:]:
        seg_all = sum_step(seg_all, bit)
    for bit in rounds[-3::-1]:
        proj_full = gather_step(proj_full, bit)
    proj_full = proj_full.reshape(-1, branch_width)
    back_inner = to_partner([main_inner])
    below_18, above_18 = trade(above_18, below_18, 2)
    main_12, above_12, below_12, weights_11 = forward((12,), far_pieces, [total_12])
    total_counts = seg_all[:, channels : channels + 1]
    pooled = lax.dynamic_slice_in_dim(seg_all, row_index * slice_rows, slice_rows, axis=1)
    pooled = pooled / total_counts
    pool_matrix = pool_weight.astype(jnp.float32)
    pool_part = jnp.dot(pooled, pool_matrix, precision=highest)
    (
        far_pieces,
        main_12,
        above_12,
        below_12,
        back_inner,
        above_18,
        below_18,
        pool_part,
        proj_full,
        all_ids,
    ) = tie(
        far_pieces,
        main_12,
        above_12,
        below_12,
        back_inner,
        above_18,
        below_18,
        pool_part,
        proj_full,
        all_ids,
    )
    row_masks = row_checks(all_ids, False)
    main_18 = beyond_bands(18, main_18, above_18, below_18)
    back_18 = to_partner([main_18])
    below_12, above_12 = trade(above_12, below_12, 2)
    main_6, above_6, below_6, weights_12 = forward((6,), far_pieces, [total_6])
    back_18, above_12, below_12, main_6, above_6, below_6, col_grad = tie(
        back_18, above_12, below_12, main_6, above_6, below_6, col_grad
    )
    main_12 = beyond_bands(12, main_12, above_12, below_12)
    back_12 = to_partner([main_12])
    below_6, above_6 = trade(above_6, below_6, 2)
    grad_above, grad_below = trade(col_grad[:2], col_grad[4 * band_rows - 2 :], 1)
    grad_ext = jnp.concatenate([grad_above, col_grad, grad_below], axis=0)
    back_12, above_6, below_6, grad_ext = tie(back_12, above_6, below_6, grad_ext)
    main_6 = beyond_bands(6, main_6, above_6, below_6)
    back_6 = to_partner([main_6])
    back_matrix = interp_matrix(
        4 * row_first - 2, 4 * band_rows + 4, row_first, band_rows, canvas_rows
    )
    act_grad = jnp.einsum("or,owb->rwb", back_matrix, grad_ext, precision=highest)
    act_grad = act_grad.reshape(band, branch_width)
    conv_outs = [
        complete(main_inner, back_inner),
        complete(main_6, back_6),
        complete(main_12, back_12),
        complete(main_18, back_18),
    ]
    conv_outs[1], act_grad = tie(conv_outs[1], act_grad)
    weights_full = [[weights_00, weights_01], [weights_10, weights_11, weights_12]]
    layouts = (((18, 0), (12, 6)), ((18, 0), (12,), (6,)))

    rows_of = []
    for conv_out in conv_outs:
        rows_of += moments_of(conv_out, valid_mask)
    rows_of.append(jnp.broadcast_to(jnp.sum(valid_mask), (branch_width,)))
    sums = sum_over(jnp.concatenate([jnp.stack(rows_of), pool_part]), "rows")
    pool_out = sums[9:]
    sums = sum_over(
        jnp.concatenate(
            [
                sums[:8],
                jnp.sum(pool_out, axis=0, keepdims=True),
                jnp.sum(pool_out * pool_out, axis=0, keepdims=True),
                sums[8:9],
            ]
        ),
        "canvas",
    )
    pixel_total = sums[10]
    entries = float(canvas_count * image_count)
    normals = [
        normalize(
            conv_out,
            sums[2 * branch : 2 * branch + 2],
            pixel_total,
            norm_gains[branch],
            norm_shifts[branch],
        )
        for branch, conv_out in enumerate(conv_outs)
    ]
    pool_norm = normalize(pool_out, sums[8:10], entries, norm_gains[4], norm_shifts[4])
    pool_act = jax.nn.silu(pool_norm[2]).astype(jnp.bfloat16)
    pool_map = jnp.dot(member_low, pool_act, preferred_element_type=jnp.float32)
    concat_act = jnp.concatenate(
        [jax.nn.silu(item[2]).astype(jnp.bfloat16) for item in normals]
        + [pool_map.astype(jnp.bfloat16)],
        axis=-1,
    )
    proj_out = jnp.dot(concat_act, proj_full, preferred_element_type=jnp.float32)
    proj_totals = sum_over(
        sum_over(jnp.stack(moments_of(proj_out, valid_mask)), "rows"), "canvas"
    )
    proj_norm = normalize(proj_out, proj_totals, pixel_total, norm_gains[5], norm_shifts[5])
    proj_act = jax.nn.silu(proj_norm[2]).astype(jnp.bfloat16)

    act_rows = proj_act.reshape(band_rows, columns, branch_width)
    act_above, act_below = trade(act_rows[:1], act_rows[band_rows - 1 :], 1)
    ext_act = jnp.concatenate([act_above, act_rows, act_below], axis=0)

    proj_slope = act_grad * silu_slope(proj_norm[2])
    proj_local = jnp.stack(
        [jnp.sum(proj_slope, axis=0), jnp.sum(proj_slope * proj_norm[0], axis=0)]
    )
    proj_grad_totals = sum_over(sum_over(proj_local, "rows"), "canvas")
    proj_grad = input_grad(
        proj_slope,
        proj_norm[0],
        proj_norm[1],
        norm_gains[5],
        proj_grad_totals,
        pixel_total,
        valid_mask,
    ).astype(jnp.bfloat16)
    joined_grad = lax.dot_general(
        proj_grad, proj_full, (((1,), (1,)), ((), ())), preferred_element_type=jnp.float32
    )
    slopes = [
        joined_grad[:, branch * branch_width : (branch + 1) * branch_width]
        * silu_slope(normals[branch][2])
        for branch in range(4)
    ]
    rows_of = []
    for branch, slope in enumerate(slopes):
        rows_of += [jnp.sum(slope, axis=0), jnp.sum(slope * normals[branch][0], axis=0)]
    seg_grads = lax.dot_general(
        members, joined_grad[:, 4 * branch_width :], (((0,), (0,)), ((), ())), precision=highest
    )
    pool_terms = seg_grads * silu_slope(pool_norm[2])
    rows_of += [jnp.sum(pool_terms, axis=0), jnp.sum(pool_terms * pool_norm[0], axis=0)]
    sums = sum_over(jnp.concatenate([jnp.stack(rows_of), seg_grads], axis=0), "rows")
    seg_grads = sums[10:]
    sums = sum_over(sums[:10], "canvas")
    branch_totals = [sums[2 * branch : 2 * branch + 2] for branch in range(5)]
    conv_grads = [
        input_grad(
            slopes[branch],
            normals[branch][0],
            normals[branch][1],
            norm_gains[branch],
            branch_totals[branch],
            pixel_total,
            valid_mask,
        ).astype(jnp.bfloat16)
        for branch in range(4)
    ]

    pool_grad = input_grad(
        seg_grads * silu_slope(pool_norm[2]),
        pool_norm[0],
        pool_norm[1],
        norm_gains[4],
        branch_totals[4],
        entries,
        1.0,
    )
    pooled_grad = (
        lax.dot_general(pool_matrix, pool_grad, (((1,), (1,)), ((), ())), precision=highest)
        / total_counts[:, 0]
    )
    grad_pool = lax.dot_general(
        pooled, pool_grad, (((0,), (0,)), ((), ())), precision=highest
    )
    grad_proj = lax.dot_general(
        concat_act, proj_grad, (((0,), (0,)), ((), ())), preferred_element_type=jnp.float32
    )

    grad_proj = grad_proj.reshape((row_count,) + (grad_proj.shape[0] // row_count, branch_width))

    def scatter_step(values, bit):
        values = values.reshape((values.shape[0] // 2, 2) + values.shape[1:])
        low, high = values[:, 0], values[:, 1]
        mine = (row_index & bit) == 0
        sent = jnp.where(mine, high, low).astype(jnp.bfloat16)
        return jnp.where(mine, low, high) + swap(sent, "rows", bit).astype(jnp.float32)

    def beyond(branch, other):
        grad = conv_grads[branch + 1]
        shift = dilations[branch] * columns
        top = jnp.where(first_band, grad[:shift], other[:shift])
        bottom = jnp.where(first_band, other[band - shift :], grad[band - shift :])
        return (grad, other, *trade(top, bottom, 2))

    def pair_sum(kept, got):
        return kept.astype(jnp.float32) + got.astype(jnp.float32)

    def halve(kept, got, dim, axis, bit):
        size = kept.shape[dim] // 2
        cut = lambda values, start: lax.slice_in_dim(values, start, start + size, axis=dim)
        sent = pair_sum(cut(kept, size), cut(got, size)).astype(jnp.bfloat16)
        return pair_sum(cut(kept, 0), cut(got, 0)), swap(sent, axis, bit)

    def weights_of(branch, inner=None):
        return weight_branch(
            feat_own,
            feat_others,
            gradients[branch],
            inner,
            row_masks[dilations[branch]],
            col_masks[dilations[branch]],
            dilations[branch],
            geometry,
        )

    plan = [(0, "canvas", bit) for bit in reversed(bits_of(parts)[1:])]
    along_rows = [(1, "rows", 2 * bit) for bit in bits_of(shards)]

    def finish(kept, got, stages):
        for dim, axis, bit in stages:
            kept, got = halve(kept, got, dim, axis, bit)
        total = pair_sum(kept, got)[0, 0]
        for bit in bits_of(lax.axis_size("canvas")):
            if bit >= parts:
                total = total + swap(total, "canvas", bit)
        return total.astype(jnp.bfloat16)

    def everywhere(finished):
        blocks = lax.optimization_barrier(jnp.concatenate(finished, axis=0))[:, None]
        for bit in reversed(bits_of(parts)):
            other = swap(blocks, "canvas", bit)
            stacked = jnp.where(
                (part & bit) == 0,
                jnp.stack([blocks, other], axis=2),
                jnp.stack([other, blocks], axis=2),
            )
            blocks = stacked.reshape((stacked.shape[0], stacked.shape[1] * 2) + stacked.shape[3:])
        return blocks.reshape(blocks.shape[0], slice_rows, branch_width)

    def features_of(half):
        return feature_branches(
            gradients,
            inner_grads,
            [row_masks[dilation] for dilation in dilations],
            [col_masks[dilation] for dilation in dilations],
            weights_full[half],
            layouts[half],
            geometry,
        )

    other = swap(conv_grads[1], "rows", 1)
    other, ext_act, *conv_grads = tie(other, ext_act, *conv_grads)
    row_matrix = interp_matrix(
        4 * row_first, 4 * band_rows, row_first - 1, band_rows + 2, canvas_rows
    ).astype(jnp.bfloat16)
    rows_up = jnp.einsum("or,rwb->owb", row_matrix, ext_act, preferred_element_type=jnp.float32)
    high = rows_up.astype(jnp.bfloat16)
    low = (rows_up - high.astype(jnp.float32)).astype(jnp.bfloat16)
    upsampled = jnp.einsum(
        "pw,owb->opb",
        jnp.concatenate([col_matrix, col_matrix], axis=1).astype(jnp.bfloat16),
        jnp.concatenate([high, low], axis=1),
        preferred_element_type=jnp.float32,
    ).astype(jnp.bfloat16)
    gradients = [beyond(0, other)]
    other = swap(conv_grads[2], "rows", 1)
    gradients, other, conv_grads, upsampled = tie(gradients, other, conv_grads, upsampled)
    gradients.append(beyond(1, other))
    other = swap(jnp.concatenate([conv_grads[3], conv_grads[0]], axis=1), "rows", 1)
    kept_6, sent_6 = weights_of(0)
    gradients, other, kept_6, sent_6, grad_proj, pooled_grad, grad_pool = tie(
        gradients, other, kept_6, sent_6, grad_proj, pooled_grad, grad_pool
    )
    gradients.append(beyond(2, other[:, :branch_width]))
    inner_grads = (conv_grads[0], other[:, branch_width:])
    got_6 = swap(sent_6, "canvas", 1)
    kept_12, sent_12 = weights_of(1)
    grad_proj = scatter_step(grad_proj, rounds[0])
    gradients, inner_grads, kept_6, got_6, kept_12, sent_12, grad_proj = tie(
        gradients, inner_grads, kept_6, got_6, kept_12, sent_12, grad_proj
    )
    kept_6, got_6 = halve(kept_6, got_6, *plan[0])
    got_12 = swap(sent_12, "canvas", 1)
    kept_18, sent_18 = weights_of(2, inner_grads)
    grad_proj = scatter_step(grad_proj, rounds[1])
    pooled_grad = gather_step(pooled_grad[None], rounds[-1])
    gradients, kept_6, got_6, kept_12, got_12, kept_18, sent_18, grad_proj, pooled_grad = tie(
        gradients, kept_6, got_6, kept_12, got_12, kept_18, sent_18, grad_proj, pooled_grad
    )
    kept_6, got_6 = halve(kept_6, got_6, *(plan[1:] + along_rows)[0])
    kept_12, got_12 = halve(kept_12, got_12, *plan[0])
    got_18 = swap(sent_18, "canvas", 1)
    feature_0 = features_of(0)
    for bit in rounds[2:]:
        grad_proj = scatter_step(grad_proj, bit)
    grad_proj = grad_proj[0]
    pooled_grad = gather_step(pooled_grad, rounds[-2])
    (
        gradients,
        kept_6,
        got_6,
        kept_12,
        got_12,
        kept_18,
        got_18,
        feature_0,
        grad_proj,
        pooled_grad,
    ) = tie(
        gradients,
        kept_6,
        got_6,
        kept_12,
        got_12,
        kept_18,
        got_18,
        feature_0,
        grad_proj,
        pooled_grad,
    )
    kept_6, got_6 = halve(kept_6, got_6, *(plan[1:] + along_rows)[1])
    kept_12, got_12 = halve(kept_12, got_12, *(plan[1:] + along_rows)[0])
    kept_18, got_18 = halve(kept_18, got_18, *plan[0])
    back_0 = swap(feature_0[1], "rows", 1)
    feature_1 = features_of(1)
    for bit in rounds[-3::-1]:
        pooled_grad = gather_step(pooled_grad, bit)
    pooled_grad = pooled_grad.reshape(channels, image_count)
    shared = jnp.concatenate([grad_pool, grad_proj], axis=0)
    canvas_bits = bits_of(lax.axis_size("canvas"))
    shared = shared + swap(shared, "canvas", canvas_bits[0])
    kept_6, got_6, kept_12, got_12, kept_18, got_18, back_0, feature_1, shared, pooled_grad = tie(
        kept_6, got_6, kept_12, got_12, kept_18, got_18, back_0, feature_1, shared, pooled_grad
    )
    back_1 = swap(feature_1[1], "rows", 1)
    part_6 = finish(kept_6, got_6, (plan[1:] + along_rows)[2:])
    kept_12, got_12 = halve(kept_12, got_12, *(plan[1:] + along_rows)[1])
    kept_18, got_18 = halve(kept_18, got_18, *(plan[1:] + along_rows)[0])
    for bit in canvas_bits[1:]:
        shared = shared + swap(shared, "canvas", bit)
    grad_pool, grad_proj = shared[:slice_rows], shared[slice_rows:]
    part_6, kept_12, got_12, kept_18, got_18, back_1, grad_pool, grad_proj = tie(
        part_6, kept_12, got_12, kept_18, got_18, back_1, grad_pool, grad_proj
    )
    evens, odds = [], []
    for (kept, _), back in ((feature_0, back_0), (feature_1, back_1)):
        other = back.astype(jnp.float32)
        evens.append(jnp.where(first_band, kept, other))
        odds.append(jnp.where(first_band, other, kept))
    low_first = depth < group
    even = jnp.where(
        low_first, jnp.concatenate(evens, axis=1), jnp.concatenate(evens[::-1], axis=1)
    )
    odd = jnp.where(low_first, jnp.concatenate(odds, axis=1), jnp.concatenate(odds[::-1], axis=1))
    joined = []
    for shard in range(shards):
        span = slice(shard * slice_rows, (shard + 1) * slice_rows)
        joined += [even[:, span], odd[:, span]]
    spread_pool = lax.dot_general(
        members, pooled_grad, (((1,), (1,)), ((), ())), precision=highest
    )
    grad_features = (jnp.concatenate(joined, axis=1) + spread_pool) * valid_mask
    kept_18, got_18 = halve(kept_18, got_18, *(plan[1:] + along_rows)[1])
    part_12 = finish(kept_12, got_12, (plan[1:] + along_rows)[2:])
    early = everywhere([part_6, part_12])
    grad_atrous = jnp.zeros((9 * len(dilations), slice_rows, branch_width), jnp.float32)
    grad_atrous = lax.dynamic_update_slice(grad_atrous, early.astype(jnp.float32), (0, 0, 0))
    kept_18, got_18, grad_atrous, grad_features = tie(kept_18, got_18, grad_atrous, grad_features)
    late = everywhere([finish(kept_18, got_18, (plan[1:] + along_rows)[2:])])
    grad_inner = late[9].astype(jnp.float32)
    grad_atrous = lax.dynamic_update_slice(
        grad_atrous, late[:9].astype(jnp.float32), (early.shape[0], 0, 0)
    ).reshape(atrous_weight.shape)

    grad_gains = jnp.stack([totals[1] for totals in branch_totals] + [proj_grad_totals[1]])
    grad_shifts = jnp.stack([totals[0] for totals in branch_totals] + [proj_grad_totals[0]])
    return (
        upsampled[None],
        grad_features.reshape(features.shape),
        grad_inner,
        grad_atrous,
        grad_pool,
        grad_proj,
        grad_gains,
        grad_shifts,
    )


def solution(mesh):
    in_specs = (
        P("canvas", "rows", None, None),
        P("canvas", "rows", None),
        P("canvas", "rows", None),
        P("rows", None),
        P(None, None, "rows", None),
        P("rows", None),
        P("rows", None),
        P(),
        P(),
        P("canvas", "rows", None, None),
    )
    out_specs = (
        P("canvas", "rows", None, None),
        P("canvas", "rows", None, None),
        P("rows", None),
        P(None, None, "rows", None),
        P("rows", None),
        P("rows", None),
        P(),
        P(),
    )
    return jax.shard_map(
        per_device, mesh=mesh, in_specs=in_specs, out_specs=out_specs, check_vma=False
    )
```

```python
import functools

import jax
import jax.numpy as jnp
from jax import lax
from jax.experimental import pallas as pl
from jax.experimental.pallas import tpu as pltpu
from jax.sharding import PartitionSpec as P

COL_IMAGES = 2
LANES = 128
SIDE = 24
TILE = 16
TILES = 4
TAPS = 4
GROUP = 6

dilations = (6, 12, 18)
epsilon = 1e-05
prev_weights = (0.375, 0.125, 0.0, 0.0)
self_weights = (0.625, 0.875, 0.875, 0.625)
next_weights = (0.0, 0.0, 0.125, 0.375)
vmem_bytes = 58 << 20
in_place = pl.BlockSpec(memory_space=pl.ANY)
in_vmem = pl.BlockSpec(memory_space=pltpu.VMEM)


def swap(values, axis, bit):
    count = lax.axis_size(axis)
    return lax.ppermute(values, axis, [(i, i ^ bit) for i in range(count)])


def bits_of(count):
    bits, bit = [], 1
    while bit < count:
        bits.append(bit)
        bit *= 2
    return bits


def sum_over(values, axis):
    bits = bits_of(lax.axis_size(axis))
    for first in range(0, len(bits), 2):
        pair = bits[first : first + 2]
        found = [swap(values, axis, bit) for bit in pair]
        if len(pair) == 2:
            found.append(swap(values, axis, pair[0] ^ pair[1]))
            values = (values + found[0]) + (found[1] + found[2])
        else:
            values = values + found[0]
    return values


def trade(above, below, width):
    count = lax.axis_size("rows")
    odd = (lax.axis_index("rows") // width) % 2 == 1
    first = swap(jnp.where(odd, above, below), "rows", width)
    pairs = []
    for band in range(count):
        other = band + width if (band // width) % 2 else band - width
        if 0 <= other < count:
            pairs.append((band, other))
    second = lax.ppermute(jnp.where(odd, below, above), "rows", pairs)
    return jnp.where(odd, first, second), jnp.where(odd, second, first)


def tie(*values):
    return lax.optimization_barrier(values)


def halves(first, lower, upper):
    return jnp.where(
        first, jnp.concatenate([lower, upper], axis=0), jnp.concatenate([upper, lower], axis=0)
    )


def place():
    row = lax.axis_index("rows")
    return row // 2, row % 2, lax.axis_index("canvas")


def other_rows(across, band):
    start = (1 - across) * band
    return [
        pl.ds(pl.multiple_of(start + piece * (band // 2), band // 2), band // 2)
        for piece in range(2)
    ]


def copy_all(copies, sems):
    started = []
    for number, (source, target) in enumerate(copies):
        copy = pltpu.make_async_copy(source, target, sems.at[number])
        copy.start()
        started.append(copy)
    return started


def spread(mask, width):
    return jnp.concatenate([mask] * (width // LANES), axis=1)


def spread_rows(mask, columns, width):
    mask = jnp.concatenate([mask] * (columns // TILE), axis=1)
    return spread(mask.reshape(mask.shape[0] * columns, LANES), width)


def shift_columns(source, rows, columns, distance, masks, side, left, right):
    inside = [masks[index] != 0 for index in range(2)]
    chunks = source.shape[-1] // LANES

    def step(group, carry):
        starts = [
            pl.multiple_of((group * GROUP + member) * columns, columns) for member in range(GROUP)
        ]
        for chunk in range(chunks):
            lanes = slice(chunk * LANES, (chunk + 1) * LANES)
            for member, start in enumerate(starts):
                side[chunk, member, SIDE : SIDE + columns, :] = source[
                    pl.ds(start, columns), lanes
                ].astype(jnp.float32)
            for member, start in enumerate(starts):
                for target, offset, mask in (
                    (left, -distance, inside[0]),
                    (right, distance, inside[1]),
                ):
                    first = SIDE + offset
                    value = side[chunk, member, first : first + columns, :]
                    target[pl.ds(start, columns), lanes] = jnp.where(mask, value, 0.0).astype(
                        jnp.bfloat16
                    )
        return carry

    lax.fori_loop(0, rows // GROUP, step, 0)


def moved_columns(source, first, count, columns, distance, inside, planes):
    lefts, rights = [], []
    for chunk in range(source.shape[-1] // LANES):
        lanes = slice(chunk * LANES, (chunk + 1) * LANES)
        left, right = [], []
        for row in range(count):
            start = first + row * columns
            planes[chunk, row, SIDE : SIDE + columns, :] = source[
                start : start + columns, lanes
            ].astype(jnp.float32)
        for row in range(count):
            for offset, mask, result in ((-distance, inside[0], left), (distance, inside[1], right)):
                place = SIDE + offset
                value = planes[chunk, row, place : place + columns, :]
                result.append(jnp.where(mask, value, 0.0).astype(jnp.bfloat16))
        lefts.append(jnp.concatenate(left, axis=0))
        rights.append(jnp.concatenate(right, axis=0))
    return jnp.concatenate(lefts, axis=1), jnp.concatenate(rights, axis=1)


def forward_kernel(which, with_inner, first_tap, half, geometry, own, *refs):
    rows, columns, shards, parts, piece = geometry
    group = shards // 2
    steps = range(1 - half, group)
    others, refs = refs[:2], refs[2:]
    if not half:
        own_taps, refs = refs[: len(which) + with_inner], refs[len(which) + with_inner :]
    pieces, refs = refs[: 2 * len(steps)], refs[2 * len(steps) :]
    count = len(which)
    row_masks, refs = refs[:count], refs[count:]
    col_masks, refs = refs[:count], refs[count:]
    earlier = ()
    if half:
        earlier, refs = refs[: count + with_inner], refs[count + with_inner :]
        mains, refs = refs[:count], refs[count:]
        above, below, *refs = refs
    else:
        mains, refs = refs[:count], refs[count:]
    if with_inner:
        inner_out, *refs = refs
    weights_out, feat, planes, weights, *refs = refs
    if half:
        totals, refs = refs[:count], refs[count:]
        before, refs = refs[: count + with_inner], refs[count + with_inner :]
    else:
        totals = list(mains) + ([inner_out] if with_inner else [])
    sems, out_sem = refs
    depth, across, canvas = place()
    part = canvas % parts
    taps, channels, width = weights.shape
    pixels = rows * columns
    band = pixels // 2
    slice_rows = parts * piece
    upper = depth // group
    if half:
        upper = 1 - upper
    lanes = pl.ds(pl.multiple_of(upper * channels, channels), channels)
    feature_copies = copy_all(
        [
            (own.at[:, lanes], feat.at[pl.ds(pl.multiple_of(across * band, band), band)]),
            *[
                (array.at[:, lanes], feat.at[target])
                for array, target in zip(others, other_rows(across, band))
            ],
        ],
        sems,
    )
    span = pl.ds(first_tap, taps)
    copies = []
    if not half:
        start = pl.multiple_of((depth % group) * slice_rows, slice_rows)
        rows_of = pl.ds(start, slice_rows)
        for number, array in enumerate(own_taps):
            if number < count:
                target = weights.at[pl.ds(9 * number, 9), rows_of]
                copies.append((array.at[dilations.index(which[number])], target))
            else:
                copies.append((array, weights.at[9 * count, rows_of]))
    for number, step in enumerate(steps):
        origin = (depth % group) ^ step
        for index in range(parts):
            start = origin * slice_rows + (part ^ index) * piece
            copies.append(
                (
                    pieces[2 * number + index % 2].at[index // 2, span],
                    weights.at[:, pl.ds(pl.multiple_of(start, piece), piece)],
                )
            )
    weight_copies = copy_all(copies, sems.at[pl.ds(3, len(copies))])
    if half:
        earlier_copies = copy_all(
            list(zip(earlier, before)), sems.at[pl.ds(3 + len(copies), len(earlier))]
        )
    for copy in feature_copies:
        copy.wait()
    tile = pixels // TILES
    tile_rows = tile // columns
    keep = None
    for number, dilation in enumerate(which):
        shift = dilation * columns
        total = totals[number]
        inside = [col_masks[number][side] != 0 for side in range(2)]
        total[...] = jnp.zeros_like(total)
        for index in range(TILES):
            first = index * tile
            span = slice(first, first + tile)
            left, right = moved_columns(
                feat, first, tile_rows, columns, dilation, inside, planes.at[index % 2]
            )
            if number == 0 and index == 0:
                for copy in weight_copies:
                    copy.wait()
                keep = pltpu.make_async_copy(weights, weights_out, out_sem)
                keep.start()
            for row_tap in range(3):
                tap = 9 * number + 3 * row_tap
                product = jnp.dot(feat[span, :], weights[tap + 1], preferred_element_type=jnp.float32)
                product += jnp.dot(left, weights[tap], preferred_element_type=jnp.float32)
                product += jnp.dot(right, weights[tap + 2], preferred_element_type=jnp.float32)
                mask = spread_rows(
                    row_masks[number][row_tap, first // columns : (first + tile) // columns],
                    columns,
                    width,
                ).astype(jnp.float32)
                target = (2 - row_tap) * shift + first
                total[target : target + tile, :] += product * mask
    if half:
        for copy in earlier_copies:
            copy.wait()
    if with_inner:
        for first in range(0, pixels, tile):
            span = slice(first, first + tile)
            product = jnp.dot(feat[span, :], weights[9 * count], preferred_element_type=jnp.float32)
            if half:
                product += before[count][span, :]
            inner_out[span, :] = product
    if half:
        edge = 0
        for number, dilation in enumerate(which):
            shift = dilation * columns
            total, old = totals[number], before[number]
            end = shift + pixels
            above[edge : edge + shift, :] = (total[0:shift, :] + old[0:shift, :]).astype(
                jnp.bfloat16
            )
            mains[number][...] = total[shift:end, :] + old[shift:end, :]
            below[edge : edge + shift, :] = (
                total[end : end + shift, :] + old[end : end + shift, :]
            ).astype(jnp.bfloat16)
            edge += shift
    keep.wait()


def forward_branches(
    own, others, own_taps, pieces, row_masks, col_masks, earlier, which, with_inner, first_tap, geometry
):
    rows, columns, shards, parts, piece = geometry
    half = int(earlier is not None)
    pixels = rows * columns
    channels = own.shape[1] // 2
    width = pieces[0].shape[-1]
    count = len(which)
    taps = 9 * count + with_inner
    sums = [
        jax.ShapeDtypeStruct((pixels + 2 * dilation * columns, width), jnp.float32)
        for dilation in which
    ] + [jax.ShapeDtypeStruct((pixels, width), jnp.float32)] * with_inner
    out_shape = sums
    if half:
        edge = jax.ShapeDtypeStruct((sum(which) * columns, width), jnp.bfloat16)
        plain = jax.ShapeDtypeStruct((pixels, width), jnp.float32)
        out_shape = [plain] * count + [edge, edge] + [plain] * with_inner
    out_specs = [in_vmem] * len(out_shape) + [in_place]
    out_shape = out_shape + [jax.ShapeDtypeStruct((taps, channels, width), jnp.bfloat16)]
    earlier = list(earlier) if half else []
    own_taps = [] if half else [own_taps[0]] * count + [own_taps[1]] * with_inner
    inputs = [own, *others, *own_taps, *pieces]
    copies = 3 + len(own_taps) + (len(pieces) // 2) * parts + len(earlier)
    return pl.pallas_call(
        functools.partial(forward_kernel, which, with_inner, first_tap, half, geometry),
        in_specs=[in_place] * len(inputs) + [in_vmem] * (2 * count) + [in_place] * len(earlier),
        out_specs=out_specs,
        out_shape=out_shape,
        scratch_shapes=[
            pltpu.VMEM((pixels, channels), jnp.bfloat16),
            pltpu.VMEM(
                (2, channels // LANES, rows // TILES, columns + 2 * SIDE, LANES), jnp.float32
            ),
            pltpu.VMEM((taps, channels, width), jnp.bfloat16),
        ]
        + [pltpu.VMEM(array.shape, jnp.float32) for array in (sums[:count] + sums if half else [])]
        + [pltpu.SemaphoreType.DMA((copies,)), pltpu.SemaphoreType.DMA],
        compiler_params=pltpu.CompilerParams(vmem_limit_bytes=vmem_bytes),
        cost_estimate=pl.CostEstimate(
            flops=2 * taps * pixels * channels * width,
            bytes_accessed=2 * pixels * channels + 4 * taps * channels * width,
            transcendentals=0,
        ),
        name=f"forward_{half}_" + "_".join(str(dilation) for dilation in which),
    )(*inputs, *row_masks, *col_masks, *earlier)


def load_gradient(rows, columns, dilation, refs, target, sems):
    depth, across, canvas = place()
    own, other, above, below = refs
    band = rows * columns // 2
    shift = dilation * columns
    return copy_all(
        [
            (own, target.at[pl.ds(pl.multiple_of(shift + across * band, columns), band)]),
            (other, target.at[pl.ds(pl.multiple_of(shift + (1 - across) * band, columns), band)]),
            (above, target.at[pl.ds(0, shift)]),
            (below, target.at[pl.ds(shift + 2 * band, shift)]),
        ],
        sems,
    )


def turned(index, count):
    result = 0
    for bit in bits_of(count):
        result = 2 * result + (index // bit) % 2
    return result


def weight_kernel(dilation, with_inner, geometry, *refs):
    rows, columns, shards, parts, piece = geometry
    own_features, refs = refs[:3], refs[3:]
    their_features, refs = refs[:4], refs[4:]
    gradient, refs = refs[:4], refs[4:]
    if with_inner:
        inner, refs = refs[:2], refs[2:]
    theirs, refs = refs[0], refs[1:]
    row_masks, refs = refs[:2], refs[2:]
    col_masks, refs = refs[:2], refs[2:]
    keep, send, feat, side, moved, result, *refs = refs
    if with_inner:
        straight, *refs = refs
    sems, out_sems = refs
    depth, across, canvas = place()
    low, upper = canvas % 2, (canvas // 2) % 2
    pixels = rows * columns
    band = pixels // 2
    shift = dilation * columns
    width = moved.shape[-1]
    lanes = pl.ds(pl.multiple_of(upper * width, width), width)
    starts = [across * band, (1 - across) * band]

    def spans(base, pieces):
        size = band // pieces
        return [
            pl.ds(pl.multiple_of(base + start + number * size, size), size)
            for start in starts
            for number in range(pieces)
        ]

    first = []
    ends = [(0, shift), (shift + pixels, shift)]
    for number in range(2):
        targets = [pl.ds(pl.multiple_of(shift + start, columns), band) for start in starts]
        targets += [pl.ds(*end) for end in ends]
        if number == 0:
            sources = [array.at[:, lanes] for array in gradient]
        else:
            places = [(0, band), (band, band), (pixels, shift), (pixels + shift, shift)]
            sources = [theirs.at[pl.ds(*where)] for where in places]
        first += [
            (source, moved.at[1, number, target]) for source, target in zip(sources, targets)
        ]
    first = copy_all(first, sems)
    second = list(zip(own_features[:1], [feat.at[spans(0, 1)[0]]]))
    second += list(zip(own_features[1:], [feat.at[span] for span in spans(0, 2)[2:]]))
    second += list(zip(their_features, [feat.at[span] for span in spans(pixels, 2)]))
    if with_inner:
        second += [
            (array.at[:, lanes], straight.at[span]) for array, span in zip(inner, spans(0, 1))
        ]
        second += [
            (theirs.at[pl.ds(pixels + 2 * shift + number * band, band)], straight.at[span])
            for number, span in enumerate(spans(pixels, 1))
        ]
    second = copy_all(second, sems.at[pl.ds(8, len(second))])
    for copy in first:
        copy.wait()
    for number in range(2):
        shift_columns(
            moved.at[1, number],
            rows + 2 * dilation,
            columns,
            dilation,
            (col_masks[number][0], col_masks[number][1]),
            side,
            moved.at[2, number],
            moved.at[0, number],
        )
    for copy in second:
        copy.wait()

    def factor(tap):
        if tap == 9:
            return straight[...]
        row_tap, col_tap = divmod(tap, 3)
        start = (2 - row_tap) * shift
        return jnp.concatenate(
            [
                moved[col_tap, number, start : start + pixels, :]
                * spread_rows(row_masks[number][row_tap], columns, width)
                for number in range(2)
            ],
            axis=0,
        )

    half = parts * piece // 2
    taps = 9 + with_inner
    pending = [[], []]
    for turn, tap in enumerate(range(0, taps, TAPS)):
        slot = turn % 2
        pair = list(range(tap, min(tap + TAPS, taps)))
        product = lax.dot_general(
            feat[...],
            jnp.concatenate([factor(member) for member in pair], axis=1),
            (((0,), (0,)), ((), ())),
            preferred_element_type=jnp.float32,
        )
        for copy in pending[slot]:
            copy.wait()
        result[slot, :, 0 : len(pair) * width] = product.astype(jnp.bfloat16)
        copies = []
        for step in range(shards):
            base = (depth ^ step) * 2 * half
            for target, offset in ((keep, low), (send, 1 - low)):
                rows_of = pl.ds(pl.multiple_of(base + offset * half, half), half)
                for number, member in enumerate(pair):
                    part_of = result.at[slot, rows_of, pl.ds(number * width, width)]
                    copies.append((part_of, target.at[turned(step, shards), member]))
        pending[slot] = copy_all(copies, out_sems.at[slot])
    for copies in pending:
        for copy in copies:
            copy.wait()


def weight_branch(features, gradient, inner, theirs, row_masks, col_masks, dilation, geometry):
    rows, columns, shards, parts, piece = geometry
    pixels = rows * columns
    channels = features[0].shape[1]
    width = theirs.shape[1]
    with_inner = int(inner is not None)
    taps = 9 + with_inner
    extended = pixels + 2 * dilation * columns
    part_shape = jax.ShapeDtypeStruct((shards, taps, parts * piece // 2, width), jnp.bfloat16)
    arrays = [*features, *gradient] + (list(inner) if with_inner else []) + [theirs]
    return pl.pallas_call(
        functools.partial(weight_kernel, dilation, with_inner, geometry),
        in_specs=[in_place] * len(arrays) + [in_vmem] * 4,
        out_specs=[in_place, in_place],
        out_shape=[part_shape, part_shape],
        scratch_shapes=[
            pltpu.VMEM((2 * pixels, channels), jnp.bfloat16),
            pltpu.VMEM((width // LANES, GROUP, columns + 2 * SIDE, LANES), jnp.float32),
            pltpu.VMEM((3, 2, extended, width), jnp.bfloat16),
            pltpu.VMEM((2, channels, TAPS * width), jnp.bfloat16),
        ]
        + [pltpu.VMEM((2 * pixels, width), jnp.bfloat16)] * with_inner
        + [
            pltpu.SemaphoreType.DMA((15 + 4 * with_inner,)),
            pltpu.SemaphoreType.DMA((2, 2 * TAPS * shards)),
        ],
        compiler_params=pltpu.CompilerParams(vmem_limit_bytes=vmem_bytes),
        cost_estimate=pl.CostEstimate(
            flops=4 * taps * pixels * channels * width,
            bytes_accessed=4 * pixels * channels + 4 * taps * channels * width,
            transcendentals=0,
        ),
        name=f"weight_{dilation}",
    )(*arrays, *row_masks, *col_masks)


def feature_kernel(geometry, layout, *refs):
    rows, columns, shards, parts, piece = geometry
    branches = len(dilations)
    gradients = [refs[4 * branch : 4 * branch + 4] for branch in range(branches)]
    refs = refs[4 * branches :]
    inner, refs = refs[:2], refs[2:]
    sources, refs = refs[: len(layout)], refs[len(layout) :]
    row_masks, refs = refs[:branches], refs[branches:]
    col_masks, refs = refs[:branches], refs[branches:]
    keep, send, side, straight, moved, result, *refs = refs
    weights, refs = refs[: len(layout)], refs[len(layout) :]
    sems, weight_sems = refs
    depth, across, canvas = place()
    pixels = rows * columns
    band = pixels // 2
    channels = result.shape[1]
    width = straight.shape[1]
    taps_of = {}
    for number, names in enumerate(layout):
        for index, name in enumerate(names):
            taps_of[name] = (number, 9 * index)
    offsets = [pl.multiple_of(across * band, band), pl.multiple_of((1 - across) * band, band)]

    def load_weights(name):
        number, base = taps_of[name]
        span = pl.ds(base, 9 if name else 1)
        order = (0,) + dilations
        return copy_all(
            [(sources[number].at[span], weights[number].at[span])],
            weight_sems.at[pl.ds(order.index(name), 1)],
        )

    waits = copy_all(
        [
            (inner[0], straight.at[pl.ds(offsets[0], band)]),
            (inner[1], straight.at[pl.ds(offsets[1], band)]),
        ],
        sems.at[pl.ds(4 * branches, 2)],
    )
    loads = {0: load_weights(0)}
    arrivals = []
    for branch, dilation in enumerate(dilations):
        arrivals.append(
            load_gradient(
                rows,
                columns,
                dilation,
                gradients[branch],
                moved.at[branch % 2, 1],
                sems.at[pl.ds(4 * branch, 4)],
            )
            if branch < 2
            else None
        )
        loads[dilation] = load_weights(dilation)
    tile = pixels // 4
    for copy in waits + loads[0]:
        copy.wait()
    for first in range(0, pixels, tile):
        span = slice(first, first + tile)
        number, base = taps_of[0]
        result[span, :] = lax.dot_general(
            straight[span, :],
            weights[number][base],
            (((1,), (1,)), ((), ())),
            preferred_element_type=jnp.float32,
        )
    for branch, dilation in enumerate(dilations):
        slot = branch % 2
        shift = dilation * columns
        for copy in arrivals[branch]:
            copy.wait()
        shift_columns(
            moved.at[slot, 1],
            rows + 2 * dilation,
            columns,
            dilation,
            (col_masks[branch][0], col_masks[branch][1]),
            side,
            moved.at[slot, 2],
            moved.at[slot, 0],
        )
        for copy in loads[dilation]:
            copy.wait()
        number, base = taps_of[dilation]
        for first in range(0, pixels, tile):
            span = slice(first, first + tile)
            product = jnp.zeros((tile, channels), jnp.float32)
            for row_tap in range(3):
                mask = spread_rows(
                    row_masks[branch][row_tap, first // columns : (first + tile) // columns],
                    columns,
                    width,
                )
                start = (2 - row_tap) * shift + first
                for col_tap in range(3):
                    product += lax.dot_general(
                        moved[slot, col_tap, start : start + tile, :] * mask,
                        weights[number][base + 3 * row_tap + col_tap],
                        (((1,), (1,)), ((), ())),
                        preferred_element_type=jnp.float32,
                    )
            result[span, :] += product
        if branch + 2 < branches:
            arrivals[branch + 2] = load_gradient(
                rows,
                columns,
                dilations[branch + 2],
                gradients[branch + 2],
                moved.at[slot, 1],
                sems.at[pl.ds(4 * (branch + 2), 4)],
            )
    keep[...] = result[pl.ds(pl.multiple_of(across * band, band), band), :]
    send[...] = result[pl.ds(pl.multiple_of((1 - across) * band, band), band), :].astype(
        jnp.bfloat16
    )


def feature_branches(gradients, inner, row_masks, col_masks, weights, layout, geometry):
    rows, columns, shards, parts, piece = geometry
    pixels = rows * columns
    band = pixels // 2
    channels, width = weights[0].shape[1:]
    arrays = [array for gradient in gradients for array in gradient] + list(inner)
    taps = sum(array.shape[0] for array in weights)
    extended = pixels + 2 * max(dilations) * columns
    return pl.pallas_call(
        functools.partial(feature_kernel, geometry, layout),
        in_specs=[in_place] * (len(arrays) + len(weights))
        + [in_vmem] * (len(row_masks) + len(col_masks)),
        out_specs=[in_vmem] * 2,
        out_shape=[
            jax.ShapeDtypeStruct((band, channels), jnp.float32),
            jax.ShapeDtypeStruct((band, channels), jnp.bfloat16),
        ],
        scratch_shapes=[
            pltpu.VMEM((width // LANES, GROUP, columns + 2 * SIDE, LANES), jnp.float32),
            pltpu.VMEM((pixels, width), jnp.bfloat16),
            pltpu.VMEM((2, 3, extended, width), jnp.bfloat16),
            pltpu.VMEM((pixels, channels), jnp.float32),
        ]
        + [pltpu.VMEM(array.shape, jnp.bfloat16) for array in weights]
        + [
            pltpu.SemaphoreType.DMA((len(arrays),)),
            pltpu.SemaphoreType.DMA((1 + len(dilations),)),
        ],
        compiler_params=pltpu.CompilerParams(vmem_limit_bytes=vmem_bytes),
        cost_estimate=pl.CostEstimate(
            flops=2 * taps * pixels * channels * width,
            bytes_accessed=6 * band * channels + 2 * taps * channels * width,
            transcendentals=0,
        ),
        name="feature_gradient",
    )(*arrays, *weights, *row_masks, *col_masks)


def interp_matrix(out_first, out_count, in_first, in_count, row_limit):
    out_rows = out_first + jnp.arange(out_count, dtype=jnp.int32)
    source = jnp.floor_divide(out_rows, 4)
    residue = out_rows - 4 * source
    targets = in_first + jnp.arange(in_count, dtype=jnp.int32)
    matrix = jnp.zeros((out_count, in_count), jnp.float32)
    for offset, coeffs in ((-1, prev_weights), (0, self_weights), (1, next_weights)):
        factor = jnp.zeros((out_count,), jnp.float32)
        for member in range(4):
            factor = factor + jnp.where(residue == member, coeffs[member], 0.0)
        clamped = jnp.clip(source + offset, 0, row_limit - 1)
        matrix = matrix + factor[:, None] * (clamped[:, None] == targets[None, :]).astype(
            jnp.float32
        )
    return matrix


def silu_slope(values):
    logistic = jax.nn.sigmoid(values)
    return logistic * (1.0 + values * (1.0 - logistic))


def normalize(values, sum_rows, total_count, scale_vec, shift_vec):
    average = sum_rows[0] / total_count
    spread_of = sum_rows[1] / total_count - average * average
    inverse = lax.rsqrt(spread_of + epsilon)
    centered = (values - average) * inverse
    return (centered, inverse, scale_vec * centered + shift_vec)


def input_grad(slope, centered, inverse, scale_vec, totals, total_count, weight_map):
    return (
        scale_vec
        * inverse
        * (slope - weight_map * (totals[0] + centered * totals[1]) / total_count)
    )


def moments_of(values, weight_map):
    weighted = weight_map * values
    return [jnp.sum(weighted, axis=0), jnp.sum(weighted * values, axis=0)]


def per_device(
    features,
    segment_map,
    pixel_mask,
    inner_weight,
    atrous_weight,
    pool_weight,
    proj_weight,
    norm_gains,
    norm_shifts,
    cotangent,
):
    highest = lax.Precision.HIGHEST
    row_count = lax.axis_size("rows")
    canvas_count = lax.axis_size("canvas") * features.shape[0]
    band_rows, columns, channels = features.shape[1:]
    branch_width = norm_gains.shape[1]
    canvas_rows = band_rows * row_count
    image_count = COL_IMAGES * (canvas_rows // 36)
    row_index = lax.axis_index("rows")
    canvas_index = lax.axis_index("canvas")
    shards = row_count // 2
    depth = row_index // 2
    first_band = row_index % 2 == 0
    row_first = row_index * band_rows
    rows = 2 * band_rows
    band = band_rows * columns
    pixels = rows * columns
    slice_rows = channels // row_count
    parts = min(lax.axis_size("canvas"), max(slice_rows // 16, 1))
    piece = slice_rows // parts
    part = canvas_index % parts
    geometry = (rows, columns, shards, parts, piece)

    flat_mask = pixel_mask.reshape(band, 1)
    valid_mask = flat_mask.astype(jnp.float32)
    segments = segment_map.reshape(band)
    places = jnp.arange(columns)
    col_ids = segment_map[0, 0, :] % COL_IMAGES

    def col_checks(col_ids):
        masks = {}
        for dilation in dilations:
            table = []
            for offset in (-dilation, dilation):
                moved = places + offset
                inside = (moved >= 0) & (moved < columns)
                table.append(inside & (jnp.roll(col_ids, -offset) == col_ids))
            table = jnp.stack(table).astype(jnp.float32)
            masks[dilation] = jnp.broadcast_to(table[:, :, None], (2, columns, LANES))
        return masks

    col_masks = col_checks(col_ids)

    taps = lax.dynamic_slice_in_dim(
        atrous_weight.reshape(9 * len(dilations), slice_rows, branch_width),
        part * piece,
        piece,
        axis=1,
    )
    inner_taps = lax.dynamic_slice_in_dim(inner_weight, part * piece, piece, axis=0)[None]
    quarter = jnp.concatenate(
        [
            item
            for dilation in (18, 0, 12, 6)
            for item in (
                [taps[9 * dilations.index(dilation) :][:9]] if dilation else [inner_taps]
            )
        ],
        axis=0,
    )
    own_taps = (
        atrous_weight.reshape(len(dilations), 9, slice_rows, branch_width),
        inner_weight,
    )
    row_ids = segment_map[0, :, 0] // COL_IMAGES + 1
    both_ids = halves(first_band, row_ids, swap(row_ids, "rows", 1))
    low_mask = flat_mask.astype(jnp.bfloat16)
    flat_features = features.reshape(band, channels)
    slices = [flat_features[:, i * slice_rows : (i + 1) * slice_rows] for i in range(row_count)]
    even = jnp.concatenate(slices[0::2], axis=1)
    odd = jnp.concatenate(slices[1::2], axis=1)
    middle = band // 2
    feat_send = jnp.where(first_band, odd, even) * low_mask
    feat_own, quarter_later, *feat_parts = tie(
        jnp.where(first_band, even, odd) * low_mask,
        quarter,
        feat_send[:middle],
        feat_send[middle:],
    )
    group = shards // 2

    def along(start, bits):
        found = [start]
        for bit in bits:
            found = found + [swap(item, "rows", 2 * bit) for item in found]
        return found

    def between(item):
        chain = [item]
        for bit in bits_of(parts)[1:]:
            chain = chain + [swap(other, "canvas", bit) for other in chain]
        return chain

    def from_partner(chain):
        stacked = jnp.stack(chain)
        return [stacked, swap(stacked, "canvas", 1)]

    def sum_step(values, bit):
        return values + swap(values, "rows", bit)

    def gather_step(values, bit):
        other = swap(values, "rows", bit)
        both = jnp.where(
            (row_index & bit) == 0,
            jnp.stack([values, other], axis=1),
            jnp.stack([other, values], axis=1),
        )
        return both.reshape((2 * values.shape[0],) + values.shape[1:])

    rounds = bits_of(row_count)
    near = along(quarter, bits_of(group))[1:]
    feat_first = swap(feat_parts[0], "rows", 1)
    reach = max(dilations)

    def row_checks(all_ids, outside):
        masks = {}
        for dilation in dilations:
            checks = []
            for row_tap in range(3):
                start = reach - (row_tap - 1) * dilation
                target = all_ids[start : start + rows]
                same = target == all_ids[reach : reach + rows]
                checks.append(jnp.where(target == 0, outside, same))
            table = jnp.stack(checks).astype(jnp.bfloat16)
            masks[dilation] = jnp.broadcast_to(table[:, :, None, None], (3, rows, TILE, LANES))
        return masks

    near_masks = row_checks(jnp.pad(both_ids, (reach, reach)), True)
    col_matrix = interp_matrix(0, 4 * columns, 0, columns, columns)
    col_grad = jnp.einsum(
        "pw,opb->owb",
        col_matrix.astype(jnp.bfloat16),
        cotangent[0],
        preferred_element_type=jnp.float32,
    )
    near, both_ids, col_grad, near_masks = tie(near, both_ids, col_grad, near_masks)

    far_first = swap(quarter_later, "rows", 2 * group)
    near_chains = [between(item) for item in near]
    feat_second = swap(feat_parts[1], "rows", 1)
    members = (segments[:, None] == jnp.arange(image_count, dtype=jnp.int32)).astype(jnp.float32)
    member_low = members.astype(jnp.bfloat16)
    seg_sums = jnp.einsum(
        "ps,pc->sc", member_low, flat_features * low_mask, preferred_element_type=jnp.float32
    )
    seg_counts = jnp.sum(members * valid_mask, axis=0)
    seg_all = jnp.concatenate(
        [seg_sums, jnp.broadcast_to(seg_counts[:, None], (image_count, LANES))], axis=1
    )
    far_first, near_chains, feat_first, feat_second, seg_all, proj_full = tie(
        far_first, near_chains, feat_first, feat_second, seg_all, proj_weight[None]
    )

    feat_others = (feat_first, feat_second)
    far = along(far_first, bits_of(group))
    far_chains = [between(far_first)]
    near_pieces = [item for chain in near_chains for item in from_partner(chain)]
    seg_all = sum_step(seg_all, rounds[0])
    proj_full = gather_step(proj_full, rounds[0])
    first_taps = {18: 0, 12: 10, 6: 19}

    def forward(which, pieces, earlier=None):
        return forward_branches(
            feat_own,
            feat_others,
            own_taps,
            pieces,
            [near_masks[dilation] for dilation in which],
            [col_masks[dilation] for dilation in which],
            earlier,
            which,
            int(which == (18,)),
            first_taps[which[0]],
            geometry,
        )

    total_18, total_inner, weights_00 = forward((18,), near_pieces)
    (far, far_chains, seg_all, proj_full, total_18, total_inner, near_pieces) = tie(
        far, far_chains, seg_all, proj_full, total_18, total_inner, near_pieces
    )

    far_chains = far_chains + [between(item) for item in far[1:]]
    far_pieces = from_partner(far_chains[0])
    total_12, total_6, weights_01 = forward((12, 6), near_pieces)
    seg_all = sum_step(seg_all, rounds[1])
    proj_full = gather_step(proj_full, rounds[-1])
    far_chains, far_pieces, total_12, total_6, seg_all, proj_full, both_ids, col_grad = tie(
        far_chains, far_pieces, total_12, total_6, seg_all, proj_full, both_ids, col_grad
    )

    far_pieces = far_pieces + [item for chain in far_chains[1:] for item in from_partner(chain)]
    id_above, id_below = trade(both_ids[:reach], both_ids[rows - reach :], 2)
    all_ids = jnp.concatenate([id_above, both_ids, id_below])
    for bit in rounds[2:]:
        seg_all = sum_step(seg_all, bit)
    for bit in rounds[-2:0:-1]:
        proj_full = gather_step(proj_full, bit)
    proj_full = proj_full.reshape((2, shards) + proj_full.shape[1:]).swapaxes(0, 1)
    proj_full = proj_full.reshape(-1, branch_width)
    grad_above, grad_below = trade(col_grad[:2], col_grad[4 * band_rows - 2 :], 1)
    grad_ext = jnp.concatenate([grad_above, col_grad, grad_below], axis=0)
    their_first = swap(feat_first, "canvas", 2)
    far_pieces, seg_all, proj_full, all_ids, grad_ext, their_first = tie(
        far_pieces, seg_all, proj_full, all_ids, grad_ext, their_first
    )
    their_ids = swap(jnp.concatenate([all_ids, col_ids]), "canvas", 2)
    their_second = swap(tie(feat_second, all_ids)[0], "canvas", 2)

    def to_partner(partials):
        sent = [
            jnp.where(first_band, partial[band:], partial[:band]).astype(jnp.bfloat16)
            for partial in partials
        ]
        return swap(jnp.concatenate(sent, axis=1), "rows", 1)

    def complete(partial, back):
        mine = jnp.where(first_band, partial[:band], partial[band:])
        return mine + back.astype(jnp.float32)

    def beyond_bands(dilation, main, above, below):
        shift = dilation * columns
        here = all_ids[reach : reach + rows]
        mask = here[:dilation] == all_ids[reach - dilation : reach]
        mask = jnp.broadcast_to(mask[:, None], (dilation, columns)).reshape(shift, 1)
        below = below.astype(jnp.float32) * mask.astype(jnp.float32)
        mask = here[rows - dilation :] == all_ids[reach + rows : reach + rows + dilation]
        mask = jnp.broadcast_to(mask[:, None], (dilation, columns)).reshape(shift, 1)
        above = above.astype(jnp.float32) * mask.astype(jnp.float32)
        return jnp.concatenate(
            [
                main[:shift] + below,
                main[shift : pixels - shift],
                main[pixels - shift :] + above,
            ],
            axis=0,
        )

    main_18, above_18, below_18, main_inner, weights_10 = forward(
        (18,), far_pieces, [total_18, total_inner]
    )
    far_pieces, main_18, above_18, below_18, main_inner, seg_all = tie(
        far_pieces, main_18, above_18, below_18, main_inner, seg_all
    )
    back_inner = to_partner([main_inner])
    their_own = [swap(tie(feat_own[:middle], main_18)[0], "canvas", 2)]
    below_18, above_18 = trade(above_18, below_18, 2)
    main_12, above_12, below_12, weights_11 = forward((12,), far_pieces, [total_12])
    total_counts = seg_all[:, channels : channels + 1]
    pooled = lax.dynamic_slice_in_dim(seg_all, row_index * slice_rows, slice_rows, axis=1)
    pooled = pooled / total_counts
    pool_matrix = pool_weight.astype(jnp.float32)
    pool_part = jnp.dot(pooled, pool_matrix, precision=highest)
    (
        far_pieces,
        main_12,
        above_12,
        below_12,
        back_inner,
        above_18,
        below_18,
        pool_part,
        their_ids,
        their_second,
    ) = tie(
        far_pieces,
        main_12,
        above_12,
        below_12,
        back_inner,
        above_18,
        below_18,
        pool_part,
        their_ids,
        their_second,
    )
    their_own.append(swap(tie(feat_own[middle:], main_12)[0], "canvas", 2))
    row_masks = row_checks(all_ids, False)
    reached = all_ids.shape[0]
    their_row_masks = row_checks(their_ids[:reached], False)
    their_col_masks = col_checks(their_ids[reached:])
    main_18 = beyond_bands(18, main_18, above_18, below_18)
    back_18 = to_partner([main_18])
    below_12, above_12 = trade(above_12, below_12, 2)
    main_6, above_6, below_6, weights_12 = forward((6,), far_pieces, [total_6])
    back_matrix = interp_matrix(
        4 * row_first - 2, 4 * band_rows + 4, row_first, band_rows, canvas_rows
    )
    back_18, above_12, below_12, main_6, above_6, below_6, grad_ext, row_masks, their_own[0] = tie(
        back_18, above_12, below_12, main_6, above_6, below_6, grad_ext, row_masks, their_own[0]
    )
    main_12 = beyond_bands(12, main_12, above_12, below_12)
    back_12 = to_partner([main_12])
    below_6, above_6 = trade(above_6, below_6, 2)
    act_grad = jnp.einsum("or,owb->rwb", back_matrix, grad_ext, precision=highest)
    act_grad = act_grad.reshape(band, branch_width)
    back_12, above_6, below_6, act_grad = tie(back_12, above_6, below_6, act_grad)
    main_6 = beyond_bands(6, main_6, above_6, below_6)
    back_6 = to_partner([main_6])
    back_6, their_own[1], their_row_masks = tie(back_6, their_own[1], their_row_masks)
    all_features = (feat_own, feat_first, feat_second, *their_own, their_first, their_second)
    conv_outs = [
        complete(main_inner, back_inner),
        complete(main_6, back_6),
        complete(main_12, back_12),
        complete(main_18, back_18),
    ]
    weights_full = [[weights_00, weights_01], [weights_10, weights_11, weights_12]]
    layouts = (((18, 0), (12, 6)), ((18, 0), (12,), (6,)))

    rows_of = []
    for conv_out in conv_outs:
        rows_of += moments_of(conv_out, valid_mask)
    rows_of.append(jnp.broadcast_to(jnp.sum(valid_mask), (branch_width,)))
    sums = sum_over(jnp.concatenate([jnp.stack(rows_of), pool_part]), "rows")
    pool_out = sums[9:]
    sums = sum_over(
        jnp.concatenate(
            [
                sums[:8],
                jnp.sum(pool_out, axis=0, keepdims=True),
                jnp.sum(pool_out * pool_out, axis=0, keepdims=True),
                sums[8:9],
            ]
        ),
        "canvas",
    )
    pixel_total = sums[10]
    entries = float(canvas_count * image_count)
    normals = [
        normalize(
            conv_out,
            sums[2 * branch : 2 * branch + 2],
            pixel_total,
            norm_gains[branch],
            norm_shifts[branch],
        )
        for branch, conv_out in enumerate(conv_outs)
    ]
    pool_norm = normalize(pool_out, sums[8:10], entries, norm_gains[4], norm_shifts[4])
    pool_act = jax.nn.silu(pool_norm[2]).astype(jnp.bfloat16)
    pool_map = jnp.dot(member_low, pool_act, preferred_element_type=jnp.float32)
    concat_act = jnp.concatenate(
        [jax.nn.silu(item[2]).astype(jnp.bfloat16) for item in normals]
        + [pool_map.astype(jnp.bfloat16)],
        axis=-1,
    )
    proj_out = jnp.dot(concat_act, proj_full, preferred_element_type=jnp.float32)
    proj_totals = sum_over(
        sum_over(jnp.stack(moments_of(proj_out, valid_mask)), "rows"), "canvas"
    )
    proj_norm = normalize(proj_out, proj_totals, pixel_total, norm_gains[5], norm_shifts[5])
    proj_act = jax.nn.silu(proj_norm[2]).astype(jnp.bfloat16)

    act_rows = proj_act.reshape(band_rows, columns, branch_width)
    act_above, act_below = trade(act_rows[:1], act_rows[band_rows - 1 :], 1)
    ext_act = jnp.concatenate([act_above, act_rows, act_below], axis=0)

    proj_slope = act_grad * silu_slope(proj_norm[2])
    proj_local = jnp.stack(
        [jnp.sum(proj_slope, axis=0), jnp.sum(proj_slope * proj_norm[0], axis=0)]
    )
    proj_grad_totals = sum_over(sum_over(proj_local, "rows"), "canvas")
    proj_grad = input_grad(
        proj_slope,
        proj_norm[0],
        proj_norm[1],
        norm_gains[5],
        proj_grad_totals,
        pixel_total,
        valid_mask,
    ).astype(jnp.bfloat16)
    joined_grad = lax.dot_general(
        proj_grad, proj_full, (((1,), (1,)), ((), ())), preferred_element_type=jnp.float32
    )
    slopes = [
        joined_grad[:, branch * branch_width : (branch + 1) * branch_width]
        * silu_slope(normals[branch][2])
        for branch in range(4)
    ]
    rows_of = []
    for branch, slope in enumerate(slopes):
        rows_of += [jnp.sum(slope, axis=0), jnp.sum(slope * normals[branch][0], axis=0)]
    seg_grads = lax.dot_general(
        members, joined_grad[:, 4 * branch_width :], (((0,), (0,)), ((), ())), precision=highest
    )
    pool_terms = seg_grads * silu_slope(pool_norm[2])
    rows_of += [jnp.sum(pool_terms, axis=0), jnp.sum(pool_terms * pool_norm[0], axis=0)]
    sums = sum_over(jnp.concatenate([jnp.stack(rows_of), seg_grads], axis=0), "rows")
    seg_grads = sums[10:]
    sums = sum_over(sums[:10], "canvas")
    branch_totals = [sums[2 * branch : 2 * branch + 2] for branch in range(5)]
    conv_grads = [
        input_grad(
            slopes[branch],
            normals[branch][0],
            normals[branch][1],
            norm_gains[branch],
            branch_totals[branch],
            pixel_total,
            valid_mask,
        ).astype(jnp.bfloat16)
        for branch in range(4)
    ]

    pool_grad = input_grad(
        seg_grads * silu_slope(pool_norm[2]),
        pool_norm[0],
        pool_norm[1],
        norm_gains[4],
        branch_totals[4],
        entries,
        1.0,
    )
    pooled_grad = (
        lax.dot_general(pool_matrix, pool_grad, (((1,), (1,)), ((), ())), precision=highest)
        / total_counts[:, 0]
    )
    grad_pool = lax.dot_general(
        pooled, pool_grad, (((0,), (0,)), ((), ())), precision=highest
    )
    grad_proj = lax.dot_general(
        concat_act, proj_grad, (((0,), (0,)), ((), ())), preferred_element_type=jnp.float32
    )

    grad_proj = grad_proj.reshape((row_count,) + (grad_proj.shape[0] // row_count, branch_width))

    def scatter_step(values, bit):
        values = values.reshape((values.shape[0] // 2, 2) + values.shape[1:])
        low, high = values[:, 0], values[:, 1]
        mine = (row_index & bit) == 0
        sent = jnp.where(mine, high, low).astype(jnp.bfloat16)
        return jnp.where(mine, low, high) + swap(sent, "rows", bit).astype(jnp.float32)

    def beyond(branch, other):
        grad = conv_grads[branch + 1]
        shift = dilations[branch] * columns
        top = jnp.where(first_band, grad[:shift], other[:shift])
        bottom = jnp.where(first_band, other[band - shift :], grad[band - shift :])
        return (grad, other, *trade(top, bottom, 2))

    def pair_sum(kept, got):
        return kept.astype(jnp.float32) + got.astype(jnp.float32)

    def halve(kept, got, axis, bit):
        size = kept.shape[0] // 2
        sent = pair_sum(kept[size:], got[size:]).astype(jnp.bfloat16)
        return pair_sum(kept[:size], got[:size]), swap(sent, axis, bit)

    def weights_of(branch, theirs, inner=None):
        dilation = dilations[branch]
        return weight_branch(
            all_features,
            gradients[branch],
            inner,
            theirs,
            [row_masks[dilation], their_row_masks[dilation]],
            [col_masks[dilation], their_col_masks[dilation]],
            dilation,
            geometry,
        )

    half_width = branch_width // 2
    upper = (canvas_index // 2) % 2 == 1

    def for_partner(arrays):
        return jnp.concatenate(
            [jnp.where(upper, array[:, :half_width], array[:, half_width:]) for array in arrays]
        )

    along_rows = [("rows", 2 * bit) for bit in bits_of(shards)]

    def finish(kept, got):
        total = pair_sum(kept, got)[0]
        for bit in bits_of(lax.axis_size("canvas"))[2:]:
            total = total + swap(total, "canvas", bit)
        return lax.optimization_barrier(total.astype(jnp.bfloat16))

    def other_channels(block):
        other = swap(block, "canvas", 2)
        return jnp.where(
            upper,
            jnp.concatenate([other, block], axis=2),
            jnp.concatenate([block, other], axis=2),
        )

    def other_rows_of(block):
        other = swap(block, "canvas", 1)
        return jnp.where(
            canvas_index % 2 == 0,
            jnp.concatenate([block, other], axis=1),
            jnp.concatenate([other, block], axis=1),
        )

    def features_of(half):
        return feature_branches(
            gradients,
            inner_grads,
            [row_masks[dilation] for dilation in dilations],
            [col_masks[dilation] for dilation in dilations],
            weights_full[half],
            layouts[half],
            geometry,
        )

    other = swap(conv_grads[1], "rows", 1)
    other, ext_act, *conv_grads = tie(other, ext_act, *conv_grads)
    row_matrix = interp_matrix(
        4 * row_first, 4 * band_rows, row_first - 1, band_rows + 2, canvas_rows
    ).astype(jnp.bfloat16)
    rows_up = jnp.einsum("or,rwb->owb", row_matrix, ext_act, preferred_element_type=jnp.float32)
    high = rows_up.astype(jnp.bfloat16)
    low = (rows_up - high.astype(jnp.float32)).astype(jnp.bfloat16)
    upsampled = jnp.einsum(
        "pw,owb->opb",
        jnp.concatenate([col_matrix, col_matrix], axis=1).astype(jnp.bfloat16),
        jnp.concatenate([high, low], axis=1),
        preferred_element_type=jnp.float32,
    ).astype(jnp.bfloat16)
    gradients = [beyond(0, other)]
    other = swap(conv_grads[2], "rows", 1)
    gradients, other, conv_grads, upsampled = tie(gradients, other, conv_grads, upsampled)
    theirs_6 = swap(for_partner(gradients[0]), "canvas", 2)
    gradients.append(beyond(1, other))
    other = swap(jnp.concatenate([conv_grads[3], conv_grads[0]], axis=1), "rows", 1)
    canvas_bits = bits_of(lax.axis_size("canvas"))
    grad_pool = grad_pool + swap(grad_pool, "canvas", canvas_bits[0])
    gradients, theirs_6, other, grad_proj, pooled_grad, grad_pool = tie(
        gradients, theirs_6, other, grad_proj, pooled_grad, grad_pool
    )
    theirs_12 = swap(for_partner(gradients[1]), "canvas", 2)
    gradients.append(beyond(2, other[:, :branch_width]))
    inner_grads = (conv_grads[0], other[:, branch_width:])
    kept_6, sent_6 = weights_of(0, theirs_6)
    grad_proj = scatter_step(grad_proj, rounds[0])
    pooled_grad = gather_step(pooled_grad[None], rounds[-1])
    (
        gradients,
        inner_grads,
        theirs_12,
        kept_6,
        sent_6,
        grad_proj,
        pooled_grad,
        grad_pool,
    ) = tie(
        gradients,
        inner_grads,
        theirs_12,
        kept_6,
        sent_6,
        grad_proj,
        pooled_grad,
        grad_pool,
    )
    theirs_18 = swap(for_partner([*gradients[2], *inner_grads]), "canvas", 2)
    got_6 = swap(sent_6, "canvas", 1)
    kept_12, sent_12 = weights_of(1, theirs_12)
    grad_proj = scatter_step(grad_proj, rounds[1])
    pooled_grad = gather_step(pooled_grad, rounds[-2])
    gradients, inner_grads, kept_6, got_6, kept_12, sent_12, grad_proj, pooled_grad = tie(
        gradients, inner_grads, kept_6, got_6, kept_12, sent_12, grad_proj, pooled_grad
    )
    kept_6, got_6 = halve(kept_6, got_6, *along_rows[0])
    got_12 = swap(sent_12, "canvas", 1)
    feature_0 = features_of(0)
    for bit in rounds[2:]:
        grad_proj = scatter_step(grad_proj, bit)
    grad_proj = grad_proj[0]
    for bit in rounds[-3::-1]:
        pooled_grad = gather_step(pooled_grad, bit)
    pooled_grad = pooled_grad.reshape(channels, image_count)
    (
        gradients,
        inner_grads,
        theirs_18,
        kept_6,
        got_6,
        kept_12,
        got_12,
        feature_0,
        grad_proj,
        pooled_grad,
    ) = tie(
        gradients,
        inner_grads,
        theirs_18,
        kept_6,
        got_6,
        kept_12,
        got_12,
        feature_0,
        grad_proj,
        pooled_grad,
    )
    kept_6, got_6 = halve(kept_6, got_6, *along_rows[1])
    kept_12, got_12 = halve(kept_12, got_12, *along_rows[0])
    back_0 = swap(feature_0[1], "rows", 1)
    kept_18, sent_18 = weights_of(2, theirs_18, inner_grads)
    grad_proj = grad_proj + swap(grad_proj, "canvas", canvas_bits[0])
    shared = jnp.concatenate([grad_pool, grad_proj], axis=0)
    (
        gradients,
        kept_6,
        got_6,
        kept_12,
        got_12,
        kept_18,
        sent_18,
        back_0,
        shared,
    ) = tie(
        gradients,
        kept_6,
        got_6,
        kept_12,
        got_12,
        kept_18,
        sent_18,
        back_0,
        shared,
    )
    for axis, bit in along_rows[2:]:
        kept_6, got_6 = halve(kept_6, got_6, axis, bit)
    part_6 = finish(kept_6, got_6)
    for axis, bit in along_rows[1:]:
        kept_12, got_12 = halve(kept_12, got_12, axis, bit)
    got_18 = swap(sent_18, "canvas", 1)
    feature_1 = features_of(1)
    for bit in canvas_bits[1:]:
        shared = shared + swap(shared, "canvas", bit)
    grad_pool, grad_proj = shared[:slice_rows], shared[slice_rows:]
    part_6, kept_12, got_12, kept_18, got_18, feature_1, grad_pool, grad_proj, back_0 = tie(
        part_6, kept_12, got_12, kept_18, got_18, feature_1, grad_pool, grad_proj, back_0
    )
    kept_18, got_18 = halve(kept_18, got_18, *along_rows[0])
    early = other_channels(jnp.concatenate([part_6, finish(kept_12, got_12)]))
    back_1 = swap(feature_1[1], "rows", 1)
    kept_18, got_18, early, back_1 = tie(kept_18, got_18, early, back_1)
    for axis, bit in along_rows[1:]:
        kept_18, got_18 = halve(kept_18, got_18, axis, bit)
    early = other_rows_of(early)
    evens, odds = [], []
    for (kept, _), back in ((feature_0, back_0), (feature_1, back_1)):
        other = back.astype(jnp.float32)
        evens.append(jnp.where(first_band, kept, other))
        odds.append(jnp.where(first_band, other, kept))
    low_first = depth < group
    even = jnp.where(
        low_first, jnp.concatenate(evens, axis=1), jnp.concatenate(evens[::-1], axis=1)
    )
    odd = jnp.where(low_first, jnp.concatenate(odds, axis=1), jnp.concatenate(odds[::-1], axis=1))
    joined = []
    for shard in range(shards):
        span = slice(shard * slice_rows, (shard + 1) * slice_rows)
        joined += [even[:, span], odd[:, span]]
    spread_pool = lax.dot_general(
        members, pooled_grad, (((1,), (1,)), ((), ())), precision=highest
    )
    grad_features = (jnp.concatenate(joined, axis=1) + spread_pool) * valid_mask
    grad_atrous = jnp.zeros((9 * len(dilations), slice_rows, branch_width), jnp.float32)
    grad_atrous = lax.dynamic_update_slice(grad_atrous, early.astype(jnp.float32), (0, 0, 0))
    kept_18, got_18, grad_atrous, grad_features = tie(kept_18, got_18, grad_atrous, grad_features)
    late = other_rows_of(other_channels(finish(kept_18, got_18)))
    grad_inner = late[9].astype(jnp.float32)
    grad_atrous = lax.dynamic_update_slice(
        grad_atrous, late[:9].astype(jnp.float32), (early.shape[0], 0, 0)
    ).reshape(atrous_weight.shape)

    grad_gains = jnp.stack([totals[1] for totals in branch_totals] + [proj_grad_totals[1]])
    grad_shifts = jnp.stack([totals[0] for totals in branch_totals] + [proj_grad_totals[0]])
    return (
        upsampled[None],
        grad_features.reshape(features.shape),
        grad_inner,
        grad_atrous,
        grad_pool,
        grad_proj,
        grad_gains,
        grad_shifts,
    )


def solution(mesh):
    in_specs = (
        P("canvas", "rows", None, None),
        P("canvas", "rows", None),
        P("canvas", "rows", None),
        P("rows", None),
        P(None, None, "rows", None),
        P("rows", None),
        P("rows", None),
        P(),
        P(),
        P("canvas", "rows", None, None),
    )
    out_specs = (
        P("canvas", "rows", None, None),
        P("canvas", "rows", None, None),
        P("rows", None),
        P(None, None, "rows", None),
        P("rows", None),
        P("rows", None),
        P(),
        P(),
    )
    return jax.shard_map(
        per_device, mesh=mesh, in_specs=in_specs, out_specs=out_specs, check_vma=False
    )
```

```python
import functools

import jax
import jax.numpy as jnp
import numpy as np
from jax import lax
from jax.experimental import pallas as pl
from jax.experimental.pallas import tpu as pltpu
from jax.sharding import PartitionSpec as P

COL_IMAGES = 2
LANES = 128
SIDE = 24
TILE = 16
TILES = 4
TAPS = 4
GROUP = 6

dilations = (6, 12, 18)
epsilon = 1e-05
prev_weights = (0.375, 0.125, 0.0, 0.0)
self_weights = (0.625, 0.875, 0.875, 0.625)
next_weights = (0.0, 0.0, 0.125, 0.375)
vmem_bytes = 58 << 20
in_place = pl.BlockSpec(memory_space=pl.ANY)
in_vmem = pl.BlockSpec(memory_space=pltpu.VMEM)


def swap(values, axis, bit):
    count = lax.axis_size(axis)
    return lax.ppermute(values, axis, [(i, i ^ bit) for i in range(count)])


def bits_of(count):
    bits, bit = [], 1
    while bit < count:
        bits.append(bit)
        bit *= 2
    return bits


def sum_over(values, axis):
    bits = bits_of(lax.axis_size(axis))
    for first in range(0, len(bits), 2):
        pair = bits[first : first + 2]
        found = [swap(values, axis, bit) for bit in pair]
        if len(pair) == 2:
            found.append(swap(values, axis, pair[0] ^ pair[1]))
            values = (values + found[0]) + (found[1] + found[2])
        else:
            values = values + found[0]
    return values


def trade(above, below, width):
    count = lax.axis_size("rows")
    odd = (lax.axis_index("rows") // width) % 2 == 1
    first = swap(jnp.where(odd, above, below), "rows", width)
    pairs = []
    for band in range(count):
        other = band + width if (band // width) % 2 else band - width
        if 0 <= other < count:
            pairs.append((band, other))
    second = lax.ppermute(jnp.where(odd, below, above), "rows", pairs)
    return jnp.where(odd, first, second), jnp.where(odd, second, first)


def tie(*values):
    return lax.optimization_barrier(values)


def halves(first, lower, upper):
    return jnp.where(
        first, jnp.concatenate([lower, upper], axis=0), jnp.concatenate([upper, lower], axis=0)
    )


def place():
    row = lax.axis_index("rows")
    return row // 2, row % 2, lax.axis_index("canvas")


def other_rows(across, band):
    start = (1 - across) * band
    return [
        pl.ds(pl.multiple_of(start + piece * (band // 2), band // 2), band // 2)
        for piece in range(2)
    ]


def copy_all(copies, sems):
    started = []
    for number, (source, target) in enumerate(copies):
        copy = pltpu.make_async_copy(source, target, sems.at[number])
        copy.start()
        started.append(copy)
    return started


def spread(mask, width):
    return jnp.concatenate([mask] * (width // LANES), axis=1)


def spread_rows(mask, columns, width):
    mask = jnp.concatenate([mask] * (columns // TILE), axis=1)
    return spread(mask.reshape(mask.shape[0] * columns, LANES), width)


def shift_columns(source, rows, columns, distance, masks, side, left, right):
    inside = [masks[index] != 0 for index in range(2)]
    chunks = source.shape[-1] // LANES

    def step(group, carry):
        starts = [
            pl.multiple_of((group * GROUP + member) * columns, columns) for member in range(GROUP)
        ]
        for chunk in range(chunks):
            lanes = slice(chunk * LANES, (chunk + 1) * LANES)
            for member, start in enumerate(starts):
                side[chunk, member, SIDE : SIDE + columns, :] = source[
                    pl.ds(start, columns), lanes
                ].astype(jnp.float32)
            for member, start in enumerate(starts):
                for target, offset, mask in (
                    (left, -distance, inside[0]),
                    (right, distance, inside[1]),
                ):
                    first = SIDE + offset
                    value = side[chunk, member, first : first + columns, :]
                    target[pl.ds(start, columns), lanes] = jnp.where(mask, value, 0.0).astype(
                        jnp.bfloat16
                    )
        return carry

    lax.fori_loop(0, rows // GROUP, step, 0)


def moved_columns(source, first, count, columns, distance, inside, planes):
    lefts, rights = [], []
    for chunk in range(source.shape[-1] // LANES):
        lanes = slice(chunk * LANES, (chunk + 1) * LANES)
        left, right = [], []
        for row in range(count):
            start = first + row * columns
            planes[chunk, row, SIDE : SIDE + columns, :] = source[
                start : start + columns, lanes
            ].astype(jnp.float32)
        for row in range(count):
            for offset, mask, result in ((-distance, inside[0], left), (distance, inside[1], right)):
                place = SIDE + offset
                value = planes[chunk, row, place : place + columns, :]
                result.append(jnp.where(mask, value, 0.0).astype(jnp.bfloat16))
        lefts.append(jnp.concatenate(left, axis=0))
        rights.append(jnp.concatenate(right, axis=0))
    return jnp.concatenate(lefts, axis=1), jnp.concatenate(rights, axis=1)


def forward_kernel(which, with_inner, first_tap, half, geometry, own, *refs):
    rows, columns, shards, parts, piece = geometry
    group = shards // 2
    steps = range(1 - half, group)
    others, refs = refs[:2], refs[2:]
    if not half:
        own_taps, refs = refs[: len(which) + with_inner], refs[len(which) + with_inner :]
    pieces, refs = refs[: 2 * len(steps)], refs[2 * len(steps) :]
    count = len(which)
    row_masks, refs = refs[:count], refs[count:]
    col_masks, refs = refs[:count], refs[count:]
    earlier = ()
    if half:
        earlier, refs = refs[: count + with_inner], refs[count + with_inner :]
        mains, refs = refs[:count], refs[count:]
        above, below, *refs = refs
    else:
        mains, refs = refs[:count], refs[count:]
    if with_inner:
        inner_out, *refs = refs
    weights_out, feat, planes, weights, *refs = refs
    if half:
        totals, refs = refs[:count], refs[count:]
        before, refs = refs[: count + with_inner], refs[count + with_inner :]
    else:
        totals = list(mains) + ([inner_out] if with_inner else [])
    sems, out_sem = refs
    depth, across, canvas = place()
    part = canvas % parts
    taps, channels, width = weights.shape
    pixels = rows * columns
    band = pixels // 2
    slice_rows = parts * piece
    upper = depth // group
    if half:
        upper = 1 - upper
    lanes = pl.ds(pl.multiple_of(upper * channels, channels), channels)
    feature_copies = copy_all(
        [
            (own.at[:, lanes], feat.at[pl.ds(pl.multiple_of(across * band, band), band)]),
            *[
                (array.at[:, lanes], feat.at[target])
                for array, target in zip(others, other_rows(across, band))
            ],
        ],
        sems,
    )
    span = pl.ds(first_tap, taps)
    copies = []
    if not half:
        start = pl.multiple_of((depth % group) * slice_rows, slice_rows)
        rows_of = pl.ds(start, slice_rows)
        for number, array in enumerate(own_taps):
            if number < count:
                target = weights.at[pl.ds(9 * number, 9), rows_of]
                copies.append((array.at[dilations.index(which[number])], target))
            else:
                copies.append((array, weights.at[9 * count, rows_of]))
    for number, step in enumerate(steps):
        origin = (depth % group) ^ step
        for index in range(parts):
            start = origin * slice_rows + (part ^ index) * piece
            copies.append(
                (
                    pieces[2 * number + index % 2].at[index // 2, span],
                    weights.at[:, pl.ds(pl.multiple_of(start, piece), piece)],
                )
            )
    weight_copies = copy_all(copies, sems.at[pl.ds(3, len(copies))])
    if half:
        earlier_copies = copy_all(
            list(zip(earlier, before)), sems.at[pl.ds(3 + len(copies), len(earlier))]
        )
    for copy in feature_copies:
        copy.wait()
    tile = pixels // TILES
    tile_rows = tile // columns
    keep = None
    for number, dilation in enumerate(which):
        shift = dilation * columns
        total = totals[number]
        inside = [col_masks[number][side] != 0 for side in range(2)]
        total[...] = jnp.zeros_like(total)
        for index in range(TILES):
            first = index * tile
            span = slice(first, first + tile)
            left, right = moved_columns(
                feat, first, tile_rows, columns, dilation, inside, planes.at[index % 2]
            )
            if number == 0 and index == 0:
                for copy in weight_copies:
                    copy.wait()
                keep = pltpu.make_async_copy(weights, weights_out, out_sem)
                keep.start()
            for row_tap in range(3):
                tap = 9 * number + 3 * row_tap
                product = jnp.dot(feat[span, :], weights[tap + 1], preferred_element_type=jnp.float32)
                product += jnp.dot(left, weights[tap], preferred_element_type=jnp.float32)
                product += jnp.dot(right, weights[tap + 2], preferred_element_type=jnp.float32)
                mask = spread_rows(
                    row_masks[number][row_tap, first // columns : (first + tile) // columns],
                    columns,
                    width,
                ).astype(jnp.float32)
                target = (2 - row_tap) * shift + first
                total[target : target + tile, :] += product * mask
    if half:
        for copy in earlier_copies:
            copy.wait()
    if with_inner:
        for first in range(0, pixels, tile):
            span = slice(first, first + tile)
            product = jnp.dot(feat[span, :], weights[9 * count], preferred_element_type=jnp.float32)
            if half:
                product += before[count][span, :]
            inner_out[span, :] = product
    if half:
        edge = 0
        for number, dilation in enumerate(which):
            shift = dilation * columns
            total, old = totals[number], before[number]
            end = shift + pixels
            above[edge : edge + shift, :] = (total[0:shift, :] + old[0:shift, :]).astype(
                jnp.bfloat16
            )
            mains[number][...] = total[shift:end, :] + old[shift:end, :]
            below[edge : edge + shift, :] = (
                total[end : end + shift, :] + old[end : end + shift, :]
            ).astype(jnp.bfloat16)
            edge += shift
    keep.wait()


def forward_branches(
    own, others, own_taps, pieces, row_masks, col_masks, earlier, which, with_inner, first_tap, geometry
):
    rows, columns, shards, parts, piece = geometry
    half = int(earlier is not None)
    pixels = rows * columns
    channels = own.shape[1] // 2
    width = pieces[0].shape[-1]
    count = len(which)
    taps = 9 * count + with_inner
    sums = [
        jax.ShapeDtypeStruct((pixels + 2 * dilation * columns, width), jnp.float32)
        for dilation in which
    ] + [jax.ShapeDtypeStruct((pixels, width), jnp.float32)] * with_inner
    out_shape = sums
    if half:
        edge = jax.ShapeDtypeStruct((sum(which) * columns, width), jnp.bfloat16)
        plain = jax.ShapeDtypeStruct((pixels, width), jnp.float32)
        out_shape = [plain] * count + [edge, edge] + [plain] * with_inner
    out_specs = [in_vmem] * len(out_shape) + [in_place]
    out_shape = out_shape + [jax.ShapeDtypeStruct((taps, channels, width), jnp.bfloat16)]
    earlier = list(earlier) if half else []
    own_taps = [] if half else [own_taps[0]] * count + [own_taps[1]] * with_inner
    inputs = [own, *others, *own_taps, *pieces]
    copies = 3 + len(own_taps) + (len(pieces) // 2) * parts + len(earlier)
    return pl.pallas_call(
        functools.partial(forward_kernel, which, with_inner, first_tap, half, geometry),
        in_specs=[in_place] * len(inputs) + [in_vmem] * (2 * count) + [in_place] * len(earlier),
        out_specs=out_specs,
        out_shape=out_shape,
        scratch_shapes=[
            pltpu.VMEM((pixels, channels), jnp.bfloat16),
            pltpu.VMEM(
                (2, channels // LANES, rows // TILES, columns + 2 * SIDE, LANES), jnp.float32
            ),
            pltpu.VMEM((taps, channels, width), jnp.bfloat16),
        ]
        + [pltpu.VMEM(array.shape, jnp.float32) for array in (sums[:count] + sums if half else [])]
        + [pltpu.SemaphoreType.DMA((copies,)), pltpu.SemaphoreType.DMA],
        compiler_params=pltpu.CompilerParams(vmem_limit_bytes=vmem_bytes),
        cost_estimate=pl.CostEstimate(
            flops=2 * taps * pixels * channels * width,
            bytes_accessed=2 * pixels * channels + 4 * taps * channels * width,
            transcendentals=0,
        ),
        name=f"forward_{half}_" + "_".join(str(dilation) for dilation in which),
    )(*inputs, *row_masks, *col_masks, *earlier)


def load_gradient(rows, columns, dilation, refs, target, sems):
    depth, across, canvas = place()
    own, other, above, below = refs
    band = rows * columns // 2
    shift = dilation * columns
    return copy_all(
        [
            (own, target.at[pl.ds(pl.multiple_of(shift + across * band, columns), band)]),
            (other, target.at[pl.ds(pl.multiple_of(shift + (1 - across) * band, columns), band)]),
            (above, target.at[pl.ds(0, shift)]),
            (below, target.at[pl.ds(shift + 2 * band, shift)]),
        ],
        sems,
    )


def turned(index, count):
    result = 0
    for bit in bits_of(count):
        result = 2 * result + (index // bit) % 2
    return result


def weight_kernel(dilation, with_inner, geometry, *refs):
    rows, columns, shards, parts, piece = geometry
    own_features, refs = refs[:3], refs[3:]
    their_features, refs = refs[:4], refs[4:]
    gradient, refs = refs[:4], refs[4:]
    if with_inner:
        inner, refs = refs[:2], refs[2:]
    theirs, refs = refs[0], refs[1:]
    row_masks, refs = refs[:2], refs[2:]
    col_masks, refs = refs[:2], refs[2:]
    keep, send, feat, side, moved, result, *refs = refs
    if with_inner:
        straight, *refs = refs
    sems, out_sems = refs
    depth, across, canvas = place()
    low, upper = canvas % 2, (canvas // 2) % 2
    pixels = rows * columns
    band = pixels // 2
    shift = dilation * columns
    width = moved.shape[-1]
    lanes = pl.ds(pl.multiple_of(upper * width, width), width)
    starts = [across * band, (1 - across) * band]

    def spans(base, pieces):
        size = band // pieces
        return [
            pl.ds(pl.multiple_of(base + start + number * size, size), size)
            for start in starts
            for number in range(pieces)
        ]

    first = []
    ends = [(0, shift), (shift + pixels, shift)]
    for number in range(2):
        targets = [pl.ds(pl.multiple_of(shift + start, columns), band) for start in starts]
        targets += [pl.ds(*end) for end in ends]
        if number == 0:
            sources = [array.at[:, lanes] for array in gradient]
        else:
            places = [(0, band), (band, band), (pixels, shift), (pixels + shift, shift)]
            sources = [theirs.at[pl.ds(*where)] for where in places]
        first += [
            (source, moved.at[1, number, target]) for source, target in zip(sources, targets)
        ]
    first = copy_all(first, sems)
    second = list(zip(own_features[:1], [feat.at[spans(0, 1)[0]]]))
    second += list(zip(own_features[1:], [feat.at[span] for span in spans(0, 2)[2:]]))
    second += list(zip(their_features, [feat.at[span] for span in spans(pixels, 2)]))
    if with_inner:
        second += [
            (array.at[:, lanes], straight.at[span]) for array, span in zip(inner, spans(0, 1))
        ]
        second += [
            (theirs.at[pl.ds(pixels + 2 * shift + number * band, band)], straight.at[span])
            for number, span in enumerate(spans(pixels, 1))
        ]
    second = copy_all(second, sems.at[pl.ds(8, len(second))])
    for copy in first:
        copy.wait()
    for number in range(2):
        shift_columns(
            moved.at[1, number],
            rows + 2 * dilation,
            columns,
            dilation,
            (col_masks[number][0], col_masks[number][1]),
            side,
            moved.at[2, number],
            moved.at[0, number],
        )
    for copy in second:
        copy.wait()

    def factor(tap):
        if tap == 9:
            return straight[...]
        row_tap, col_tap = divmod(tap, 3)
        start = (2 - row_tap) * shift
        return jnp.concatenate(
            [
                moved[col_tap, number, start : start + pixels, :]
                * spread_rows(row_masks[number][row_tap], columns, width)
                for number in range(2)
            ],
            axis=0,
        )

    half = parts * piece // 2
    taps = 9 + with_inner
    pending = [[], []]
    for turn, tap in enumerate(range(0, taps, TAPS)):
        slot = turn % 2
        pair = list(range(tap, min(tap + TAPS, taps)))
        product = lax.dot_general(
            feat[...],
            jnp.concatenate([factor(member) for member in pair], axis=1),
            (((0,), (0,)), ((), ())),
            preferred_element_type=jnp.float32,
        )
        for copy in pending[slot]:
            copy.wait()
        result[slot, :, 0 : len(pair) * width] = product.astype(jnp.bfloat16)
        copies = []
        for step in range(shards):
            base = (depth ^ step) * 2 * half
            for target, offset in ((keep, low), (send, 1 - low)):
                rows_of = pl.ds(pl.multiple_of(base + offset * half, half), half)
                for number, member in enumerate(pair):
                    part_of = result.at[slot, rows_of, pl.ds(number * width, width)]
                    copies.append((part_of, target.at[turned(step, shards), member]))
        pending[slot] = copy_all(copies, out_sems.at[slot])
    for copies in pending:
        for copy in copies:
            copy.wait()


def weight_branch(features, gradient, inner, theirs, row_masks, col_masks, dilation, geometry):
    rows, columns, shards, parts, piece = geometry
    pixels = rows * columns
    channels = features[0].shape[1]
    width = theirs.shape[1]
    with_inner = int(inner is not None)
    taps = 9 + with_inner
    extended = pixels + 2 * dilation * columns
    part_shape = jax.ShapeDtypeStruct((shards, taps, parts * piece // 2, width), jnp.bfloat16)
    arrays = [*features, *gradient] + (list(inner) if with_inner else []) + [theirs]
    return pl.pallas_call(
        functools.partial(weight_kernel, dilation, with_inner, geometry),
        in_specs=[in_place] * len(arrays) + [in_vmem] * 4,
        out_specs=[in_place, in_place],
        out_shape=[part_shape, part_shape],
        scratch_shapes=[
            pltpu.VMEM((2 * pixels, channels), jnp.bfloat16),
            pltpu.VMEM((width // LANES, GROUP, columns + 2 * SIDE, LANES), jnp.float32),
            pltpu.VMEM((3, 2, extended, width), jnp.bfloat16),
            pltpu.VMEM((2, channels, TAPS * width), jnp.bfloat16),
        ]
        + [pltpu.VMEM((2 * pixels, width), jnp.bfloat16)] * with_inner
        + [
            pltpu.SemaphoreType.DMA((15 + 4 * with_inner,)),
            pltpu.SemaphoreType.DMA((2, 2 * TAPS * shards)),
        ],
        compiler_params=pltpu.CompilerParams(vmem_limit_bytes=vmem_bytes),
        cost_estimate=pl.CostEstimate(
            flops=4 * taps * pixels * channels * width,
            bytes_accessed=4 * pixels * channels + 4 * taps * channels * width,
            transcendentals=0,
        ),
        name=f"weight_{dilation}",
    )(*arrays, *row_masks, *col_masks)


def feature_kernel(geometry, layout, *refs):
    rows, columns, shards, parts, piece = geometry
    branches = len(dilations)
    gradients = [refs[4 * branch : 4 * branch + 4] for branch in range(branches)]
    refs = refs[4 * branches :]
    inner, refs = refs[:2], refs[2:]
    sources, refs = refs[: len(layout)], refs[len(layout) :]
    row_masks, refs = refs[:branches], refs[branches:]
    col_masks, refs = refs[:branches], refs[branches:]
    keep, send, side, straight, moved, result, *refs = refs
    weights, refs = refs[: len(layout)], refs[len(layout) :]
    sems, weight_sems = refs
    depth, across, canvas = place()
    pixels = rows * columns
    band = pixels // 2
    channels = result.shape[1]
    width = straight.shape[1]
    taps_of = {}
    for number, names in enumerate(layout):
        for index, name in enumerate(names):
            taps_of[name] = (number, 9 * index)
    offsets = [pl.multiple_of(across * band, band), pl.multiple_of((1 - across) * band, band)]

    def load_weights(name):
        number, base = taps_of[name]
        span = pl.ds(base, 9 if name else 1)
        order = (0,) + dilations
        return copy_all(
            [(sources[number].at[span], weights[number].at[span])],
            weight_sems.at[pl.ds(order.index(name), 1)],
        )

    waits = copy_all(
        [
            (inner[0], straight.at[pl.ds(offsets[0], band)]),
            (inner[1], straight.at[pl.ds(offsets[1], band)]),
        ],
        sems.at[pl.ds(4 * branches, 2)],
    )
    loads = {0: load_weights(0)}
    arrivals = []
    for branch, dilation in enumerate(dilations):
        arrivals.append(
            load_gradient(
                rows,
                columns,
                dilation,
                gradients[branch],
                moved.at[branch % 2, 1],
                sems.at[pl.ds(4 * branch, 4)],
            )
            if branch < 2
            else None
        )
        loads[dilation] = load_weights(dilation)
    tile = pixels // 4
    for copy in waits + loads[0]:
        copy.wait()
    for first in range(0, pixels, tile):
        span = slice(first, first + tile)
        number, base = taps_of[0]
        result[span, :] = lax.dot_general(
            straight[span, :],
            weights[number][base],
            (((1,), (1,)), ((), ())),
            preferred_element_type=jnp.float32,
        )
    for branch, dilation in enumerate(dilations):
        slot = branch % 2
        shift = dilation * columns
        for copy in arrivals[branch]:
            copy.wait()
        shift_columns(
            moved.at[slot, 1],
            rows + 2 * dilation,
            columns,
            dilation,
            (col_masks[branch][0], col_masks[branch][1]),
            side,
            moved.at[slot, 2],
            moved.at[slot, 0],
        )
        for copy in loads[dilation]:
            copy.wait()
        number, base = taps_of[dilation]
        for first in range(0, pixels, tile):
            span = slice(first, first + tile)
            product = jnp.zeros((tile, channels), jnp.float32)
            for row_tap in range(3):
                mask = spread_rows(
                    row_masks[branch][row_tap, first // columns : (first + tile) // columns],
                    columns,
                    width,
                )
                start = (2 - row_tap) * shift + first
                for col_tap in range(3):
                    product += lax.dot_general(
                        moved[slot, col_tap, start : start + tile, :] * mask,
                        weights[number][base + 3 * row_tap + col_tap],
                        (((1,), (1,)), ((), ())),
                        preferred_element_type=jnp.float32,
                    )
            result[span, :] += product
        if branch + 2 < branches:
            arrivals[branch + 2] = load_gradient(
                rows,
                columns,
                dilations[branch + 2],
                gradients[branch + 2],
                moved.at[slot, 1],
                sems.at[pl.ds(4 * (branch + 2), 4)],
            )
    keep[...] = result[pl.ds(pl.multiple_of(across * band, band), band), :]
    send[...] = result[pl.ds(pl.multiple_of((1 - across) * band, band), band), :].astype(
        jnp.bfloat16
    )


def feature_branches(gradients, inner, row_masks, col_masks, weights, layout, geometry):
    rows, columns, shards, parts, piece = geometry
    pixels = rows * columns
    band = pixels // 2
    channels, width = weights[0].shape[1:]
    arrays = [array for gradient in gradients for array in gradient] + list(inner)
    taps = sum(array.shape[0] for array in weights)
    extended = pixels + 2 * max(dilations) * columns
    return pl.pallas_call(
        functools.partial(feature_kernel, geometry, layout),
        in_specs=[in_place] * (len(arrays) + len(weights))
        + [in_vmem] * (len(row_masks) + len(col_masks)),
        out_specs=[in_vmem] * 2,
        out_shape=[
            jax.ShapeDtypeStruct((band, channels), jnp.float32),
            jax.ShapeDtypeStruct((band, channels), jnp.bfloat16),
        ],
        scratch_shapes=[
            pltpu.VMEM((width // LANES, GROUP, columns + 2 * SIDE, LANES), jnp.float32),
            pltpu.VMEM((pixels, width), jnp.bfloat16),
            pltpu.VMEM((2, 3, extended, width), jnp.bfloat16),
            pltpu.VMEM((pixels, channels), jnp.float32),
        ]
        + [pltpu.VMEM(array.shape, jnp.bfloat16) for array in weights]
        + [
            pltpu.SemaphoreType.DMA((len(arrays),)),
            pltpu.SemaphoreType.DMA((1 + len(dilations),)),
        ],
        compiler_params=pltpu.CompilerParams(vmem_limit_bytes=vmem_bytes),
        cost_estimate=pl.CostEstimate(
            flops=2 * taps * pixels * channels * width,
            bytes_accessed=6 * band * channels + 2 * taps * channels * width,
            transcendentals=0,
        ),
        name="feature_gradient",
    )(*arrays, *weights, *row_masks, *col_masks)


def interp_matrix(out_count, in_count, before):
    free = np.zeros((out_count, in_count), np.float32)
    edges = np.zeros((out_count, in_count), np.float32)
    for row in range(out_count):
        for offset, coeffs in ((-1, prev_weights), (0, self_weights), (1, next_weights)):
            place = row // 4 + offset + before
            if 0 <= place < in_count:
                free[row, place] += coeffs[row % 4]
            edges[row, min(max(place, 0), in_count - 1)] += coeffs[row % 4]
    return free, edges


def silu_slope(values):
    logistic = jax.nn.sigmoid(values)
    return logistic * (1.0 + values * (1.0 - logistic))


def normalize(values, sum_rows, total_count, scale_vec, shift_vec):
    average = sum_rows[0] / total_count
    spread_of = sum_rows[1] / total_count - average * average
    inverse = lax.rsqrt(spread_of + epsilon)
    centered = (values - average) * inverse
    return (centered, inverse, scale_vec * centered + shift_vec)


def input_grad(slope, centered, inverse, scale_vec, totals, total_count, weight_map):
    return (
        scale_vec
        * inverse
        * (slope - weight_map * (totals[0] + centered * totals[1]) / total_count)
    )


def moments_of(values, weight_map):
    weighted = weight_map * values
    return [jnp.sum(weighted, axis=0), jnp.sum(weighted * values, axis=0)]


def per_device(
    features,
    segment_map,
    pixel_mask,
    inner_weight,
    atrous_weight,
    pool_weight,
    proj_weight,
    norm_gains,
    norm_shifts,
    cotangent,
):
    highest = lax.Precision.HIGHEST
    row_count = lax.axis_size("rows")
    canvas_count = lax.axis_size("canvas") * features.shape[0]
    band_rows, columns, channels = features.shape[1:]
    branch_width = norm_gains.shape[1]
    canvas_rows = band_rows * row_count
    image_count = COL_IMAGES * (canvas_rows // 36)
    row_index = lax.axis_index("rows")
    canvas_index = lax.axis_index("canvas")
    shards = row_count // 2
    depth = row_index // 2
    first_band = row_index % 2 == 0
    row_first = row_index * band_rows
    rows = 2 * band_rows
    band = band_rows * columns
    pixels = rows * columns
    slice_rows = channels // row_count
    parts = min(lax.axis_size("canvas"), max(slice_rows // 16, 1))
    piece = slice_rows // parts
    part = canvas_index % parts
    geometry = (rows, columns, shards, parts, piece)

    flat_mask = pixel_mask.reshape(band, 1)
    valid_mask = flat_mask.astype(jnp.float32)
    segments = segment_map.reshape(band)
    places = jnp.arange(columns)
    col_ids = segment_map[0, 0, :] % COL_IMAGES

    def col_checks(col_ids):
        masks = {}
        for dilation in dilations:
            table = []
            for offset in (-dilation, dilation):
                moved = places + offset
                inside = (moved >= 0) & (moved < columns)
                table.append(inside & (jnp.roll(col_ids, -offset) == col_ids))
            table = jnp.stack(table).astype(jnp.float32)
            masks[dilation] = jnp.broadcast_to(table[:, :, None], (2, columns, LANES))
        return masks

    col_masks = col_checks(col_ids)

    taps = lax.dynamic_slice_in_dim(
        atrous_weight.reshape(9 * len(dilations), slice_rows, branch_width),
        part * piece,
        piece,
        axis=1,
    )
    inner_taps = lax.dynamic_slice_in_dim(inner_weight, part * piece, piece, axis=0)[None]
    quarter = jnp.concatenate(
        [
            item
            for dilation in (18, 0, 12, 6)
            for item in (
                [taps[9 * dilations.index(dilation) :][:9]] if dilation else [inner_taps]
            )
        ],
        axis=0,
    )
    own_taps = (
        atrous_weight.reshape(len(dilations), 9, slice_rows, branch_width),
        inner_weight,
    )
    row_ids = segment_map[0, :, 0] // COL_IMAGES + 1
    both_ids = halves(first_band, row_ids, swap(row_ids, "rows", 1))
    low_mask = flat_mask.astype(jnp.bfloat16)
    flat_features = features.reshape(band, channels)
    slices = [flat_features[:, i * slice_rows : (i + 1) * slice_rows] for i in range(row_count)]
    even = jnp.concatenate(slices[0::2], axis=1)
    odd = jnp.concatenate(slices[1::2], axis=1)
    middle = band // 2
    feat_send = jnp.where(first_band, odd, even) * low_mask
    feat_own, quarter_later, *feat_parts = tie(
        jnp.where(first_band, even, odd) * low_mask,
        quarter,
        feat_send[:middle],
        feat_send[middle:],
    )
    group = shards // 2

    def along(start, bits):
        found = [start]
        for bit in bits:
            found = found + [swap(item, "rows", 2 * bit) for item in found]
        return found

    def between(item):
        chain = [item]
        for bit in bits_of(parts)[1:]:
            chain = chain + [swap(other, "canvas", bit) for other in chain]
        return chain

    def from_partner(chain):
        stacked = jnp.stack(chain)
        return [stacked, swap(stacked, "canvas", 1)]

    def sum_step(values, bit):
        return values + swap(values, "rows", bit)

    def gather_step(values, bit):
        other = swap(values, "rows", bit)
        both = jnp.where(
            (row_index & bit) == 0,
            jnp.stack([values, other], axis=1),
            jnp.stack([other, values], axis=1),
        )
        return both.reshape((2 * values.shape[0],) + values.shape[1:])

    rounds = bits_of(row_count)
    near = along(quarter, bits_of(group))[1:]
    feat_first = swap(feat_parts[0], "rows", 1)
    reach = max(dilations)

    def row_checks(all_ids, outside):
        masks = {}
        for dilation in dilations:
            checks = []
            for row_tap in range(3):
                start = reach - (row_tap - 1) * dilation
                target = all_ids[start : start + rows]
                same = target == all_ids[reach : reach + rows]
                checks.append(jnp.where(target == 0, outside, same))
            table = jnp.stack(checks).astype(jnp.bfloat16)
            masks[dilation] = jnp.broadcast_to(table[:, :, None, None], (3, rows, TILE, LANES))
        return masks

    near_masks = row_checks(jnp.pad(both_ids, (reach, reach)), True)
    col_matrix = jnp.asarray(interp_matrix(4 * columns, columns, 0)[1])
    col_grad = jnp.einsum(
        "pw,opb->owb",
        col_matrix.astype(jnp.bfloat16),
        cotangent[0],
        preferred_element_type=jnp.float32,
    )
    near, both_ids, col_grad, near_masks = tie(near, both_ids, col_grad, near_masks)

    far_first = swap(quarter_later, "rows", 2 * group)
    near_chains = [between(item) for item in near]
    feat_second = swap(feat_parts[1], "rows", 1)
    members = (segments[:, None] == jnp.arange(image_count, dtype=jnp.int32)).astype(jnp.float32)
    member_low = members.astype(jnp.bfloat16)
    seg_sums = jnp.einsum(
        "ps,pc->sc", member_low, flat_features * low_mask, preferred_element_type=jnp.float32
    )
    seg_counts = jnp.sum(members * valid_mask, axis=0)
    seg_all = jnp.concatenate(
        [seg_sums, jnp.broadcast_to(seg_counts[:, None], (image_count, LANES))], axis=1
    )
    far_first, near_chains, feat_first, feat_second, seg_all, proj_full = tie(
        far_first, near_chains, feat_first, feat_second, seg_all, proj_weight[None]
    )

    feat_others = (feat_first, feat_second)
    far = along(far_first, bits_of(group))
    far_chains = [between(far_first)]
    near_pieces = [item for chain in near_chains for item in from_partner(chain)]
    seg_all = sum_step(seg_all, rounds[0])
    proj_full = gather_step(proj_full, rounds[0])
    first_taps = {18: 0, 12: 10, 6: 19}

    def forward(which, pieces, earlier=None):
        return forward_branches(
            feat_own,
            feat_others,
            own_taps,
            pieces,
            [near_masks[dilation] for dilation in which],
            [col_masks[dilation] for dilation in which],
            earlier,
            which,
            int(which == (18,)),
            first_taps[which[0]],
            geometry,
        )

    total_18, total_inner, weights_00 = forward((18,), near_pieces)
    (far, far_chains, seg_all, proj_full, total_18, total_inner, near_pieces) = tie(
        far, far_chains, seg_all, proj_full, total_18, total_inner, near_pieces
    )

    far_chains = far_chains + [between(item) for item in far[1:]]
    far_pieces = from_partner(far_chains[0])
    total_12, total_6, weights_01 = forward((12, 6), near_pieces)
    seg_all = sum_step(seg_all, rounds[1])
    proj_full = gather_step(proj_full, rounds[-1])
    far_chains, far_pieces, total_12, total_6, seg_all, proj_full, both_ids, col_grad = tie(
        far_chains, far_pieces, total_12, total_6, seg_all, proj_full, both_ids, col_grad
    )

    far_pieces = far_pieces + [item for chain in far_chains[1:] for item in from_partner(chain)]
    id_above, id_below = trade(both_ids[:reach], both_ids[rows - reach :], 2)
    all_ids = jnp.concatenate([id_above, both_ids, id_below])
    for bit in rounds[2:]:
        seg_all = sum_step(seg_all, bit)
    for bit in rounds[-2:0:-1]:
        proj_full = gather_step(proj_full, bit)
    proj_full = proj_full.reshape((2, shards) + proj_full.shape[1:]).swapaxes(0, 1)
    proj_full = proj_full.reshape(-1, branch_width)
    grad_above, grad_below = trade(col_grad[:2], col_grad[4 * band_rows - 2 :], 1)
    grad_ext = jnp.concatenate([grad_above, col_grad, grad_below], axis=0)
    their_first = swap(feat_first, "canvas", 2)
    far_pieces, seg_all, proj_full, all_ids, grad_ext, their_first = tie(
        far_pieces, seg_all, proj_full, all_ids, grad_ext, their_first
    )
    their_ids = swap(jnp.concatenate([all_ids, col_ids]), "canvas", 2)
    their_second = swap(tie(feat_second, all_ids)[0], "canvas", 2)

    def to_partner(partials):
        sent = [
            jnp.where(first_band, partial[band:], partial[:band]).astype(jnp.bfloat16)
            for partial in partials
        ]
        return swap(jnp.concatenate(sent, axis=1), "rows", 1)

    def complete(partial, back):
        mine = jnp.where(first_band, partial[:band], partial[band:])
        return mine + back.astype(jnp.float32)

    def beyond_bands(dilation, main, above, below):
        shift = dilation * columns
        here = all_ids[reach : reach + rows]
        mask = here[:dilation] == all_ids[reach - dilation : reach]
        mask = jnp.broadcast_to(mask[:, None], (dilation, columns)).reshape(shift, 1)
        below = below.astype(jnp.float32) * mask.astype(jnp.float32)
        mask = here[rows - dilation :] == all_ids[reach + rows : reach + rows + dilation]
        mask = jnp.broadcast_to(mask[:, None], (dilation, columns)).reshape(shift, 1)
        above = above.astype(jnp.float32) * mask.astype(jnp.float32)
        return jnp.concatenate(
            [
                main[:shift] + below,
                main[shift : pixels - shift],
                main[pixels - shift :] + above,
            ],
            axis=0,
        )

    main_18, above_18, below_18, main_inner, weights_10 = forward(
        (18,), far_pieces, [total_18, total_inner]
    )
    far_pieces, main_18, above_18, below_18, main_inner, seg_all = tie(
        far_pieces, main_18, above_18, below_18, main_inner, seg_all
    )
    back_inner = to_partner([main_inner])
    their_own = [swap(tie(feat_own[:middle], main_18)[0], "canvas", 2)]
    below_18, above_18 = trade(above_18, below_18, 2)
    main_12, above_12, below_12, weights_11 = forward((12,), far_pieces, [total_12])
    total_counts = seg_all[:, channels : channels + 1]
    pooled = lax.dynamic_slice_in_dim(seg_all, row_index * slice_rows, slice_rows, axis=1)
    pooled = pooled / total_counts
    pool_matrix = pool_weight.astype(jnp.float32)
    pool_part = jnp.dot(pooled, pool_matrix, precision=highest)
    (
        far_pieces,
        main_12,
        above_12,
        below_12,
        back_inner,
        above_18,
        below_18,
        pool_part,
        their_ids,
        their_second,
    ) = tie(
        far_pieces,
        main_12,
        above_12,
        below_12,
        back_inner,
        above_18,
        below_18,
        pool_part,
        their_ids,
        their_second,
    )
    their_own.append(swap(tie(feat_own[middle:], main_12)[0], "canvas", 2))
    row_masks = row_checks(all_ids, False)
    reached = all_ids.shape[0]
    their_row_masks = row_checks(their_ids[:reached], False)
    their_col_masks = col_checks(their_ids[reached:])
    main_18 = beyond_bands(18, main_18, above_18, below_18)
    back_18 = to_partner([main_18])
    below_12, above_12 = trade(above_12, below_12, 2)
    main_6, above_6, below_6, weights_12 = forward((6,), far_pieces, [total_6])
    free, edges = interp_matrix(4 * band_rows, band_rows, 0)
    beyond_ends = interp_matrix(4 * band_rows + 8, band_rows + 2, 0)[0][2:-2, 1:-1]
    change = np.pad(edges - free, ((2, 2), (0, 0)))
    halfway = 2 * band_rows + 2
    at_top = np.where(np.arange(4 * band_rows + 4)[:, None] < halfway, change, 0.0)
    back_matrix = (
        jnp.asarray(beyond_ends)
        + jnp.where(row_index == 0, 1.0, 0.0) * jnp.asarray(at_top, jnp.float32)
        + jnp.where(row_index == row_count - 1, 1.0, 0.0)
        * jnp.asarray(change - at_top, jnp.float32)
    )
    back_18, above_12, below_12, main_6, above_6, below_6, grad_ext, row_masks, their_own[0] = tie(
        back_18, above_12, below_12, main_6, above_6, below_6, grad_ext, row_masks, their_own[0]
    )
    main_12 = beyond_bands(12, main_12, above_12, below_12)
    back_12 = to_partner([main_12])
    below_6, above_6 = trade(above_6, below_6, 2)
    act_grad = jnp.einsum("or,owb->rwb", back_matrix, grad_ext, precision=highest)
    act_grad = act_grad.reshape(band, branch_width)
    back_12, above_6, below_6, act_grad = tie(back_12, above_6, below_6, act_grad)
    main_6 = beyond_bands(6, main_6, above_6, below_6)
    back_6 = to_partner([main_6])
    back_6, their_own[1], their_row_masks = tie(back_6, their_own[1], their_row_masks)
    all_features = (feat_own, feat_first, feat_second, *their_own, their_first, their_second)
    conv_outs = [
        complete(main_inner, back_inner),
        complete(main_6, back_6),
        complete(main_12, back_12),
        complete(main_18, back_18),
    ]
    weights_full = [[weights_00, weights_01], [weights_10, weights_11, weights_12]]
    layouts = (((18, 0), (12, 6)), ((18, 0), (12,), (6,)))

    rows_of = []
    for conv_out in conv_outs:
        rows_of += moments_of(conv_out, valid_mask)
    rows_of.append(jnp.broadcast_to(jnp.sum(valid_mask), (branch_width,)))
    sums = sum_over(jnp.concatenate([jnp.stack(rows_of), pool_part]), "rows")
    pool_out = sums[9:]
    sums = sum_over(
        jnp.concatenate(
            [
                sums[:8],
                jnp.sum(pool_out, axis=0, keepdims=True),
                jnp.sum(pool_out * pool_out, axis=0, keepdims=True),
                sums[8:9],
            ]
        ),
        "canvas",
    )
    pixel_total = sums[10]
    entries = float(canvas_count * image_count)
    normals = [
        normalize(
            conv_out,
            sums[2 * branch : 2 * branch + 2],
            pixel_total,
            norm_gains[branch],
            norm_shifts[branch],
        )
        for branch, conv_out in enumerate(conv_outs)
    ]
    pool_norm = normalize(pool_out, sums[8:10], entries, norm_gains[4], norm_shifts[4])
    pool_act = jax.nn.silu(pool_norm[2]).astype(jnp.bfloat16)
    pool_map = jnp.dot(member_low, pool_act, preferred_element_type=jnp.float32)
    concat_act = jnp.concatenate(
        [jax.nn.silu(item[2]).astype(jnp.bfloat16) for item in normals]
        + [pool_map.astype(jnp.bfloat16)],
        axis=-1,
    )
    proj_out = jnp.dot(concat_act, proj_full, preferred_element_type=jnp.float32)
    proj_totals = sum_over(
        sum_over(jnp.stack(moments_of(proj_out, valid_mask)), "rows"), "canvas"
    )
    proj_norm = normalize(proj_out, proj_totals, pixel_total, norm_gains[5], norm_shifts[5])
    proj_act = jax.nn.silu(proj_norm[2]).astype(jnp.bfloat16)

    act_rows = proj_act.reshape(band_rows, columns, branch_width)
    act_above, act_below = trade(act_rows[:1], act_rows[band_rows - 1 :], 1)
    ext_act = jnp.concatenate(
        [
            jnp.where(row_index == 0, act_rows[:1], act_above),
            act_rows,
            jnp.where(row_index == row_count - 1, act_rows[band_rows - 1 :], act_below),
        ],
        axis=0,
    )

    proj_slope = act_grad * silu_slope(proj_norm[2])
    proj_local = jnp.stack(
        [jnp.sum(proj_slope, axis=0), jnp.sum(proj_slope * proj_norm[0], axis=0)]
    )
    proj_grad_totals = sum_over(sum_over(proj_local, "rows"), "canvas")
    proj_grad = input_grad(
        proj_slope,
        proj_norm[0],
        proj_norm[1],
        norm_gains[5],
        proj_grad_totals,
        pixel_total,
        valid_mask,
    ).astype(jnp.bfloat16)
    joined_grad = lax.dot_general(
        proj_grad, proj_full, (((1,), (1,)), ((), ())), preferred_element_type=jnp.float32
    )
    slopes = [
        joined_grad[:, branch * branch_width : (branch + 1) * branch_width]
        * silu_slope(normals[branch][2])
        for branch in range(4)
    ]
    rows_of = []
    for branch, slope in enumerate(slopes):
        rows_of += [jnp.sum(slope, axis=0), jnp.sum(slope * normals[branch][0], axis=0)]
    seg_grads = lax.dot_general(
        members, joined_grad[:, 4 * branch_width :], (((0,), (0,)), ((), ())), precision=highest
    )
    pool_terms = seg_grads * silu_slope(pool_norm[2])
    rows_of += [jnp.sum(pool_terms, axis=0), jnp.sum(pool_terms * pool_norm[0], axis=0)]
    sums = sum_over(jnp.concatenate([jnp.stack(rows_of), seg_grads], axis=0), "rows")
    seg_grads = sums[10:]
    sums = sum_over(sums[:10], "canvas")
    branch_totals = [sums[2 * branch : 2 * branch + 2] for branch in range(5)]
    conv_grads = [
        input_grad(
            slopes[branch],
            normals[branch][0],
            normals[branch][1],
            norm_gains[branch],
            branch_totals[branch],
            pixel_total,
            valid_mask,
        ).astype(jnp.bfloat16)
        for branch in range(4)
    ]

    pool_grad = input_grad(
        seg_grads * silu_slope(pool_norm[2]),
        pool_norm[0],
        pool_norm[1],
        norm_gains[4],
        branch_totals[4],
        entries,
        1.0,
    )
    pooled_grad = (
        lax.dot_general(pool_matrix, pool_grad, (((1,), (1,)), ((), ())), precision=highest)
        / total_counts[:, 0]
    )
    grad_pool = lax.dot_general(
        pooled, pool_grad, (((0,), (0,)), ((), ())), precision=highest
    )
    grad_proj = lax.dot_general(
        concat_act, proj_grad, (((0,), (0,)), ((), ())), preferred_element_type=jnp.float32
    )

    grad_proj = grad_proj.reshape((row_count,) + (grad_proj.shape[0] // row_count, branch_width))

    def scatter_step(values, bit):
        values = values.reshape((values.shape[0] // 2, 2) + values.shape[1:])
        low, high = values[:, 0], values[:, 1]
        mine = (row_index & bit) == 0
        sent = jnp.where(mine, high, low).astype(jnp.bfloat16)
        return jnp.where(mine, low, high) + swap(sent, "rows", bit).astype(jnp.float32)

    def beyond(branch, other):
        grad = conv_grads[branch + 1]
        shift = dilations[branch] * columns
        top = jnp.where(first_band, grad[:shift], other[:shift])
        bottom = jnp.where(first_band, other[band - shift :], grad[band - shift :])
        return (grad, other, *trade(top, bottom, 2))

    def pair_sum(kept, got):
        return kept.astype(jnp.float32) + got.astype(jnp.float32)

    def halve(kept, got, axis, bit):
        size = kept.shape[0] // 2
        sent = pair_sum(kept[size:], got[size:]).astype(jnp.bfloat16)
        return pair_sum(kept[:size], got[:size]), swap(sent, axis, bit)

    def weights_of(branch, theirs, inner=None):
        dilation = dilations[branch]
        return weight_branch(
            all_features,
            gradients[branch],
            inner,
            theirs,
            [row_masks[dilation], their_row_masks[dilation]],
            [col_masks[dilation], their_col_masks[dilation]],
            dilation,
            geometry,
        )

    half_width = branch_width // 2
    upper = (canvas_index // 2) % 2 == 1

    def for_partner(arrays):
        return jnp.concatenate(
            [jnp.where(upper, array[:, :half_width], array[:, half_width:]) for array in arrays]
        )

    along_rows = [("rows", 2 * bit) for bit in bits_of(shards)]

    def finish(kept, got):
        total = pair_sum(kept, got)[0]
        for bit in bits_of(lax.axis_size("canvas"))[2:]:
            total = total + swap(total, "canvas", bit)
        return lax.optimization_barrier(total.astype(jnp.bfloat16))

    def other_channels(block):
        other = swap(block, "canvas", 2)
        return jnp.where(
            upper,
            jnp.concatenate([other, block], axis=2),
            jnp.concatenate([block, other], axis=2),
        )

    def other_rows_of(block):
        other = swap(block, "canvas", 1)
        return jnp.where(
            canvas_index % 2 == 0,
            jnp.concatenate([block, other], axis=1),
            jnp.concatenate([other, block], axis=1),
        )

    def features_of(half):
        return feature_branches(
            gradients,
            inner_grads,
            [row_masks[dilation] for dilation in dilations],
            [col_masks[dilation] for dilation in dilations],
            weights_full[half],
            layouts[half],
            geometry,
        )

    other = swap(conv_grads[1], "rows", 1)
    other, ext_act, *conv_grads = tie(other, ext_act, *conv_grads)
    row_matrix = jnp.asarray(interp_matrix(4 * band_rows, band_rows + 2, 1)[0], jnp.bfloat16)
    rows_up = jnp.einsum("or,rwb->owb", row_matrix, ext_act, preferred_element_type=jnp.float32)
    high = rows_up.astype(jnp.bfloat16)
    low = (rows_up - high.astype(jnp.float32)).astype(jnp.bfloat16)
    upsampled = jnp.einsum(
        "pw,owb->opb",
        jnp.concatenate([col_matrix, col_matrix], axis=1).astype(jnp.bfloat16),
        jnp.concatenate([high, low], axis=1),
        preferred_element_type=jnp.float32,
    ).astype(jnp.bfloat16)
    gradients = [beyond(0, other)]
    other = swap(conv_grads[2], "rows", 1)
    gradients, other, conv_grads, upsampled = tie(gradients, other, conv_grads, upsampled)
    theirs_6 = swap(for_partner(gradients[0]), "canvas", 2)
    gradients.append(beyond(1, other))
    other = swap(jnp.concatenate([conv_grads[3], conv_grads[0]], axis=1), "rows", 1)
    canvas_bits = bits_of(lax.axis_size("canvas"))
    grad_pool = grad_pool + swap(grad_pool, "canvas", canvas_bits[0])
    gradients, theirs_6, other, grad_proj, pooled_grad, grad_pool = tie(
        gradients, theirs_6, other, grad_proj, pooled_grad, grad_pool
    )
    theirs_12 = swap(for_partner(gradients[1]), "canvas", 2)
    gradients.append(beyond(2, other[:, :branch_width]))
    inner_grads = (conv_grads[0], other[:, branch_width:])
    kept_6, sent_6 = weights_of(0, theirs_6)
    grad_proj = scatter_step(grad_proj, rounds[0])
    pooled_grad = gather_step(pooled_grad[None], rounds[-1])
    (
        gradients,
        inner_grads,
        theirs_12,
        kept_6,
        sent_6,
        grad_proj,
        pooled_grad,
        grad_pool,
    ) = tie(
        gradients,
        inner_grads,
        theirs_12,
        kept_6,
        sent_6,
        grad_proj,
        pooled_grad,
        grad_pool,
    )
    theirs_18 = swap(for_partner([*gradients[2], *inner_grads]), "canvas", 2)
    got_6 = swap(sent_6, "canvas", 1)
    kept_12, sent_12 = weights_of(1, theirs_12)
    grad_proj = scatter_step(grad_proj, rounds[1])
    pooled_grad = gather_step(pooled_grad, rounds[-2])
    gradients, inner_grads, kept_6, got_6, kept_12, sent_12, grad_proj, pooled_grad = tie(
        gradients, inner_grads, kept_6, got_6, kept_12, sent_12, grad_proj, pooled_grad
    )
    kept_6, got_6 = halve(kept_6, got_6, *along_rows[0])
    got_12 = swap(sent_12, "canvas", 1)
    feature_0 = features_of(0)
    for bit in rounds[2:]:
        grad_proj = scatter_step(grad_proj, bit)
    grad_proj = grad_proj[0]
    for bit in rounds[-3::-1]:
        pooled_grad = gather_step(pooled_grad, bit)
    pooled_grad = pooled_grad.reshape(channels, image_count)
    (
        gradients,
        inner_grads,
        theirs_18,
        kept_6,
        got_6,
        kept_12,
        got_12,
        feature_0,
        grad_proj,
        pooled_grad,
    ) = tie(
        gradients,
        inner_grads,
        theirs_18,
        kept_6,
        got_6,
        kept_12,
        got_12,
        feature_0,
        grad_proj,
        pooled_grad,
    )
    kept_6, got_6 = halve(kept_6, got_6, *along_rows[1])
    kept_12, got_12 = halve(kept_12, got_12, *along_rows[0])
    back_0 = swap(feature_0[1], "rows", 1)
    kept_18, sent_18 = weights_of(2, theirs_18, inner_grads)
    grad_proj = grad_proj + swap(grad_proj, "canvas", canvas_bits[0])
    shared = jnp.concatenate([grad_pool, grad_proj], axis=0)
    (
        gradients,
        kept_6,
        got_6,
        kept_12,
        got_12,
        kept_18,
        sent_18,
        back_0,
        shared,
    ) = tie(
        gradients,
        kept_6,
        got_6,
        kept_12,
        got_12,
        kept_18,
        sent_18,
        back_0,
        shared,
    )
    for axis, bit in along_rows[2:]:
        kept_6, got_6 = halve(kept_6, got_6, axis, bit)
    part_6 = finish(kept_6, got_6)
    for axis, bit in along_rows[1:]:
        kept_12, got_12 = halve(kept_12, got_12, axis, bit)
    got_18 = swap(sent_18, "canvas", 1)
    block_6 = other_channels(part_6)
    feature_1 = features_of(1)
    for bit in canvas_bits[1:]:
        shared = shared + swap(shared, "canvas", bit)
    grad_pool, grad_proj = shared[:slice_rows], shared[slice_rows:]
    block_6, kept_12, got_12, kept_18, got_18, feature_1, grad_pool, grad_proj, back_0 = tie(
        block_6, kept_12, got_12, kept_18, got_18, feature_1, grad_pool, grad_proj, back_0
    )
    kept_18, got_18 = halve(kept_18, got_18, *along_rows[0])
    early = jnp.concatenate([block_6, other_channels(finish(kept_12, got_12))])
    back_1 = swap(feature_1[1], "rows", 1)
    kept_18, got_18, early = tie(kept_18, got_18, early)
    for axis, bit in along_rows[1:]:
        kept_18, got_18 = halve(kept_18, got_18, axis, bit)
    early = other_rows_of(early)
    evens, odds = [], []
    for (kept, _), back in ((feature_0, back_0), (feature_1, back_1)):
        other = back.astype(jnp.float32)
        evens.append(jnp.where(first_band, kept, other))
        odds.append(jnp.where(first_band, other, kept))
    low_first = depth < group
    even = jnp.where(
        low_first, jnp.concatenate(evens, axis=1), jnp.concatenate(evens[::-1], axis=1)
    )
    odd = jnp.where(low_first, jnp.concatenate(odds, axis=1), jnp.concatenate(odds[::-1], axis=1))
    joined = []
    for shard in range(shards):
        span = slice(shard * slice_rows, (shard + 1) * slice_rows)
        joined += [even[:, span], odd[:, span]]
    spread_pool = lax.dot_general(
        members, pooled_grad, (((1,), (1,)), ((), ())), precision=highest
    )
    grad_features = (jnp.concatenate(joined, axis=1) + spread_pool) * valid_mask
    grad_atrous = jnp.zeros((9 * len(dilations), slice_rows, branch_width), jnp.float32)
    grad_atrous = lax.dynamic_update_slice(grad_atrous, early.astype(jnp.float32), (0, 0, 0))
    kept_18, got_18, grad_atrous, grad_features = tie(kept_18, got_18, grad_atrous, grad_features)
    late = other_rows_of(other_channels(finish(kept_18, got_18)))
    grad_inner = late[9].astype(jnp.float32)
    grad_atrous = lax.dynamic_update_slice(
        grad_atrous, late[:9].astype(jnp.float32), (early.shape[0], 0, 0)
    ).reshape(atrous_weight.shape)

    grad_gains = jnp.stack([totals[1] for totals in branch_totals] + [proj_grad_totals[1]])
    grad_shifts = jnp.stack([totals[0] for totals in branch_totals] + [proj_grad_totals[0]])
    return (
        upsampled[None],
        grad_features.reshape(features.shape),
        grad_inner,
        grad_atrous,
        grad_pool,
        grad_proj,
        grad_gains,
        grad_shifts,
    )


def solution(mesh):
    in_specs = (
        P("canvas", "rows", None, None),
        P("canvas", "rows", None),
        P("canvas", "rows", None),
        P("rows", None),
        P(None, None, "rows", None),
        P("rows", None),
        P("rows", None),
        P(),
        P(),
        P("canvas", "rows", None, None),
    )
    out_specs = (
        P("canvas", "rows", None, None),
        P("canvas", "rows", None, None),
        P("rows", None),
        P(None, None, "rows", None),
        P("rows", None),
        P("rows", None),
        P(),
        P(),
    )
    return jax.shard_map(
        per_device, mesh=mesh, in_specs=in_specs, out_specs=out_specs, check_vma=False
    )
```

```python
import functools

import jax
import jax.numpy as jnp
import numpy as np
from jax import lax
from jax.experimental import pallas as pl
from jax.experimental.pallas import tpu as pltpu
from jax.sharding import PartitionSpec as P

COL_IMAGES = 2
LANES = 128
SIDE = 24
TILE = 16
TILES = 4
TAPS = 4
GROUP = 6

dilations = (6, 12, 18)
epsilon = 1e-05
prev_weights = (0.375, 0.125, 0.0, 0.0)
self_weights = (0.625, 0.875, 0.875, 0.625)
next_weights = (0.0, 0.0, 0.125, 0.375)
vmem_bytes = 52 << 20
in_place = pl.BlockSpec(memory_space=pl.ANY)
in_vmem = pl.BlockSpec(memory_space=pltpu.VMEM)


def swap(values, axis, bit):
    count = lax.axis_size(axis)
    return lax.ppermute(values, axis, [(i, i ^ bit) for i in range(count)])


def bits_of(count):
    bits, bit = [], 1
    while bit < count:
        bits.append(bit)
        bit *= 2
    return bits


def sum_over(values, axis):
    bits = bits_of(lax.axis_size(axis))
    for first in range(0, len(bits), 2):
        pair = bits[first : first + 2]
        found = [swap(values, axis, bit) for bit in pair]
        if len(pair) == 2:
            found.append(swap(values, axis, pair[0] ^ pair[1]))
            values = (values + found[0]) + (found[1] + found[2])
        else:
            values = values + found[0]
    return values


def trade(above, below, width):
    count = lax.axis_size("rows")
    odd = (lax.axis_index("rows") // width) % 2 == 1
    first = swap(jnp.where(odd, above, below), "rows", width)
    pairs = []
    for band in range(count):
        other = band + width if (band // width) % 2 else band - width
        if 0 <= other < count:
            pairs.append((band, other))
    second = lax.ppermute(jnp.where(odd, below, above), "rows", pairs)
    return jnp.where(odd, first, second), jnp.where(odd, second, first)


def tie(*values):
    return lax.optimization_barrier(values)


def halves(first, lower, upper):
    return jnp.where(
        first, jnp.concatenate([lower, upper], axis=0), jnp.concatenate([upper, lower], axis=0)
    )


def place():
    row = lax.axis_index("rows")
    return row // 2, row % 2, lax.axis_index("canvas")


def other_rows(across, band):
    start = (1 - across) * band
    return [
        pl.ds(pl.multiple_of(start + piece * (band // 2), band // 2), band // 2)
        for piece in range(2)
    ]


def copy_all(copies, sems):
    started = []
    for number, (source, target) in enumerate(copies):
        copy = pltpu.make_async_copy(source, target, sems.at[number])
        copy.start()
        started.append(copy)
    return started


def spread(mask, width):
    return jnp.concatenate([mask] * (width // LANES), axis=1)


def spread_rows(mask, columns, width):
    mask = jnp.concatenate([mask] * (columns // TILE), axis=1)
    return spread(mask.reshape(mask.shape[0] * columns, LANES), width)


def shift_columns(source, rows, columns, distance, masks, side, left, right):
    inside = [masks[index] != 0 for index in range(2)]
    chunks = source.shape[-1] // LANES

    def step(group, carry):
        starts = [
            pl.multiple_of((group * GROUP + member) * columns, columns) for member in range(GROUP)
        ]
        for chunk in range(chunks):
            lanes = slice(chunk * LANES, (chunk + 1) * LANES)
            for member, start in enumerate(starts):
                side[chunk, member, SIDE : SIDE + columns, :] = source[
                    pl.ds(start, columns), lanes
                ].astype(jnp.float32)
            for member, start in enumerate(starts):
                for target, offset, mask in (
                    (left, -distance, inside[0]),
                    (right, distance, inside[1]),
                ):
                    first = SIDE + offset
                    value = side[chunk, member, first : first + columns, :]
                    target[pl.ds(start, columns), lanes] = jnp.where(mask, value, 0.0).astype(
                        jnp.bfloat16
                    )
        return carry

    lax.fori_loop(0, rows // GROUP, step, 0)


def moved_columns(source, first, count, columns, distance, inside, planes):
    lefts, rights = [], []
    for chunk in range(source.shape[-1] // LANES):
        lanes = slice(chunk * LANES, (chunk + 1) * LANES)
        left, right = [], []
        for row in range(count):
            start = first + row * columns
            planes[chunk, row, SIDE : SIDE + columns, :] = source[
                start : start + columns, lanes
            ].astype(jnp.float32)
        for row in range(count):
            for offset, mask, result in ((-distance, inside[0], left), (distance, inside[1], right)):
                place = SIDE + offset
                value = planes[chunk, row, place : place + columns, :]
                result.append(jnp.where(mask, value, 0.0).astype(jnp.bfloat16))
        lefts.append(jnp.concatenate(left, axis=0))
        rights.append(jnp.concatenate(right, axis=0))
    return jnp.concatenate(lefts, axis=1), jnp.concatenate(rights, axis=1)


def forward_kernel(which, with_inner, first_tap, half, geometry, own, *refs):
    rows, columns, shards, parts, piece = geometry
    group = shards // 2
    steps = range(1 - half, group)
    others, refs = refs[:2], refs[2:]
    if not half:
        own_taps, refs = refs[: len(which) + with_inner], refs[len(which) + with_inner :]
    pieces, refs = refs[: 2 * len(steps)], refs[2 * len(steps) :]
    count = len(which)
    row_masks, refs = refs[:count], refs[count:]
    col_masks, refs = refs[:count], refs[count:]
    earlier = ()
    if half:
        earlier, refs = refs[: count + with_inner], refs[count + with_inner :]
        mains, refs = refs[:count], refs[count:]
        above, below, *refs = refs
    else:
        mains, refs = refs[:count], refs[count:]
    if with_inner:
        inner_out, *refs = refs
    weights_out, feat, planes, weights, *refs = refs
    if half:
        totals, refs = refs[:count], refs[count:]
        before, refs = refs[: count + with_inner], refs[count + with_inner :]
    else:
        totals = list(mains) + ([inner_out] if with_inner else [])
    sems, out_sem = refs
    depth, across, canvas = place()
    part = canvas % parts
    taps, channels, width = weights.shape
    pixels = rows * columns
    band = pixels // 2
    slice_rows = parts * piece
    upper = depth // group
    if half:
        upper = 1 - upper
    lanes = pl.ds(pl.multiple_of(upper * channels, channels), channels)
    feature_copies = copy_all(
        [
            (own.at[:, lanes], feat.at[pl.ds(pl.multiple_of(across * band, band), band)]),
            *[
                (array.at[:, lanes], feat.at[target])
                for array, target in zip(others, other_rows(across, band))
            ],
        ],
        sems,
    )
    span = pl.ds(first_tap, taps)
    copies = []
    if not half:
        start = pl.multiple_of((depth % group) * slice_rows, slice_rows)
        rows_of = pl.ds(start, slice_rows)
        for number, array in enumerate(own_taps):
            if number < count:
                target = weights.at[pl.ds(9 * number, 9), rows_of]
                copies.append((array.at[dilations.index(which[number])], target))
            else:
                copies.append((array, weights.at[9 * count, rows_of]))
    for number, step in enumerate(steps):
        origin = (depth % group) ^ step
        for index in range(parts):
            start = origin * slice_rows + (part ^ index) * piece
            copies.append(
                (
                    pieces[2 * number + index % 2].at[index // 2, span],
                    weights.at[:, pl.ds(pl.multiple_of(start, piece), piece)],
                )
            )
    weight_copies = copy_all(copies, sems.at[pl.ds(3, len(copies))])
    if half:
        earlier_copies = copy_all(
            list(zip(earlier, before)), sems.at[pl.ds(3 + len(copies), len(earlier))]
        )
    for copy in feature_copies:
        copy.wait()
    tile = pixels // TILES
    tile_rows = tile // columns
    keep = None
    for number, dilation in enumerate(which):
        shift = dilation * columns
        total = totals[number]
        inside = [col_masks[number][side] != 0 for side in range(2)]
        total[...] = jnp.zeros_like(total)
        for index in range(TILES):
            first = index * tile
            span = slice(first, first + tile)
            left, right = moved_columns(
                feat, first, tile_rows, columns, dilation, inside, planes.at[index % 2]
            )
            if number == 0 and index == 0:
                for copy in weight_copies:
                    copy.wait()
                keep = pltpu.make_async_copy(weights, weights_out, out_sem)
                keep.start()
            for row_tap in range(3):
                tap = 9 * number + 3 * row_tap
                product = jnp.dot(feat[span, :], weights[tap + 1], preferred_element_type=jnp.float32)
                product += jnp.dot(left, weights[tap], preferred_element_type=jnp.float32)
                product += jnp.dot(right, weights[tap + 2], preferred_element_type=jnp.float32)
                mask = spread_rows(
                    row_masks[number][row_tap, first // columns : (first + tile) // columns],
                    columns,
                    width,
                ).astype(jnp.float32)
                target = (2 - row_tap) * shift + first
                total[target : target + tile, :] += product * mask
    if half:
        for copy in earlier_copies:
            copy.wait()
    if with_inner:
        for first in range(0, pixels, tile):
            span = slice(first, first + tile)
            product = jnp.dot(feat[span, :], weights[9 * count], preferred_element_type=jnp.float32)
            if half:
                product += before[count][span, :]
            inner_out[span, :] = product
    if half:
        edge = 0
        for number, dilation in enumerate(which):
            shift = dilation * columns
            total, old = totals[number], before[number]
            end = shift + pixels
            above[edge : edge + shift, :] = (total[0:shift, :] + old[0:shift, :]).astype(
                jnp.bfloat16
            )
            mains[number][...] = total[shift:end, :] + old[shift:end, :]
            below[edge : edge + shift, :] = (
                total[end : end + shift, :] + old[end : end + shift, :]
            ).astype(jnp.bfloat16)
            edge += shift
    keep.wait()


def forward_branches(
    own, others, own_taps, pieces, row_masks, col_masks, earlier, which, with_inner, first_tap, geometry
):
    rows, columns, shards, parts, piece = geometry
    half = int(earlier is not None)
    pixels = rows * columns
    channels = own.shape[1] // 2
    width = pieces[0].shape[-1]
    count = len(which)
    taps = 9 * count + with_inner
    sums = [
        jax.ShapeDtypeStruct((pixels + 2 * dilation * columns, width), jnp.float32)
        for dilation in which
    ] + [jax.ShapeDtypeStruct((pixels, width), jnp.float32)] * with_inner
    out_shape = sums
    if half:
        edge = jax.ShapeDtypeStruct((sum(which) * columns, width), jnp.bfloat16)
        plain = jax.ShapeDtypeStruct((pixels, width), jnp.float32)
        out_shape = [plain] * count + [edge, edge] + [plain] * with_inner
    out_specs = [in_vmem] * len(out_shape) + [in_place]
    out_shape = out_shape + [jax.ShapeDtypeStruct((taps, channels, width), jnp.bfloat16)]
    earlier = list(earlier) if half else []
    own_taps = [] if half else [own_taps[0]] * count + [own_taps[1]] * with_inner
    inputs = [own, *others, *own_taps, *pieces]
    copies = 3 + len(own_taps) + (len(pieces) // 2) * parts + len(earlier)
    return pl.pallas_call(
        functools.partial(forward_kernel, which, with_inner, first_tap, half, geometry),
        in_specs=[in_place] * len(inputs) + [in_vmem] * (2 * count) + [in_place] * len(earlier),
        out_specs=out_specs,
        out_shape=out_shape,
        scratch_shapes=[
            pltpu.VMEM((pixels, channels), jnp.bfloat16),
            pltpu.VMEM(
                (2, channels // LANES, rows // TILES, columns + 2 * SIDE, LANES), jnp.float32
            ),
            pltpu.VMEM((taps, channels, width), jnp.bfloat16),
        ]
        + [pltpu.VMEM(array.shape, jnp.float32) for array in (sums[:count] + sums if half else [])]
        + [pltpu.SemaphoreType.DMA((copies,)), pltpu.SemaphoreType.DMA],
        compiler_params=pltpu.CompilerParams(vmem_limit_bytes=vmem_bytes),
        cost_estimate=pl.CostEstimate(
            flops=2 * taps * pixels * channels * width,
            bytes_accessed=2 * pixels * channels + 4 * taps * channels * width,
            transcendentals=0,
        ),
        name=f"forward_{half}_" + "_".join(str(dilation) for dilation in which),
    )(*inputs, *row_masks, *col_masks, *earlier)


def load_gradient(rows, columns, dilation, refs, target, sems):
    depth, across, canvas = place()
    own, other, above, below = refs
    band = rows * columns // 2
    shift = dilation * columns
    return copy_all(
        [
            (own, target.at[pl.ds(pl.multiple_of(shift + across * band, columns), band)]),
            (other, target.at[pl.ds(pl.multiple_of(shift + (1 - across) * band, columns), band)]),
            (above, target.at[pl.ds(0, shift)]),
            (below, target.at[pl.ds(shift + 2 * band, shift)]),
        ],
        sems,
    )


def turned(index, count):
    result = 0
    for bit in bits_of(count):
        result = 2 * result + (index // bit) % 2
    return result


def weight_kernel(dilation, with_inner, geometry, *refs):
    rows, columns, shards, parts, piece = geometry
    own_features, refs = refs[:3], refs[3:]
    their_features, refs = refs[:4], refs[4:]
    gradient, refs = refs[:4], refs[4:]
    if with_inner:
        inner, refs = refs[:2], refs[2:]
    theirs, refs = refs[0], refs[1:]
    row_masks, refs = refs[:2], refs[2:]
    col_masks, refs = refs[:2], refs[2:]
    keep, send, feat, side, moved, result, *refs = refs
    if with_inner:
        straight, *refs = refs
    sems, out_sems = refs
    depth, across, canvas = place()
    low, upper = canvas % 2, (canvas // 2) % 2
    pixels = rows * columns
    band = pixels // 2
    shift = dilation * columns
    width = moved.shape[-1]
    lanes = pl.ds(pl.multiple_of(upper * width, width), width)
    starts = [across * band, (1 - across) * band]

    def spans(base, pieces):
        size = band // pieces
        return [
            pl.ds(pl.multiple_of(base + start + number * size, size), size)
            for start in starts
            for number in range(pieces)
        ]

    first = []
    ends = [(0, shift), (shift + pixels, shift)]
    for number in range(2):
        targets = [pl.ds(pl.multiple_of(shift + start, columns), band) for start in starts]
        targets += [pl.ds(*end) for end in ends]
        if number == 0:
            sources = [array.at[:, lanes] for array in gradient]
        else:
            places = [(0, band), (band, band), (pixels, shift), (pixels + shift, shift)]
            sources = [theirs.at[pl.ds(*where)] for where in places]
        first += [
            (source, moved.at[1, number, target]) for source, target in zip(sources, targets)
        ]
    first = copy_all(first, sems)
    second = list(zip(own_features[:1], [feat.at[spans(0, 1)[0]]]))
    second += list(zip(own_features[1:], [feat.at[span] for span in spans(0, 2)[2:]]))
    second += list(zip(their_features, [feat.at[span] for span in spans(pixels, 2)]))
    if with_inner:
        second += [
            (array.at[:, lanes], straight.at[span]) for array, span in zip(inner, spans(0, 1))
        ]
        second += [
            (theirs.at[pl.ds(pixels + 2 * shift + number * band, band)], straight.at[span])
            for number, span in enumerate(spans(pixels, 1))
        ]
    second = copy_all(second, sems.at[pl.ds(8, len(second))])
    for copy in first:
        copy.wait()
    for number in range(2):
        shift_columns(
            moved.at[1, number],
            rows + 2 * dilation,
            columns,
            dilation,
            (col_masks[number][0], col_masks[number][1]),
            side,
            moved.at[2, number],
            moved.at[0, number],
        )
    for copy in second:
        copy.wait()

    def factor(tap):
        if tap == 9:
            return straight[...]
        row_tap, col_tap = divmod(tap, 3)
        start = (2 - row_tap) * shift
        return jnp.concatenate(
            [
                moved[col_tap, number, start : start + pixels, :]
                * spread_rows(row_masks[number][row_tap], columns, width)
                for number in range(2)
            ],
            axis=0,
        )

    half = parts * piece // 2
    taps = 9 + with_inner
    pending = [[], []]
    for turn, tap in enumerate(range(0, taps, TAPS)):
        slot = turn % 2
        pair = list(range(tap, min(tap + TAPS, taps)))
        product = lax.dot_general(
            feat[...],
            jnp.concatenate([factor(member) for member in pair], axis=1),
            (((0,), (0,)), ((), ())),
            preferred_element_type=jnp.float32,
        )
        for copy in pending[slot]:
            copy.wait()
        result[slot, :, 0 : len(pair) * width] = product.astype(jnp.bfloat16)
        copies = []
        for step in range(shards):
            base = (depth ^ step) * 2 * half
            for target, offset in ((keep, low), (send, 1 - low)):
                rows_of = pl.ds(pl.multiple_of(base + offset * half, half), half)
                for number, member in enumerate(pair):
                    part_of = result.at[slot, rows_of, pl.ds(number * width, width)]
                    copies.append((part_of, target.at[turned(step, shards), member]))
        pending[slot] = copy_all(copies, out_sems.at[slot])
    for copies in pending:
        for copy in copies:
            copy.wait()


def weight_branch(features, gradient, inner, theirs, row_masks, col_masks, dilation, geometry):
    rows, columns, shards, parts, piece = geometry
    pixels = rows * columns
    channels = features[0].shape[1]
    width = theirs.shape[1]
    with_inner = int(inner is not None)
    taps = 9 + with_inner
    extended = pixels + 2 * dilation * columns
    part_shape = jax.ShapeDtypeStruct((shards, taps, parts * piece // 2, width), jnp.bfloat16)
    arrays = [*features, *gradient] + (list(inner) if with_inner else []) + [theirs]
    return pl.pallas_call(
        functools.partial(weight_kernel, dilation, with_inner, geometry),
        in_specs=[in_place] * len(arrays) + [in_vmem] * 4,
        out_specs=[in_place, in_place],
        out_shape=[part_shape, part_shape],
        scratch_shapes=[
            pltpu.VMEM((2 * pixels, channels), jnp.bfloat16),
            pltpu.VMEM((width // LANES, GROUP, columns + 2 * SIDE, LANES), jnp.float32),
            pltpu.VMEM((3, 2, extended, width), jnp.bfloat16),
            pltpu.VMEM((2, channels, TAPS * width), jnp.bfloat16),
        ]
        + [pltpu.VMEM((2 * pixels, width), jnp.bfloat16)] * with_inner
        + [
            pltpu.SemaphoreType.DMA((15 + 4 * with_inner,)),
            pltpu.SemaphoreType.DMA((2, 2 * TAPS * shards)),
        ],
        compiler_params=pltpu.CompilerParams(vmem_limit_bytes=vmem_bytes),
        cost_estimate=pl.CostEstimate(
            flops=4 * taps * pixels * channels * width,
            bytes_accessed=4 * pixels * channels + 4 * taps * channels * width,
            transcendentals=0,
        ),
        name=f"weight_{dilation}",
    )(*arrays, *row_masks, *col_masks)


def feature_kernel(geometry, layout, *refs):
    rows, columns, shards, parts, piece = geometry
    branches = len(dilations)
    gradients = [refs[4 * branch : 4 * branch + 4] for branch in range(branches)]
    refs = refs[4 * branches :]
    inner, refs = refs[:2], refs[2:]
    sources, refs = refs[: len(layout)], refs[len(layout) :]
    row_masks, refs = refs[:branches], refs[branches:]
    col_masks, refs = refs[:branches], refs[branches:]
    keep, send, side, straight, moved, result, *refs = refs
    weights, refs = refs[: len(layout)], refs[len(layout) :]
    sems, weight_sems = refs
    depth, across, canvas = place()
    pixels = rows * columns
    band = pixels // 2
    channels = result.shape[1]
    width = straight.shape[1]
    taps_of = {}
    for number, names in enumerate(layout):
        for index, name in enumerate(names):
            taps_of[name] = (number, 9 * index)
    offsets = [pl.multiple_of(across * band, band), pl.multiple_of((1 - across) * band, band)]

    def load_weights(name):
        number, base = taps_of[name]
        span = pl.ds(base, 9 if name else 1)
        order = (0,) + dilations
        return copy_all(
            [(sources[number].at[span], weights[number].at[span])],
            weight_sems.at[pl.ds(order.index(name), 1)],
        )

    waits = copy_all(
        [
            (inner[0], straight.at[pl.ds(offsets[0], band)]),
            (inner[1], straight.at[pl.ds(offsets[1], band)]),
        ],
        sems.at[pl.ds(4 * branches, 2)],
    )
    loads = {0: load_weights(0)}
    arrivals = []
    for branch, dilation in enumerate(dilations):
        arrivals.append(
            load_gradient(
                rows,
                columns,
                dilation,
                gradients[branch],
                moved.at[branch % 2, 1],
                sems.at[pl.ds(4 * branch, 4)],
            )
            if branch < 2
            else None
        )
        loads[dilation] = load_weights(dilation)
    tile = pixels // 4
    for copy in waits + loads[0]:
        copy.wait()
    for first in range(0, pixels, tile):
        span = slice(first, first + tile)
        number, base = taps_of[0]
        result[span, :] = lax.dot_general(
            straight[span, :],
            weights[number][base],
            (((1,), (1,)), ((), ())),
            preferred_element_type=jnp.float32,
        )
    for branch, dilation in enumerate(dilations):
        slot = branch % 2
        shift = dilation * columns
        for copy in arrivals[branch]:
            copy.wait()
        shift_columns(
            moved.at[slot, 1],
            rows + 2 * dilation,
            columns,
            dilation,
            (col_masks[branch][0], col_masks[branch][1]),
            side,
            moved.at[slot, 2],
            moved.at[slot, 0],
        )
        for copy in loads[dilation]:
            copy.wait()
        number, base = taps_of[dilation]
        for first in range(0, pixels, tile):
            span = slice(first, first + tile)
            product = jnp.zeros((tile, channels), jnp.float32)
            for row_tap in range(3):
                mask = spread_rows(
                    row_masks[branch][row_tap, first // columns : (first + tile) // columns],
                    columns,
                    width,
                )
                start = (2 - row_tap) * shift + first
                for col_tap in range(3):
                    product += lax.dot_general(
                        moved[slot, col_tap, start : start + tile, :] * mask,
                        weights[number][base + 3 * row_tap + col_tap],
                        (((1,), (1,)), ((), ())),
                        preferred_element_type=jnp.float32,
                    )
            result[span, :] += product
        if branch + 2 < branches:
            arrivals[branch + 2] = load_gradient(
                rows,
                columns,
                dilations[branch + 2],
                gradients[branch + 2],
                moved.at[slot, 1],
                sems.at[pl.ds(4 * (branch + 2), 4)],
            )
    keep[...] = result[pl.ds(pl.multiple_of(across * band, band), band), :]
    send[...] = result[pl.ds(pl.multiple_of((1 - across) * band, band), band), :].astype(
        jnp.bfloat16
    )


def feature_branches(gradients, inner, row_masks, col_masks, weights, layout, geometry):
    rows, columns, shards, parts, piece = geometry
    pixels = rows * columns
    band = pixels // 2
    channels, width = weights[0].shape[1:]
    arrays = [array for gradient in gradients for array in gradient] + list(inner)
    taps = sum(array.shape[0] for array in weights)
    extended = pixels + 2 * max(dilations) * columns
    return pl.pallas_call(
        functools.partial(feature_kernel, geometry, layout),
        in_specs=[in_place] * (len(arrays) + len(weights))
        + [in_vmem] * (len(row_masks) + len(col_masks)),
        out_specs=[in_vmem] * 2,
        out_shape=[
            jax.ShapeDtypeStruct((band, channels), jnp.float32),
            jax.ShapeDtypeStruct((band, channels), jnp.bfloat16),
        ],
        scratch_shapes=[
            pltpu.VMEM((width // LANES, GROUP, columns + 2 * SIDE, LANES), jnp.float32),
            pltpu.VMEM((pixels, width), jnp.bfloat16),
            pltpu.VMEM((2, 3, extended, width), jnp.bfloat16),
            pltpu.VMEM((pixels, channels), jnp.float32),
        ]
        + [pltpu.VMEM(array.shape, jnp.bfloat16) for array in weights]
        + [
            pltpu.SemaphoreType.DMA((len(arrays),)),
            pltpu.SemaphoreType.DMA((1 + len(dilations),)),
        ],
        compiler_params=pltpu.CompilerParams(vmem_limit_bytes=vmem_bytes),
        cost_estimate=pl.CostEstimate(
            flops=2 * taps * pixels * channels * width,
            bytes_accessed=6 * band * channels + 2 * taps * channels * width,
            transcendentals=0,
        ),
        name="feature_gradient",
    )(*arrays, *weights, *row_masks, *col_masks)


def interp_matrix(out_count, in_count, before):
    free = np.zeros((out_count, in_count), np.float32)
    edges = np.zeros((out_count, in_count), np.float32)
    for row in range(out_count):
        for offset, coeffs in ((-1, prev_weights), (0, self_weights), (1, next_weights)):
            place = row // 4 + offset + before
            if 0 <= place < in_count:
                free[row, place] += coeffs[row % 4]
            edges[row, min(max(place, 0), in_count - 1)] += coeffs[row % 4]
    return free, edges


def silu_slope(values):
    logistic = jax.nn.sigmoid(values)
    return logistic * (1.0 + values * (1.0 - logistic))


def normalize(values, sum_rows, total_count, scale_vec, shift_vec):
    average = sum_rows[0] / total_count
    spread_of = sum_rows[1] / total_count - average * average
    inverse = lax.rsqrt(spread_of + epsilon)
    centered = (values - average) * inverse
    return (centered, inverse, scale_vec * centered + shift_vec)


def input_grad(slope, centered, inverse, scale_vec, totals, total_count, weight_map):
    return (
        scale_vec
        * inverse
        * (slope - weight_map * (totals[0] + centered * totals[1]) / total_count)
    )


def moments_of(values, weight_map):
    weighted = weight_map * values
    return [jnp.sum(weighted, axis=0), jnp.sum(weighted * values, axis=0)]


def per_device(
    features,
    segment_map,
    pixel_mask,
    inner_weight,
    atrous_weight,
    pool_weight,
    proj_weight,
    norm_gains,
    norm_shifts,
    cotangent,
):
    highest = lax.Precision.HIGHEST
    row_count = lax.axis_size("rows")
    canvas_count = lax.axis_size("canvas") * features.shape[0]
    band_rows, columns, channels = features.shape[1:]
    branch_width = norm_gains.shape[1]
    canvas_rows = band_rows * row_count
    image_count = COL_IMAGES * (canvas_rows // 36)
    row_index = lax.axis_index("rows")
    canvas_index = lax.axis_index("canvas")
    shards = row_count // 2
    depth = row_index // 2
    first_band = row_index % 2 == 0
    row_first = row_index * band_rows
    rows = 2 * band_rows
    band = band_rows * columns
    pixels = rows * columns
    slice_rows = channels // row_count
    parts = min(lax.axis_size("canvas"), max(slice_rows // 16, 1))
    piece = slice_rows // parts
    part = canvas_index % parts
    geometry = (rows, columns, shards, parts, piece)

    flat_mask = pixel_mask.reshape(band, 1)
    valid_mask = flat_mask.astype(jnp.float32)
    segments = segment_map.reshape(band)
    places = jnp.arange(columns)
    col_ids = segment_map[0, 0, :] % COL_IMAGES

    def col_checks(col_ids):
        masks = {}
        for dilation in dilations:
            table = []
            for offset in (-dilation, dilation):
                moved = places + offset
                inside = (moved >= 0) & (moved < columns)
                table.append(inside & (jnp.roll(col_ids, -offset) == col_ids))
            table = jnp.stack(table).astype(jnp.float32)
            masks[dilation] = jnp.broadcast_to(table[:, :, None], (2, columns, LANES))
        return masks

    col_masks = col_checks(col_ids)

    taps = lax.dynamic_slice_in_dim(
        atrous_weight.reshape(9 * len(dilations), slice_rows, branch_width),
        part * piece,
        piece,
        axis=1,
    )
    inner_taps = lax.dynamic_slice_in_dim(inner_weight, part * piece, piece, axis=0)[None]
    quarter = jnp.concatenate(
        [
            item
            for dilation in (18, 0, 12, 6)
            for item in (
                [taps[9 * dilations.index(dilation) :][:9]] if dilation else [inner_taps]
            )
        ],
        axis=0,
    )
    own_taps = (
        atrous_weight.reshape(len(dilations), 9, slice_rows, branch_width),
        inner_weight,
    )
    row_ids = segment_map[0, :, 0] // COL_IMAGES + 1
    both_ids = halves(first_band, row_ids, swap(row_ids, "rows", 1))
    low_mask = flat_mask.astype(jnp.bfloat16)
    flat_features = features.reshape(band, channels)
    slices = [flat_features[:, i * slice_rows : (i + 1) * slice_rows] for i in range(row_count)]
    even = jnp.concatenate(slices[0::2], axis=1)
    odd = jnp.concatenate(slices[1::2], axis=1)
    middle = band // 2
    feat_send = jnp.where(first_band, odd, even) * low_mask
    feat_own, quarter_later, *feat_parts = tie(
        jnp.where(first_band, even, odd) * low_mask,
        quarter,
        feat_send[:middle],
        feat_send[middle:],
    )
    group = shards // 2

    def along(start, bits):
        found = [start]
        for bit in bits:
            found = found + [swap(item, "rows", 2 * bit) for item in found]
        return found

    def between(item):
        chain = [item]
        for bit in bits_of(parts)[1:]:
            chain = chain + [swap(other, "canvas", bit) for other in chain]
        return chain

    def from_partner(chain):
        stacked = jnp.stack(chain)
        return [stacked, swap(stacked, "canvas", 1)]

    def sum_step(values, bit):
        return values + swap(values, "rows", bit)

    def gather_step(values, bit):
        other = swap(values, "rows", bit)
        both = jnp.where(
            (row_index & bit) == 0,
            jnp.stack([values, other], axis=1),
            jnp.stack([other, values], axis=1),
        )
        return both.reshape((2 * values.shape[0],) + values.shape[1:])

    rounds = bits_of(row_count)
    near = along(quarter, bits_of(group))[1:]
    feat_first = swap(feat_parts[0], "rows", 1)
    reach = max(dilations)

    def row_checks(all_ids, outside):
        masks = {}
        for dilation in dilations:
            checks = []
            for row_tap in range(3):
                start = reach - (row_tap - 1) * dilation
                target = all_ids[start : start + rows]
                same = target == all_ids[reach : reach + rows]
                checks.append(jnp.where(target == 0, outside, same))
            table = jnp.stack(checks).astype(jnp.bfloat16)
            masks[dilation] = jnp.broadcast_to(table[:, :, None, None], (3, rows, TILE, LANES))
        return masks

    near_masks = row_checks(jnp.pad(both_ids, (reach, reach)), True)
    col_matrix = jnp.asarray(interp_matrix(4 * columns, columns, 0)[1])
    col_grad = jnp.einsum(
        "pw,opb->owb",
        col_matrix.astype(jnp.bfloat16),
        cotangent[0],
        preferred_element_type=jnp.float32,
    )
    near, both_ids, col_grad, near_masks = tie(near, both_ids, col_grad, near_masks)

    far_first = swap(quarter_later, "rows", 2 * group)
    near_chains = [between(item) for item in near]
    feat_second = swap(feat_parts[1], "rows", 1)
    members = (segments[:, None] == jnp.arange(image_count, dtype=jnp.int32)).astype(jnp.float32)
    member_low = members.astype(jnp.bfloat16)
    seg_sums = jnp.einsum(
        "ps,pc->sc", member_low, flat_features * low_mask, preferred_element_type=jnp.float32
    )
    seg_counts = jnp.sum(members * valid_mask, axis=0)
    seg_all = jnp.concatenate(
        [seg_sums, jnp.broadcast_to(seg_counts[:, None], (image_count, LANES))], axis=1
    )
    far_first, near_chains, feat_first, feat_second, seg_all, proj_full = tie(
        far_first, near_chains, feat_first, feat_second, seg_all, proj_weight[None]
    )

    feat_others = (feat_first, feat_second)
    far = along(far_first, bits_of(group))
    far_chains = [between(far_first)]
    near_pieces = [item for chain in near_chains for item in from_partner(chain)]
    seg_all = sum_step(seg_all, rounds[0])
    proj_full = gather_step(proj_full, rounds[0])
    first_taps = {18: 0, 12: 10, 6: 19}

    def forward(which, pieces, earlier=None):
        return forward_branches(
            feat_own,
            feat_others,
            own_taps,
            pieces,
            [near_masks[dilation] for dilation in which],
            [col_masks[dilation] for dilation in which],
            earlier,
            which,
            int(which == (18,)),
            first_taps[which[0]],
            geometry,
        )

    total_18, total_inner, weights_00 = forward((18,), near_pieces)
    (far, far_chains, seg_all, proj_full, total_18, total_inner, near_pieces) = tie(
        far, far_chains, seg_all, proj_full, total_18, total_inner, near_pieces
    )

    far_chains = far_chains + [between(item) for item in far[1:]]
    far_pieces = from_partner(far_chains[0])
    total_12, total_6, weights_01 = forward((12, 6), near_pieces)
    seg_all = sum_step(seg_all, rounds[1])
    proj_full = gather_step(proj_full, rounds[-1])
    far_chains, far_pieces, total_12, total_6, seg_all, proj_full, both_ids, col_grad = tie(
        far_chains, far_pieces, total_12, total_6, seg_all, proj_full, both_ids, col_grad
    )

    far_pieces = far_pieces + [item for chain in far_chains[1:] for item in from_partner(chain)]
    id_above, id_below = trade(both_ids[:reach], both_ids[rows - reach :], 2)
    all_ids = jnp.concatenate([id_above, both_ids, id_below])
    for bit in rounds[2:]:
        seg_all = sum_step(seg_all, bit)
    for bit in rounds[-2:0:-1]:
        proj_full = gather_step(proj_full, bit)
    proj_full = proj_full.reshape((2, shards) + proj_full.shape[1:]).swapaxes(0, 1)
    proj_full = proj_full.reshape(-1, branch_width)
    grad_above, grad_below = trade(col_grad[:2], col_grad[4 * band_rows - 2 :], 1)
    grad_ext = jnp.concatenate([grad_above, col_grad, grad_below], axis=0)
    their_first = swap(feat_first, "canvas", 2)
    far_pieces, seg_all, proj_full, all_ids, grad_ext, their_first = tie(
        far_pieces, seg_all, proj_full, all_ids, grad_ext, their_first
    )
    their_ids = swap(jnp.concatenate([all_ids, col_ids]), "canvas", 2)
    their_second = swap(tie(feat_second, all_ids)[0], "canvas", 2)

    def to_partner(partials):
        sent = [
            jnp.where(first_band, partial[band:], partial[:band]).astype(jnp.bfloat16)
            for partial in partials
        ]
        return swap(jnp.concatenate(sent, axis=1), "rows", 1)

    def complete(partial, back):
        mine = jnp.where(first_band, partial[:band], partial[band:])
        return mine + back.astype(jnp.float32)

    def beyond_bands(dilation, main, above, below):
        shift = dilation * columns
        here = all_ids[reach : reach + rows]
        mask = here[:dilation] == all_ids[reach - dilation : reach]
        mask = jnp.broadcast_to(mask[:, None], (dilation, columns)).reshape(shift, 1)
        below = below.astype(jnp.float32) * mask.astype(jnp.float32)
        mask = here[rows - dilation :] == all_ids[reach + rows : reach + rows + dilation]
        mask = jnp.broadcast_to(mask[:, None], (dilation, columns)).reshape(shift, 1)
        above = above.astype(jnp.float32) * mask.astype(jnp.float32)
        return jnp.concatenate(
            [
                main[:shift] + below,
                main[shift : pixels - shift],
                main[pixels - shift :] + above,
            ],
            axis=0,
        )

    main_18, above_18, below_18, main_inner, weights_10 = forward(
        (18,), far_pieces, [total_18, total_inner]
    )
    far_pieces, main_18, above_18, below_18, main_inner, seg_all = tie(
        far_pieces, main_18, above_18, below_18, main_inner, seg_all
    )
    back_inner = to_partner([main_inner])
    their_own = [swap(tie(feat_own[:middle], main_18)[0], "canvas", 2)]
    below_18, above_18 = trade(above_18, below_18, 2)
    main_12, above_12, below_12, weights_11 = forward((12,), far_pieces, [total_12])
    total_counts = seg_all[:, channels : channels + 1]
    pooled = lax.dynamic_slice_in_dim(seg_all, row_index * slice_rows, slice_rows, axis=1)
    pooled = pooled / total_counts
    pool_matrix = pool_weight.astype(jnp.float32)
    pool_part = jnp.dot(pooled, pool_matrix, precision=highest)
    (
        far_pieces,
        main_12,
        above_12,
        below_12,
        back_inner,
        above_18,
        below_18,
        pool_part,
        their_ids,
        their_second,
    ) = tie(
        far_pieces,
        main_12,
        above_12,
        below_12,
        back_inner,
        above_18,
        below_18,
        pool_part,
        their_ids,
        their_second,
    )
    their_own.append(swap(tie(feat_own[middle:], main_12)[0], "canvas", 2))
    row_masks = row_checks(all_ids, False)
    reached = all_ids.shape[0]
    their_row_masks = row_checks(their_ids[:reached], False)
    their_col_masks = col_checks(their_ids[reached:])
    main_18 = beyond_bands(18, main_18, above_18, below_18)
    back_18 = to_partner([main_18])
    below_12, above_12 = trade(above_12, below_12, 2)
    main_6, above_6, below_6, weights_12 = forward((6,), far_pieces, [total_6])
    free, edges = interp_matrix(4 * band_rows, band_rows, 0)
    beyond_ends = interp_matrix(4 * band_rows + 8, band_rows + 2, 0)[0][2:-2, 1:-1]
    change = np.pad(edges - free, ((2, 2), (0, 0)))
    halfway = 2 * band_rows + 2
    at_top = np.where(np.arange(4 * band_rows + 4)[:, None] < halfway, change, 0.0)
    back_matrix = (
        jnp.asarray(beyond_ends)
        + jnp.where(row_index == 0, 1.0, 0.0) * jnp.asarray(at_top, jnp.float32)
        + jnp.where(row_index == row_count - 1, 1.0, 0.0)
        * jnp.asarray(change - at_top, jnp.float32)
    )
    back_18, above_12, below_12, main_6, above_6, below_6, grad_ext, row_masks, their_own[0] = tie(
        back_18, above_12, below_12, main_6, above_6, below_6, grad_ext, row_masks, their_own[0]
    )
    main_12 = beyond_bands(12, main_12, above_12, below_12)
    back_12 = to_partner([main_12])
    below_6, above_6 = trade(above_6, below_6, 2)
    act_grad = jnp.einsum("or,owb->rwb", back_matrix, grad_ext, precision=highest)
    act_grad = act_grad.reshape(band, branch_width)
    back_12, above_6, below_6, act_grad = tie(back_12, above_6, below_6, act_grad)
    main_6 = beyond_bands(6, main_6, above_6, below_6)
    back_6 = to_partner([main_6])
    back_6, their_own[1], their_row_masks = tie(back_6, their_own[1], their_row_masks)
    all_features = (feat_own, feat_first, feat_second, *their_own, their_first, their_second)
    conv_outs = [
        complete(main_inner, back_inner),
        complete(main_6, back_6),
        complete(main_12, back_12),
        complete(main_18, back_18),
    ]
    weights_full = [[weights_00, weights_01], [weights_10, weights_11, weights_12]]
    layouts = (((18, 0), (12, 6)), ((18, 0), (12,), (6,)))

    rows_of = []
    for conv_out in conv_outs:
        rows_of += moments_of(conv_out, valid_mask)
    rows_of.append(jnp.broadcast_to(jnp.sum(valid_mask), (branch_width,)))
    sums = sum_over(jnp.concatenate([jnp.stack(rows_of), pool_part]), "rows")
    pool_out = sums[9:]
    sums = sum_over(
        jnp.concatenate(
            [
                sums[:8],
                jnp.sum(pool_out, axis=0, keepdims=True),
                jnp.sum(pool_out * pool_out, axis=0, keepdims=True),
                sums[8:9],
            ]
        ),
        "canvas",
    )
    pixel_total = sums[10]
    entries = float(canvas_count * image_count)
    normals = [
        normalize(
            conv_out,
            sums[2 * branch : 2 * branch + 2],
            pixel_total,
            norm_gains[branch],
            norm_shifts[branch],
        )
        for branch, conv_out in enumerate(conv_outs)
    ]
    pool_norm = normalize(pool_out, sums[8:10], entries, norm_gains[4], norm_shifts[4])
    pool_act = jax.nn.silu(pool_norm[2]).astype(jnp.bfloat16)
    pool_map = jnp.dot(member_low, pool_act, preferred_element_type=jnp.float32)
    concat_act = jnp.concatenate(
        [jax.nn.silu(item[2]).astype(jnp.bfloat16) for item in normals]
        + [pool_map.astype(jnp.bfloat16)],
        axis=-1,
    )
    proj_out = jnp.dot(concat_act, proj_full, preferred_element_type=jnp.float32)
    proj_totals = sum_over(
        sum_over(jnp.stack(moments_of(proj_out, valid_mask)), "rows"), "canvas"
    )
    proj_norm = normalize(proj_out, proj_totals, pixel_total, norm_gains[5], norm_shifts[5])
    proj_act = jax.nn.silu(proj_norm[2]).astype(jnp.bfloat16)

    act_rows = proj_act.reshape(band_rows, columns, branch_width)
    act_above, act_below = trade(act_rows[:1], act_rows[band_rows - 1 :], 1)
    ext_act = jnp.concatenate(
        [
            jnp.where(row_index == 0, act_rows[:1], act_above),
            act_rows,
            jnp.where(row_index == row_count - 1, act_rows[band_rows - 1 :], act_below),
        ],
        axis=0,
    )

    proj_slope = act_grad * silu_slope(proj_norm[2])
    proj_local = jnp.stack(
        [jnp.sum(proj_slope, axis=0), jnp.sum(proj_slope * proj_norm[0], axis=0)]
    )
    proj_grad_totals = sum_over(sum_over(proj_local, "rows"), "canvas")
    proj_grad = input_grad(
        proj_slope,
        proj_norm[0],
        proj_norm[1],
        norm_gains[5],
        proj_grad_totals,
        pixel_total,
        valid_mask,
    ).astype(jnp.bfloat16)
    joined_grad = lax.dot_general(
        proj_grad, proj_full, (((1,), (1,)), ((), ())), preferred_element_type=jnp.float32
    )
    slopes = [
        joined_grad[:, branch * branch_width : (branch + 1) * branch_width]
        * silu_slope(normals[branch][2])
        for branch in range(4)
    ]
    rows_of = []
    for branch, slope in enumerate(slopes):
        rows_of += [jnp.sum(slope, axis=0), jnp.sum(slope * normals[branch][0], axis=0)]
    seg_grads = lax.dot_general(
        members, joined_grad[:, 4 * branch_width :], (((0,), (0,)), ((), ())), precision=highest
    )
    pool_terms = seg_grads * silu_slope(pool_norm[2])
    rows_of += [jnp.sum(pool_terms, axis=0), jnp.sum(pool_terms * pool_norm[0], axis=0)]
    sums = sum_over(jnp.concatenate([jnp.stack(rows_of), seg_grads], axis=0), "rows")
    seg_grads = sums[10:]
    sums = sum_over(sums[:10], "canvas")
    branch_totals = [sums[2 * branch : 2 * branch + 2] for branch in range(5)]
    conv_grads = [
        input_grad(
            slopes[branch],
            normals[branch][0],
            normals[branch][1],
            norm_gains[branch],
            branch_totals[branch],
            pixel_total,
            valid_mask,
        ).astype(jnp.bfloat16)
        for branch in range(4)
    ]

    pool_grad = input_grad(
        seg_grads * silu_slope(pool_norm[2]),
        pool_norm[0],
        pool_norm[1],
        norm_gains[4],
        branch_totals[4],
        entries,
        1.0,
    )
    pooled_grad = (
        lax.dot_general(pool_matrix, pool_grad, (((1,), (1,)), ((), ())), precision=highest)
        / total_counts[:, 0]
    )
    grad_pool = lax.dot_general(
        pooled, pool_grad, (((0,), (0,)), ((), ())), precision=highest
    )
    grad_proj = lax.dot_general(
        concat_act, proj_grad, (((0,), (0,)), ((), ())), preferred_element_type=jnp.float32
    )

    grad_proj = grad_proj.reshape((row_count,) + (grad_proj.shape[0] // row_count, branch_width))

    def scatter_step(values, bit):
        values = values.reshape((values.shape[0] // 2, 2) + values.shape[1:])
        low, high = values[:, 0], values[:, 1]
        mine = (row_index & bit) == 0
        sent = jnp.where(mine, high, low).astype(jnp.bfloat16)
        return jnp.where(mine, low, high) + swap(sent, "rows", bit).astype(jnp.float32)

    def beyond(branch, other):
        grad = conv_grads[branch + 1]
        shift = dilations[branch] * columns
        top = jnp.where(first_band, grad[:shift], other[:shift])
        bottom = jnp.where(first_band, other[band - shift :], grad[band - shift :])
        return (grad, other, *trade(top, bottom, 2))

    def pair_sum(kept, got):
        return kept.astype(jnp.float32) + got.astype(jnp.float32)

    def halve(kept, got, axis, bit):
        size = kept.shape[0] // 2
        sent = pair_sum(kept[size:], got[size:]).astype(jnp.bfloat16)
        return pair_sum(kept[:size], got[:size]), swap(sent, axis, bit)

    def weights_of(branch, theirs, inner=None):
        dilation = dilations[branch]
        return weight_branch(
            all_features,
            gradients[branch],
            inner,
            theirs,
            [row_masks[dilation], their_row_masks[dilation]],
            [col_masks[dilation], their_col_masks[dilation]],
            dilation,
            geometry,
        )

    half_width = branch_width // 2
    upper = (canvas_index // 2) % 2 == 1

    def for_partner(arrays):
        return jnp.concatenate(
            [jnp.where(upper, array[:, :half_width], array[:, half_width:]) for array in arrays]
        )

    along_rows = [("rows", 2 * bit) for bit in bits_of(shards)]

    def finish(kept, got):
        total = pair_sum(kept, got)[0]
        for bit in bits_of(lax.axis_size("canvas"))[2:]:
            total = total + swap(total, "canvas", bit)
        return lax.optimization_barrier(total.astype(jnp.bfloat16))

    def other_channels(block):
        other = swap(block, "canvas", 2)
        return jnp.where(
            upper,
            jnp.concatenate([other, block], axis=2),
            jnp.concatenate([block, other], axis=2),
        )

    def other_rows_of(block):
        other = swap(block, "canvas", 1)
        return jnp.where(
            canvas_index % 2 == 0,
            jnp.concatenate([block, other], axis=1),
            jnp.concatenate([other, block], axis=1),
        )

    def features_of(half):
        return feature_branches(
            gradients,
            inner_grads,
            [row_masks[dilation] for dilation in dilations],
            [col_masks[dilation] for dilation in dilations],
            weights_full[half],
            layouts[half],
            geometry,
        )

    other = swap(conv_grads[1], "rows", 1)
    other, ext_act, *conv_grads = tie(other, ext_act, *conv_grads)
    row_matrix = jnp.asarray(interp_matrix(4 * band_rows, band_rows + 2, 1)[0], jnp.bfloat16)
    rows_up = jnp.einsum("or,rwb->owb", row_matrix, ext_act, preferred_element_type=jnp.float32)
    high = rows_up.astype(jnp.bfloat16)
    low = (rows_up - high.astype(jnp.float32)).astype(jnp.bfloat16)
    upsampled = jnp.einsum(
        "pw,owb->opb",
        jnp.concatenate([col_matrix, col_matrix], axis=1).astype(jnp.bfloat16),
        jnp.concatenate([high, low], axis=1),
        preferred_element_type=jnp.float32,
    ).astype(jnp.bfloat16)
    gradients = [beyond(0, other)]
    other = swap(conv_grads[2], "rows", 1)
    gradients, other, conv_grads, upsampled = tie(gradients, other, conv_grads, upsampled)
    theirs_6 = swap(for_partner(gradients[0]), "canvas", 2)
    gradients.append(beyond(1, other))
    other = swap(jnp.concatenate([conv_grads[3], conv_grads[0]], axis=1), "rows", 1)
    canvas_bits = bits_of(lax.axis_size("canvas"))
    grad_pool = grad_pool + swap(grad_pool, "canvas", canvas_bits[0])
    gradients, theirs_6, other, grad_proj, pooled_grad, grad_pool = tie(
        gradients, theirs_6, other, grad_proj, pooled_grad, grad_pool
    )
    theirs_12 = swap(for_partner(gradients[1]), "canvas", 2)
    gradients.append(beyond(2, other[:, :branch_width]))
    inner_grads = (conv_grads[0], other[:, branch_width:])
    kept_6, sent_6 = weights_of(0, theirs_6)
    grad_proj = scatter_step(grad_proj, rounds[0])
    pooled_grad = gather_step(pooled_grad[None], rounds[-1])
    (
        gradients,
        inner_grads,
        theirs_12,
        kept_6,
        sent_6,
        grad_proj,
        pooled_grad,
        grad_pool,
    ) = tie(
        gradients,
        inner_grads,
        theirs_12,
        kept_6,
        sent_6,
        grad_proj,
        pooled_grad,
        grad_pool,
    )
    theirs_18 = swap(for_partner([*gradients[2], *inner_grads]), "canvas", 2)
    got_6 = swap(sent_6, "canvas", 1)
    kept_12, sent_12 = weights_of(1, theirs_12)
    grad_proj = scatter_step(grad_proj, rounds[1])
    pooled_grad = gather_step(pooled_grad, rounds[-2])
    gradients, inner_grads, kept_6, got_6, kept_12, sent_12, grad_proj, pooled_grad = tie(
        gradients, inner_grads, kept_6, got_6, kept_12, sent_12, grad_proj, pooled_grad
    )
    kept_6, got_6 = halve(kept_6, got_6, *along_rows[0])
    got_12 = swap(sent_12, "canvas", 1)
    feature_0 = features_of(0)
    for bit in rounds[2:]:
        grad_proj = scatter_step(grad_proj, bit)
    grad_proj = grad_proj[0]
    for bit in rounds[-3::-1]:
        pooled_grad = gather_step(pooled_grad, bit)
    pooled_grad = pooled_grad.reshape(channels, image_count)
    (
        gradients,
        inner_grads,
        theirs_18,
        kept_6,
        got_6,
        kept_12,
        got_12,
        feature_0,
        grad_proj,
        pooled_grad,
    ) = tie(
        gradients,
        inner_grads,
        theirs_18,
        kept_6,
        got_6,
        kept_12,
        got_12,
        feature_0,
        grad_proj,
        pooled_grad,
    )
    kept_6, got_6 = halve(kept_6, got_6, *along_rows[1])
    kept_12, got_12 = halve(kept_12, got_12, *along_rows[0])
    back_0 = swap(feature_0[1], "rows", 1)
    kept_18, sent_18 = weights_of(2, theirs_18, inner_grads)
    grad_proj = grad_proj + swap(grad_proj, "canvas", canvas_bits[0])
    shared = jnp.concatenate([grad_pool, grad_proj], axis=0)
    (
        gradients,
        kept_6,
        got_6,
        kept_12,
        got_12,
        kept_18,
        sent_18,
        back_0,
        shared,
    ) = tie(
        gradients,
        kept_6,
        got_6,
        kept_12,
        got_12,
        kept_18,
        sent_18,
        back_0,
        shared,
    )
    for axis, bit in along_rows[2:]:
        kept_6, got_6 = halve(kept_6, got_6, axis, bit)
    part_6 = finish(kept_6, got_6)
    for axis, bit in along_rows[1:]:
        kept_12, got_12 = halve(kept_12, got_12, axis, bit)
    got_18 = swap(sent_18, "canvas", 1)
    block_6 = other_channels(part_6)
    feature_1 = features_of(1)
    for bit in canvas_bits[1:]:
        shared = shared + swap(shared, "canvas", bit)
    grad_pool, grad_proj = shared[:slice_rows], shared[slice_rows:]
    block_6, kept_12, got_12, kept_18, got_18, feature_1, grad_pool, grad_proj, back_0 = tie(
        block_6, kept_12, got_12, kept_18, got_18, feature_1, grad_pool, grad_proj, back_0
    )
    kept_18, got_18 = halve(kept_18, got_18, *along_rows[0])
    early = jnp.concatenate([block_6, other_channels(finish(kept_12, got_12))])
    back_1 = swap(feature_1[1], "rows", 1)
    kept_18, got_18, early = tie(kept_18, got_18, early)
    for axis, bit in along_rows[1:]:
        kept_18, got_18 = halve(kept_18, got_18, axis, bit)
    early = other_rows_of(early)
    evens, odds = [], []
    for (kept, _), back in ((feature_0, back_0), (feature_1, back_1)):
        other = back.astype(jnp.float32)
        evens.append(jnp.where(first_band, kept, other))
        odds.append(jnp.where(first_band, other, kept))
    low_first = depth < group
    even = jnp.where(
        low_first, jnp.concatenate(evens, axis=1), jnp.concatenate(evens[::-1], axis=1)
    )
    odd = jnp.where(low_first, jnp.concatenate(odds, axis=1), jnp.concatenate(odds[::-1], axis=1))
    joined = []
    for shard in range(shards):
        span = slice(shard * slice_rows, (shard + 1) * slice_rows)
        joined += [even[:, span], odd[:, span]]
    spread_pool = lax.dot_general(
        members, pooled_grad, (((1,), (1,)), ((), ())), precision=highest
    )
    grad_features = (jnp.concatenate(joined, axis=1) + spread_pool) * valid_mask
    grad_atrous = jnp.zeros((9 * len(dilations), slice_rows, branch_width), jnp.float32)
    grad_atrous = lax.dynamic_update_slice(grad_atrous, early.astype(jnp.float32), (0, 0, 0))
    kept_18, got_18, grad_atrous, grad_features = tie(kept_18, got_18, grad_atrous, grad_features)
    late = other_rows_of(other_channels(finish(kept_18, got_18)))
    grad_inner = late[9].astype(jnp.float32)
    grad_atrous = lax.dynamic_update_slice(
        grad_atrous, late[:9].astype(jnp.float32), (early.shape[0], 0, 0)
    ).reshape(atrous_weight.shape)

    grad_gains = jnp.stack([totals[1] for totals in branch_totals] + [proj_grad_totals[1]])
    grad_shifts = jnp.stack([totals[0] for totals in branch_totals] + [proj_grad_totals[0]])
    return (
        upsampled[None],
        grad_features.reshape(features.shape),
        grad_inner,
        grad_atrous,
        grad_pool,
        grad_proj,
        grad_gains,
        grad_shifts,
    )


def solution(mesh):
    in_specs = (
        P("canvas", "rows", None, None),
        P("canvas", "rows", None),
        P("canvas", "rows", None),
        P("rows", None),
        P(None, None, "rows", None),
        P("rows", None),
        P("rows", None),
        P(),
        P(),
        P("canvas", "rows", None, None),
    )
    out_specs = (
        P("canvas", "rows", None, None),
        P("canvas", "rows", None, None),
        P("rows", None),
        P(None, None, "rows", None),
        P("rows", None),
        P("rows", None),
        P(),
        P(),
    )
    return jax.shard_map(
        per_device, mesh=mesh, in_specs=in_specs, out_specs=out_specs, check_vma=False
    )
```
